32 devices in a mesh: dp: 8 (over y, x, core), rep: 4 (over z).
Axes of the slice: x: 2, y: 2, z: 4, core: 2. Of those that a mesh axis runs over, the one named last changes fastest.
Arguments:
- tokens: bfloat16 [2, 6144, 768], P(None, ('dp', 'rep')), may hold values from -6 to 6
- positions: int32 [64, 96], P(('dp', 'rep')), may hold values from 0 to 95, each once within a row
- missing: int32 [64], replicated, may hold values 0 or 1
- qkv_weight: bfloat16 [2, 768, 2304], replicated, may hold values from -0.21875 to 0.21875
- out_weight: bfloat16 [2, 768, 768], replicated, may hold values from -0.625 to 0.625
- up_weight: bfloat16 [2, 768, 3072], replicated, may hold values from -0.21875 to 0.21875
- down_weight: bfloat16 [2, 3072, 768], replicated, may hold values from -0.109375 to 0.109375
- norm_gains: float32 [2, 2, 768], replicated, may hold values from 0.5 to 1.5
Outputs:
- loss_value: float32 [], replicated
- token_grads: float32 [2, 6144, 768], P(None, ('dp', 'rep'))
- qkv_grads: float32 [2, 768, 2304], P(None, 'dp')
- out_grads: float32 [2, 768, 768], P(None, 'dp')
- up_grads: float32 [2, 768, 3072], P(None, 'dp')
- down_grads: float32 [2, 3072, 768], P(None, 'dp')
- gain_grads: float32 [2, 2, 768], P(None, None, 'dp')
The draws below stay inside these ranges and needn't reach their ends.
Inputs may be any that keep to these rules, and one draw needn't show every extreme that they name: Each image's 96 positions name every cell of a 8 by 12 grid once.
All inputs are finite; a program needn't handle non-finite values.
Results may differ from the reference program's by a relative error of at most 0.018.
Values may be sent and summed in bfloat16 or wider, within the bound.
A program may use at most 256 MiB of HBM per device.

```python
import math
import jax
import jax.numpy as jnp
from jax import lax

D = 768
HEADS = 12
FF = 3072
GRID_W = 12
PATCHES = 96
IMAGES = 64
TOKENS = 6144


def place_ends(entries, own_key, smallest, high):
    longest = entries.shape.index(max(entries.shape))
    spots = []
    for shift in (0, 1):
        where = [jax.random.randint(jax.random.fold_in(own_key, axis), (), 0, length) for axis, length in enumerate(entries.shape)]
        where[longest] = (where[longest] + shift) % entries.shape[longest]
        spots.append(tuple(where))
    return entries.at[spots[0]].set(smallest).at[spots[1]].set(high)


def level_of(own_key, dims, split, low, largest):
    level = 1.0
    for dim, blocks in split:
        heights = jax.random.uniform(jax.random.fold_in(jax.random.fold_in(own_key, 6), dim), (blocks,), jnp.float32, low / len(split), largest / len(split))
        level = level * jnp.repeat(jnp.exp(heights), dims[dim] // blocks).reshape((-1,) + (1,) * (len(dims) - 1 - dim))
    return level


def noise(rng, extent, width, most, split=(), kind=jnp.bfloat16):
    result = width * jax.random.normal(rng, extent, jnp.float32)
    if split:
        result = result * level_of(rng, extent, split, -0.22, 0.18)
    return jnp.clip(result, -most, most).astype(kind)


def setup_inputs(seed: int = 0) -> dict:
    key_of = jax.random.split(jax.random.key(seed), 9)
    return {
        "tokens": noise(key_of[0], (2, TOKENS, D), 1.0, 6.0, ((1, 32),)),
        "positions": jax.vmap(lambda own: jax.random.permutation(own, PATCHES))(jax.random.split(key_of[1], IMAGES)).reshape((IMAGES, PATCHES)).astype(jnp.int32),
        "missing": place_ends((jax.random.randint(key_of[2], (IMAGES,), 0, 4) < 1).astype(jnp.int32), jax.random.fold_in(key_of[2], 1), 0, 1),
        "qkv_weight": noise(key_of[3], (2, D, 3 * D), D ** -0.5, 0.21875),
        "out_weight": noise(key_of[4], (2, D, D), (D // 8) ** -0.5, 0.625),
        "up_weight": noise(key_of[5], (2, D, FF), D ** -0.5, 0.21875),
        "down_weight": noise(key_of[6], (2, FF, D), FF ** -0.5, 0.109375),
        "norm_gains": jnp.clip(1.0 + 0.1 * jax.random.normal(key_of[7], (2, 2, D), jnp.float32), 0.5, 1.5),
    }


@jax.custom_vjp
def low(v):
    return lax.optimization_barrier(v.astype(jnp.bfloat16)).astype(jnp.float32)

@jax.custom_vjp
def low_back(v):
    return v

def low_keep(v):
    return (low(v), None)

def low_pass(kept, grad):
    return (grad,)

def back_keep(v):
    return (v, None)

def back_low(kept, grad):
    return (low(grad),)
low.defvjp(low_keep, low_pass)
low_back.defvjp(back_keep, back_low)
eps_norm = 1e-06
inv_temp = 32.0

def dot_high(left, right):
    return jnp.dot(left, right, precision=lax.Precision.HIGHEST)

def norm_gain(values, gain):
    centre = values - lax.optimization_barrier(jnp.mean(values, axis=-1, keepdims=True))
    spread = lax.optimization_barrier(jnp.mean(centre * centre, axis=-1, keepdims=True))
    return centre * lax.rsqrt(spread + eps_norm) * gain

def alibi_bias(positions):
    grid_rows = (positions // GRID_W).astype(jnp.float32)
    grid_cols = (positions % GRID_W).astype(jnp.float32)
    row_gap = grid_rows[:, :, None] - grid_rows[:, None, :]
    col_gap = grid_cols[:, :, None] - grid_cols[:, None, :]
    distance = jnp.sqrt(row_gap * row_gap + col_gap * col_gap)
    slopes = jnp.exp2(-8.0 * (jnp.arange(HEADS) + 1).astype(jnp.float32) / HEADS)
    return -slopes[None, :, None, None] * distance[:, None, :, :]

def block_pooled(token_rows, position_rows, qkv_weight, out_weight, up_weight, down_weight, norm_gains):
    row_count = token_rows.shape[0]
    images = position_rows.shape[0]
    head_dim = D // HEADS
    alibi_terms = alibi_bias(position_rows)
    normed_one = low(norm_gain(token_rows, norm_gains[0]))
    projected = low_back(low(dot_high(normed_one, qkv_weight)))
    queries = projected[:, :D].reshape(images, PATCHES, HEADS, head_dim)
    key_rows = projected[:, D:2 * D].reshape(images, PATCHES, HEADS, head_dim)
    value_rows = projected[:, 2 * D:].reshape(images, PATCHES, HEADS, head_dim)
    scores = jnp.einsum('iqhd,ikhd->ihqk', queries, key_rows, precision=lax.Precision.HIGHEST)
    scores = low_back(scores * head_dim ** (-0.5) + alibi_terms)
    attn_probs = low(jax.nn.softmax(scores, axis=-1))
    attended = jnp.einsum('ihqk,ikhd->iqhd', attn_probs, value_rows, precision=lax.Precision.HIGHEST)
    attended = low_back(low(attended.reshape(row_count, D)))
    residual = token_rows + low_back(dot_high(attended, out_weight))
    normed_two = low(norm_gain(residual, norm_gains[1]))
    hidden_pre = low_back(dot_high(normed_two, up_weight))
    active = low(jax.nn.gelu(hidden_pre, approximate=False))
    out_rows = residual + low_back(dot_high(active, down_weight))
    return lax.optimization_barrier(jnp.sum(out_rows.reshape(images, PATCHES, D), axis=1))

def log_total(logits, valid):
    row_max = lax.optimization_barrier(jnp.max(logits, axis=1, keepdims=True))
    summed = lax.optimization_barrier(jnp.sum(valid[None, :] * jnp.exp(logits - row_max), axis=1)) + (1.0 - valid)
    return row_max[:, 0] + jnp.log(summed)

def forward(token_all, qkv_weight, out_weight, up_weight, down_weight, norm_gains, positions, valid):
    group_size = math.gcd(IMAGES, 32)
    groups = IMAGES // group_size
    position_groups = positions.reshape(groups, group_size, PATCHES)
    block = jax.checkpoint(block_pooled)
    embeds = []
    for modality in range(2):
        token_groups = token_all[modality].reshape(groups, group_size * PATCHES, D)

        def step(carry, item, modality=modality):
            pooled_group = block(item[0], item[1], qkv_weight[modality], out_weight[modality], up_weight[modality], down_weight[modality], norm_gains[modality])
            return (carry, pooled_group)
        _, pooled = lax.scan(step, jnp.zeros((), jnp.float32), (token_groups, position_groups))
        pooled = pooled.reshape(IMAGES, D)
        unit = pooled * lax.rsqrt(lax.optimization_barrier(jnp.sum(pooled * pooled, axis=1, keepdims=True)) + eps_norm)
        embeds.append(low(unit))
    logits_r = low_back(dot_high(embeds[0], embeds[1].T) * inv_temp)
    logits_o = low_back(dot_high(embeds[1], embeds[0].T) * inv_temp)
    item_terms = valid * (log_total(logits_r, valid) - jnp.diagonal(logits_r) + log_total(logits_o, valid) - jnp.diagonal(logits_o))
    return jnp.sum(item_terms) / (2.0 * IMAGES)

def reference(tokens, positions, missing, qkv_weight, out_weight, up_weight, down_weight, norm_gains):
    valid = 1.0 - missing.astype(jnp.float32)

    def objective(token_all, w_qkv, w_out, w_up, w_down, gain_all):
        return forward(token_all, w_qkv, w_out, w_up, w_down, gain_all, positions, valid)
    loss_value, pull_back = jax.vjp(objective, tokens.astype(jnp.float32), qkv_weight.astype(jnp.float32), out_weight.astype(jnp.float32), up_weight.astype(jnp.float32), down_weight.astype(jnp.float32), norm_gains.astype(jnp.float32))
    grads = pull_back(jnp.ones_like(loss_value))
    return (loss_value, grads[0], grads[1], grads[2], grads[3], grads[4], grads[5])
```

```python
import functools

import jax
import jax.numpy as jnp
from jax import lax
from jax.experimental import pallas as pl
from jax.experimental.pallas import tpu as pltpu
from jax.sharding import PartitionSpec as P

HEADS = 12
GRID_W = 12
MESH = pl.DeviceIdType.MESH
F32 = jnp.float32
BF16 = jnp.bfloat16

eps_norm = 1e-06
inv_temp = 32.0
SQRT_HALF = 0.7071067811865476
INV_SQRT_TWO_PI = 0.3989422804014327

DP = 8
REP = 4
CHUNK = 256


def nt_dot(left, right):
    return lax.dot_general(left, right, (((1,), (1,)), ((), ())), preferred_element_type=F32)


def tn_dot(left, right):
    return lax.dot_general(left, right, (((0,), (0,)), ((), ())), preferred_element_type=F32)


def nn_dot(left, right):
    return jnp.dot(left, right, preferred_element_type=F32)


def normalized(values):
    centre = values - jnp.mean(values, axis=-1, keepdims=True)
    scale = lax.rsqrt(jnp.mean(centre * centre, axis=-1, keepdims=True) + eps_norm)
    return centre * scale, scale


def gelu_and_slope(values):
    bell = jnp.exp(values * values * -0.5)
    t = 1.0 / (1.0 + (0.3275911 * SQRT_HALF) * jnp.abs(values))
    poly = t * (0.127414796 + t * (-0.142248368 + t * (0.7107068705 + t * (-0.7265760135 + t * 0.5307027145))))
    tail = poly * bell
    cdf = jnp.where(values >= 0.0, 1.0 - tail, tail)
    return values * cdf, cdf + values * (bell * INV_SQRT_TWO_PI)


S_TOK, S_POS, S_A, S_AX, S_B, S_BX, S_G, S_GX = 0, 1, 2, 18, 19, 35, 36, 52
S_HT, S_GB, S_TG = 53, 65, 73
S_Y = 74


def layer_kernel(
    tokens, positions, missing, wqkv_h, wout_h, wup_h, wdown_h, gains,
    grad_out, down_out, token_out, gain_out, loss_out,
    wqkv, wout, wup, wdown, tok, posb, h_one, proj, probs, att, resid, h_two, slope,
    asum, rsum, pool, msg_a, recv_a, msg_b, send_b, recv_b, recv_b2, units, downs, downs_lo, ga, gp_own,
    h_t, ht, gbuf, gatt, gh, gacc, recv_g, gx_send, gx_recv, as_mat, down_stage,
    ysend, keep, yrecv, ring_a, ring_b,
    load_sem, out_sem, ss, rs,
):
    width = h_one.shape[1]
    hidden = wup.shape[1]
    rows = h_one.shape[0]
    half = rows // 2
    patches = half // 2
    pairs = HEADS // 2
    lanes = 128
    pieces = width // lanes
    items = missing.shape[1]
    n_wide = hidden // width
    n_blocks = n_wide + 4
    per_block = width // CHUNK
    n_chunks = n_blocks * per_block
    score_scale = (width // HEADS) ** -0.5

    S_OI, S_II, S_IO, S_X = (S_Y + n_chunks * n for n in range(1, 5))

    dp = lax.axis_index("dp")
    z = lax.axis_index("rep")
    c = dp % 2
    x = (dp // 2) % 2
    y = dp // 4
    yz = y * 4 + z

    def at(yy, xx, cc, zz):
        return (yy * 4 + xx * 2 + cc, zz)

    core_dev = at(y, x, 1 - c, z)
    x_dev = at(y, 1 - x, c, z)
    y_dev = at(1 - y, x, c, z)
    inner = jnp.logical_and(z >= 1, z <= 2)
    outer = jnp.logical_not(inner)
    high = z // 2
    inner_peer = at(y, x, c, 3 - z)
    outer_peer = at(y, x, c, 3 * high)
    inward_peer = at(y, x, c, 1 + high)

    def others():
        for k in range(1, 16):
            yield k, y ^ (k & 1), x ^ ((k >> 1) & 1), (z + (k >> 2)) % 4

    def rc(src, dst, idx, dev):
        return pltpu.make_async_remote_copy(
            src_ref=src, dst_ref=dst, send_sem=ss.at[idx], recv_sem=rs.at[idx],
            device_id=dev, device_id_type=MESH,
        )

    def own_rows(xx):
        return pl.ds(pl.multiple_of(xx * half, half), half)

    tok_load = pltpu.make_async_copy(tokens.at[x], tok.at[own_rows(x)], load_sem.at[4])
    tok_load.start()
    loads = []
    for n, (src, dst) in enumerate(((wqkv_h, wqkv), (wout_h, wout), (wup_h, wup), (wdown_h, wdown))):
        loads.append(pltpu.make_async_copy(src.at[x], dst, load_sem.at[n]))
        loads[-1].start()
    barrier = pltpu.get_barrier_semaphore()
    for k, yy, xx, zz in others():
        pl.semaphore_signal(barrier, inc=1, device_id=at(yy, xx, c, zz), device_id_type=MESH)
    pl.semaphore_signal(barrier, inc=1, device_id=core_dev, device_id_type=MESH)

    cells = positions[...].astype(F32)
    cell_rows = jnp.floor((cells + 0.5) * (1.0 / GRID_W))
    cell_cols = cells - GRID_W * cell_rows
    posb[x] = jnp.zeros((8, lanes), F32)
    posb[x, 0:2, 0:patches] = cell_rows
    posb[x, 2:4, 0:patches] = cell_cols
    asum[...] = jnp.zeros_like(asum)
    rsum[...] = jnp.zeros_like(rsum)
    pool[...] = jnp.zeros_like(pool)
    gacc[...] = jnp.zeros_like(gacc)
    msg_b[...] = jnp.zeros_like(msg_b)

    pl.semaphore_wait(barrier, 16)
    tok_send = rc(tokens.at[1 - x], tok.at[own_rows(x)], S_TOK, x_dev)
    pos_send = rc(posb.at[x], posb.at[x], S_POS, x_dev)
    tok_send.start()
    pos_send.start()
    tok_load.wait()

    low_lanes = lax.broadcasted_iota(jnp.int32, (patches, lanes), 1) < lanes // 2
    mask_low = low_lanes.astype(F32).astype(BF16)
    mask_high = (1.0 - low_lanes.astype(F32)).astype(BF16)

    def two_heads(values):
        return jnp.concatenate([values * mask_low, values * mask_high], axis=0)

    def fold_heads(values):
        return jnp.where(low_lanes, values[:patches], values[patches:])

    def img_rows(i):
        return pl.ds(pl.multiple_of(i * patches, patches), patches)

    gain_one = gains[x, 0:1, :]
    gain_two = gains[x, 1:2, :]

    loads[0].wait()

    def forward_half(step, carry):
        xx = x + step - 2 * x * step
        where = own_rows(xx)

        @pl.when(step == 1)
        def _():
            tok_send.wait_recv()
            pos_send.wait_recv()

        for j in range(2):
            r = img_rows(xx * 2 + j)
            n, _ = normalized(tok[r, :].astype(F32))
            h_one[r, :] = (n * gain_one).astype(BF16)
        lhs = h_one[where, :]
        for n in range(3):
            cols = slice(n * width, (n + 1) * width)
            proj[where, cols] = nn_dot(lhs, wqkv[:, cols]).astype(BF16)

        def image(j, carry):
            i = xx * 2 + j
            r = img_rows(i)
            cr = jnp.broadcast_to(posb[xx, pl.ds(j, 1), :], (lanes, lanes))
            cc = jnp.broadcast_to(posb[xx, pl.ds(j + 2, 1), :], (lanes, lanes))
            row_gap = cr.T - cr
            col_gap = cc.T - cc
            dist = jnp.sqrt(row_gap * row_gap + col_gap * col_gap)[:patches, :patches]
            for p in range(pairs):
                q = two_heads(proj[r, p * lanes : (p + 1) * lanes])
                k = proj[r, width + p * lanes : width + (p + 1) * lanes]
                v = proj[r, 2 * width + p * lanes : 2 * width + (p + 1) * lanes]
                slopes = [2.0 ** (-8.0 * (2 * p + h + 1) / HEADS) for h in range(2)]
                alibi = jnp.concatenate([dist * -slopes[0], dist * -slopes[1]], axis=0)
                s = nt_dot(q, k) * score_scale + alibi
                e = jnp.exp(s - jnp.max(s, axis=-1, keepdims=True))
                prob = e * (1.0 / jnp.sum(e, axis=-1, keepdims=True))
                probs[i * pairs + p] = prob
                att[r, p * lanes : (p + 1) * lanes] = fold_heads(nn_dot(prob.astype(BF16), v)).astype(BF16)
            return carry

        lax.fori_loop(0, 2, image, 0)
        return carry

    lax.fori_loop(0, 2, forward_half, 0)

    loads[1].wait()
    resid[...] = tok[...].astype(F32) + nn_dot(att[...], wout[...])
    for i in range(4):
        r = slice(i * patches, (i + 1) * patches)
        v = resid[r, :]
        rsum[i : i + 1, :] = jnp.sum(v, axis=0, keepdims=True)
        n, _ = normalized(v)
        h_two[r, :] = (n * gain_two).astype(BF16)
    loads[2].wait()
    loads[3].wait()

    def feed(j, carry):
        cols = pl.ds(pl.multiple_of(j * width, width), width)
        pre = nn_dot(h_two[...], wup[:, cols])
        for i in range(4):
            r = slice(i * patches, (i + 1) * patches)
            act, slp = gelu_and_slope(pre[r])
            slope[r, cols] = slp.astype(BF16)
            asum[i : i + 1, cols] = jnp.sum(act.astype(BF16).astype(F32), axis=0, keepdims=True)
        a = asum[:, cols]
        a_high = a.astype(BF16).astype(F32)
        both = jnp.concatenate([a_high, a - a_high], axis=0).astype(BF16)
        pool[...] += nn_dot(both, wdown[cols, :])
        return carry

    lax.fori_loop(0, n_wide, feed, 0)

    pooled = rsum[...] + pool[0:8, :] + pool[8:16, :]
    s_own = lax.rsqrt(jnp.sum(pooled * pooled, axis=1, keepdims=True) + eps_norm)
    unit = pooled * s_own
    for q in range(pieces):
        msg_a[4 * q : 4 * q + 4, :] = unit[0:4, q * lanes : (q + 1) * lanes]
    s_high = s_own.astype(BF16).astype(F32)
    msg_a[24:28, :] = jnp.broadcast_to(s_high[0:4], (4, lanes))
    msg_a[28:32, :] = jnp.broadcast_to((s_own - s_high)[0:4], (4, lanes))
    recv_a[c, x, yz] = msg_a[...].astype(BF16)
    a_copies = []
    for k, yy, xx, zz in others():
        a_copies.append(rc(recv_a.at[c, x, yz], recv_a.at[c, x, yz], S_A + k, at(yy, xx, c, zz)))
        a_copies[-1].start()

    for block in range(DP):
        for q in range(3):
            lo = block * 3 * lanes + q * lanes
            msg_b[block, 4 * q : 4 * q + 4, :] = asum[0:4, lo : lo + lanes]
    for block in range(DP):
        send_b[block // 2, block % 2] = msg_b[block].astype(BF16)
    recv_b[x, yz] = send_b[y * 2 + x]
    b_copies = []
    for k, yy, xx, zz in others():
        b_copies.append(rc(send_b.at[yy * 2 + xx], recv_b.at[x, yz], S_B + k, at(yy, xx, c, zz)))
        b_copies[-1].start()

    ht_copies = []
    for w, src in enumerate((h_two, att, h_one)):
        h_t[w] = src[...].T
        for rel in range(2):
            yy = y if rel == 1 else 1 - y
            for xx in range(2):
                base = yy * (width // 2) + xx * (width // 4)
                mine = pl.ds(pl.multiple_of(base + c * (width // 8), width // 8), width // 8)
                theirs = pl.ds(pl.multiple_of(base + (1 - c) * (width // 8), width // 8), width // 8)
                lo = (rel * 2 + xx) * (width // 8)
                ht[w, lo : lo + width // 8, 0:rows] = h_t[w, mine, :]
                ht_copies.append(
                    rc(
                        h_t.at[w, theirs, :],
                        ht.at[w, pl.ds(lo, width // 8), pl.ds(rows, rows)],
                        S_HT + w * 4 + rel * 2 + xx,
                        core_dev,
                    )
                )
                ht_copies[-1].start()

    n_sel = 8 * 32
    sel_row = lax.broadcasted_iota(jnp.int32, (n_sel, n_sel), 0)
    sel_col = lax.broadcasted_iota(jnp.int32, (n_sel, n_sel), 1)
    pick = ((sel_row >> 2) & 7) * 32 + (sel_row >> 5) * 4 + (sel_row & 3)
    select_a = (sel_col == pick).astype(F32).astype(BF16)

    p_i = lax.broadcasted_iota(jnp.int32, (items, items), 0)
    q_i = lax.broadcasted_iota(jnp.int32, (items, items), 1)
    place = ((((p_i >> 4) & 1) * 4 + ((p_i >> 1) & 1) * 2 + (p_i >> 5)) * 4 + ((p_i >> 2) & 3)) * 2 + (p_i & 1)
    eye = (p_i == q_i).astype(F32)
    v_nat = 1.0 - missing[...].astype(F32)
    v_col = jnp.sum((q_i == place).astype(F32) * v_nat, axis=1, keepdims=True)
    v_row = jnp.sum(eye * v_col, axis=0, keepdims=True)

    for cp in a_copies:
        cp.wait_recv()
    ax_copy = rc(recv_a.at[c], recv_a.at[c], S_AX, core_dev)
    ax_copy.start()
    ax_copy.wait_recv()

    scales = [[None, None], [None, None]]
    for core in range(2):
        for m in range(2):
            got = nn_dot(select_a, recv_a[core, m].reshape(n_sel, lanes))
            for q in range(pieces):
                units[m, core * 32 : core * 32 + 32, q * lanes : (q + 1) * lanes] = got[q * 32 : q * 32 + 32].astype(BF16)
            scales[m][core] = got[6 * 32 : 7 * 32] + got[7 * 32 :]
    scale_cols = [jnp.concatenate(scales[m], axis=0)[:, 0:1] for m in range(2)]

    u_r, u_o = units[0], units[1]
    logits = nt_dot(u_r, u_o) * inv_temp
    top_r = jnp.max(logits, axis=1, keepdims=True)
    lse_r = top_r + jnp.log(jnp.sum(v_row * jnp.exp(logits - top_r), axis=1, keepdims=True) + (1.0 - v_col))
    top_o = jnp.max(logits, axis=0, keepdims=True)
    lse_o = top_o + jnp.log(jnp.sum(v_col * jnp.exp(logits - top_o), axis=0, keepdims=True) + (1.0 - v_row))
    diag = logits * eye
    terms_r = v_col * (lse_r - jnp.sum(diag, axis=1, keepdims=True))
    terms_o = v_row * (lse_o - jnp.sum(diag, axis=0, keepdims=True))
    loss = (jnp.sum(terms_r, axis=0, keepdims=True) + jnp.sum(terms_o, axis=1, keepdims=True)) / (2.0 * items)
    loss_out[...] = jnp.broadcast_to(loss, loss_out.shape)
    grad_r = (v_col / (2.0 * items) * (v_row * jnp.exp(logits - lse_r) - eye)).astype(BF16)
    grad_ot = (v_row / (2.0 * items) * (v_col * jnp.exp(logits - lse_o) - eye)).astype(BF16)
    grad_u = [
        (nn_dot(grad_r, u_o) + nn_dot(grad_ot, u_o)) * inv_temp,
        (tn_dot(grad_r, u_r) + tn_dot(grad_ot, u_r)) * inv_temp,
    ]
    for m in range(2):
        u = units[m].astype(F32)
        g = grad_u[m]
        gp = scale_cols[m] * (g - u * jnp.sum(u * g, axis=1, keepdims=True))
        high_part = gp.astype(BF16)
        downs[m] = high_part
        downs_lo[m] = (gp - high_part.astype(F32)).astype(BF16)
    own_r = lax.broadcasted_iota(jnp.int32, (16, items), 0)
    own_c = lax.broadcasted_iota(jnp.int32, (16, items), 1)
    mine = jnp.logical_and(own_r < 4, own_c == c * 32 + yz * 4 + own_r).astype(F32).astype(BF16)
    down_own = nn_dot(mine, downs[x])
    gp_own[...] = (down_own + nn_dot(mine, downs_lo[x]))[0:8]
    down_own = down_own.astype(BF16)

    def y_copy(k):
        return rc(ysend.at[k], yrecv.at[k], S_Y + k, y_dev)

    def oi_copy(k):
        return rc(keep.at[k], ring_a.at[k], S_OI + k, inward_peer)

    def ii_copy(k):
        return rc(ring_a.at[k], ring_b.at[k], S_II + k, inner_peer)

    def io_copy(k):
        return rc(ring_b.at[k], ring_a.at[k], S_IO + k, outer_peer)

    def out_cols(k):
        return pl.ds(pl.multiple_of(k * CHUNK, CHUNK), CHUNK)

    quarter = width // 8

    def x_copy(k):
        return rc(
            yrecv.at[k, pl.ds(pl.multiple_of((1 - x) * quarter, quarter), quarter), :],
            grad_out.at[x, :, out_cols(k)], S_X + k, x_dev,
        )

    def here_copy(k):
        return pltpu.make_async_copy(
            yrecv.at[k, pl.ds(pl.multiple_of(x * quarter, quarter), quarter), :],
            grad_out.at[x, :, out_cols(k)], out_sem.at[k],
        )

    def step_y(k):
        y_copy(k).wait_recv()
        keep[k] = (keep[k].astype(F32) + yrecv[k].astype(F32)).astype(BF16)

        @pl.when(outer)
        def _():
            oi_copy(k).start()

    def step_a(k):
        @pl.when(inner)
        def _():
            oi_copy(k).wait_recv()
            ring_a[k] = (ring_a[k].astype(F32) + keep[k].astype(F32)).astype(BF16)
            ii_copy(k).start()

    def step_b(k):
        @pl.when(inner)
        def _():
            ii_copy(k).wait_recv()
            got = ring_b[k].astype(F32)
            ring_b[k] = (got + keep[k].astype(F32)).astype(BF16)
            io_copy(k).start()
            yrecv[k] = (got + ring_a[k].astype(F32)).astype(BF16)
            x_copy(k).start()
            here_copy(k).start()

    def step_c(k):
        @pl.when(outer)
        def _():
            io_copy(k).wait_recv()
            yrecv[k] = (keep[k].astype(F32) + ring_a[k].astype(F32)).astype(BF16)
            x_copy(k).start()
            here_copy(k).start()

    def comm(t):
        for lag, step in ((0, step_y), (1, step_a), (2, step_b), (3, step_c)):
            @pl.when(jnp.logical_and(t >= lag, t < n_chunks + lag))
            def _(step=step, lag=lag):
                step(t - lag)

    def gb_copy(j):
        return rc(gbuf.at[j, pl.ds(0, rows), :], gbuf.at[j, pl.ds(rows, rows), :], S_GB + j, core_dev)

    def wgrad(j, w):
        gb_copy(j).wait_recv()
        for n in range(per_block):
            both = nn_dot(ht[w], gbuf[j, :, n * CHUNK : (n + 1) * CHUNK])
            k = j * per_block + n
            ysend[k] = both[:half].astype(BF16)
            y_copy(k).start()
            keep[k] = both[half:].astype(BF16)

    for cp in ht_copies[:4]:
        cp.wait_recv()

    def back_hidden(j, carry):
        cols = pl.ds(pl.multiple_of(j * width, width), width)
        ga[...] = nt_dot(down_own, wdown[cols, :])
        for i in range(4):
            r = slice(i * patches, (i + 1) * patches)
            gbuf[j, r, :] = (ga[i : i + 1, :] * slope[r, cols].astype(F32)).astype(BF16)
        gb_copy(j).start()

        @pl.when(j > 0)
        def _():
            wgrad(j - 1, 0)

        return carry

    lax.fori_loop(0, n_wide, back_hidden, 0)
    wgrad(n_wide - 1, 0)

    gh[...] = jnp.zeros_like(gh)

    def back_up(j, carry):
        cols = pl.ds(pl.multiple_of(j * width, width), width)
        gh[...] += nt_dot(gbuf[j, 0:rows, :], wup[:, cols])
        comm(j)
        return carry

    lax.fori_loop(0, n_wide, back_up, 0)
    comm(4)

    for i in range(4):
        r = slice(i * patches, (i + 1) * patches)
        n, s = normalized(resid[r, :])
        gy = gh[r, :]
        gacc[1:2, :] += jnp.sum(gy * n, axis=0, keepdims=True)
        gyg = gy * gain_two
        grad = s * (gyg - jnp.mean(gyg, axis=-1, keepdims=True) - n * jnp.mean(gyg * n, axis=-1, keepdims=True))
        grad = grad + gp_own[i : i + 1, :]
        resid[r, :] = grad
        gbuf[n_wide, r, :] = grad.astype(BF16)
    gb_copy(n_wide).start()
    comm(5)
    gatt[...] = nt_dot(gbuf[n_wide, 0:rows, :], wout[...]).astype(BF16)
    for cp in ht_copies[4:8]:
        cp.wait_recv()
    wgrad(n_wide, 1)
    comm(6)

    def back_attention(i, carry):
        r = img_rows(i)
        for p in range(pairs):
            cols = slice(p * lanes, (p + 1) * lanes)
            q = two_heads(proj[r, cols])
            k = proj[r, width + p * lanes : width + (p + 1) * lanes]
            v = proj[r, 2 * width + p * lanes : 2 * width + (p + 1) * lanes]
            da = two_heads(gatt[r, cols])
            prob = probs[i * pairs + p]
            dprob = nt_dot(da, v)
            ds = prob * (dprob - jnp.sum(dprob * prob, axis=-1, keepdims=True))
            ds = ds.astype(BF16)
            gbuf[n_wide + 3, r, cols] = tn_dot(prob.astype(BF16), da).astype(BF16)
            gbuf[n_wide + 1, r, cols] = (fold_heads(nn_dot(ds, k)) * score_scale).astype(BF16)
            gbuf[n_wide + 2, r, cols] = (tn_dot(ds, q) * score_scale).astype(BF16)
        comm(7 + i)
        return carry

    lax.fori_loop(0, 4, back_attention, 0)
    for n in range(3):
        gb_copy(n_wide + 1 + n).start()
    gh[...] = jnp.zeros_like(gh)

    def back_proj(n, carry):
        cols = pl.ds(pl.multiple_of(n * width, width), width)
        gh[...] += nt_dot(gbuf[n_wide + 1 + n, 0:rows, :], wqkv[:, cols])
        comm(11 + n)
        return carry

    for cp in ht_copies[8:12]:
        cp.wait_recv()
    wgrad(n_wide + 1, 2)
    lax.fori_loop(0, 3, back_proj, 0)
    wgrad(n_wide + 2, 2)
    comm(14)
    wgrad(n_wide + 3, 2)
    comm(15)

    for i in range(4):
        r = slice(i * patches, (i + 1) * patches)
        n, s = normalized(tok[r, :].astype(F32))
        gy = gh[r, :]
        gacc[0:1, :] += jnp.sum(gy * n, axis=0, keepdims=True)
        gyg = gy * gain_one
        grad = s * (gyg - jnp.mean(gyg, axis=-1, keepdims=True) - n * jnp.mean(gyg * n, axis=-1, keepdims=True))
        resid[r, :] += grad
    tg_copy = rc(resid.at[own_rows(1 - x)], token_out.at[x], S_TG, x_dev)
    tg_copy.start()
    tg_here = pltpu.make_async_copy(resid.at[own_rows(x)], token_out.at[x], load_sem.at[5])
    tg_here.start()

    gx_send[...] = jnp.zeros_like(gx_send)
    for n in range(2):
        for q in range(pieces):
            row = n * pieces + q
            gx_send[0, row : row + 1, :] = gacc[n : n + 1, q * lanes : (q + 1) * lanes]
    recv_g[x, yz] = gx_send[0]
    g_copies = []
    for k, yy, xx, zz in others():
        g_copies.append(rc(recv_g.at[x, yz], recv_g.at[x, yz], S_G + k, at(yy, xx, c, zz)))
        g_copies[-1].start()
    comm(16)

    for cp in b_copies:
        cp.wait_recv()
    bx_copy = rc(recv_b.at[:, :, 1 - c], recv_b2, S_BX, core_dev)
    bx_copy.start()
    sb_row = lax.broadcasted_iota(jnp.int32, (96, 128), 0)
    sb_col = lax.broadcasted_iota(jnp.int32, (96, 128), 1)
    pick_b = ((sb_row >> 2) & 7) * 16 + (sb_row >> 5) * 4 + (sb_row & 3)
    select_b = (sb_col == pick_b).astype(F32).astype(BF16)
    comm(17)
    bx_copy.wait_recv()
    for m in range(2):
        for src, cc in ((recv_b[m, :, c], c), (recv_b2[m], 1 - c)):
            got = nn_dot(select_b, src.reshape(128, lanes)).astype(BF16)
            to = pl.ds(pl.multiple_of(cc * 32, 32), 32)
            for q in range(3):
                as_mat[to, q * lanes : (q + 1) * lanes] = got[q * 32 : (q + 1) * 32]
        down_stage[m] = tn_dot(as_mat[...], downs[m]).astype(BF16)
    down_copy = pltpu.make_async_copy(down_stage, down_out, load_sem.at[6])
    down_copy.start()
    comm(18)

    for cp in g_copies:
        cp.wait_recv()
    for m in range(2):
        total = recv_g[m, 0]
        for n in range(1, 8):
            total = total + recv_g[m, n]
        gx_send[m] = total
    gx_copy = rc(gx_send, gx_recv, S_GX, core_dev)
    gx_copy.start()

    def drain(t, carry):
        comm(t)
        return carry

    lax.fori_loop(19, n_chunks + 3, drain, 0)
    gx_copy.wait_recv()
    gain_out[...] = gx_send[...] + gx_recv[...]

    def finish(k, carry):
        y_copy(k).wait_send()
        here_copy(k).wait()
        x_copy(k).wait()

        @pl.when(outer)
        def _():
            oi_copy(k).wait_send()

        @pl.when(inner)
        def _():
            ii_copy(k).wait_send()
            io_copy(k).wait_send()

        return carry

    lax.fori_loop(0, n_chunks, finish, 0)
    for cp in a_copies + b_copies + ht_copies + g_copies + [tok_send, pos_send, ax_copy, bx_copy, gx_copy]:
        cp.wait_send()
    for j in range(n_blocks):
        gb_copy(j).wait_send()
    tg_copy.wait()
    tg_here.wait()
    down_copy.wait()


def layer_call(tokens, positions, missing, wqkv, wout, wup, wdown, gains):
    own, patches = positions.shape
    width = tokens.shape[2]
    hidden = wup.shape[2]
    rows = 2 * own * patches
    items = missing.shape[0]
    n_blocks = hidden // width + 4
    n_chunks = n_blocks * (width // CHUNK)
    piece = (n_chunks, width // 4, CHUNK)
    vm = pltpu.VMEM
    any_spec = pl.BlockSpec(memory_space=pl.ANY)
    vmem_spec = pl.BlockSpec(memory_space=pltpu.VMEM)
    n_sems = S_Y + 5 * n_chunks
    scratch = [
        vm((width, 3 * width), BF16), vm((width, width), BF16), vm((width, hidden), BF16), vm((hidden, width), BF16),
        vm((rows, width), BF16),
        vm((2, 8, 128), F32),
        vm((rows, width), BF16),
        vm((rows, 3 * width), BF16),
        vm((4 * (HEADS // 2), 2 * patches, patches), F32),
        vm((rows, width), BF16),
        vm((rows, width), F32),
        vm((rows, width), BF16),
        vm((rows, hidden), BF16),
        vm((8, hidden), F32),
        vm((8, width), F32),
        vm((16, width), F32),
        vm((32, 128), F32),
        vm((2, 2, 8, 32, 128), BF16),
        vm((8, 16, 128), F32),
        vm((4, 2, 16, 128), BF16),
        vm((2, 8, 2, 16, 128), BF16),
        vm((2, 8, 16, 128), BF16),
        vm((2, items, width), BF16),
        vm((2, items, width), BF16),
        vm((2, items, width), BF16),
        vm((16, width), F32),
        vm((8, width), F32),
        vm((3, width, rows), BF16),
        vm((3, width // 2, 2 * rows), BF16),
        vm((n_blocks, 2 * rows, width), BF16),
        vm((rows, width), BF16),
        vm((rows, width), F32),
        vm((8, width), F32),
        vm((2, 8, 16, 128), F32),
        vm((2, 16, 128), F32),
        vm((2, 16, 128), F32),
        vm((items, hidden // DP), BF16),
        vm((2, hidden // DP, width), BF16),
        vm(piece, BF16), vm(piece, BF16), vm(piece, BF16), vm(piece, BF16), vm(piece, BF16),
        pltpu.SemaphoreType.DMA((8,)),
        pltpu.SemaphoreType.DMA((n_chunks,)),
        pltpu.SemaphoreType.DMA((n_sems,)),
        pltpu.SemaphoreType.DMA((n_sems,)),
    ]
    return pl.pallas_call(
        layer_kernel,
        out_shape=(
            jax.ShapeDtypeStruct((2, width // DP, n_chunks * CHUNK), BF16),
            jax.ShapeDtypeStruct((2, hidden // DP, width), BF16),
            jax.ShapeDtypeStruct((2, own * patches, width), F32),
            jax.ShapeDtypeStruct((2, 16, 128), F32),
            jax.ShapeDtypeStruct((8, 128), F32),
        ),
        in_specs=[any_spec, vmem_spec, vmem_spec, any_spec, any_spec, any_spec, any_spec, vmem_spec],
        out_specs=(any_spec, any_spec, any_spec, vmem_spec, vmem_spec),
        scratch_shapes=scratch,
        compiler_params=pltpu.CompilerParams(
            collective_id=0, has_side_effects=True, vmem_limit_bytes=62 * 2**20
        ),
    )(tokens, positions, missing.reshape(1, items), wqkv, wout, wup, wdown, gains)


def fused(tokens, positions, missing, qkv_weight, out_weight, up_weight, down_weight, norm_gains):
    width = tokens.shape[2]
    hidden = up_weight.shape[2]
    grads, down, token_grads, gain, loss = layer_call(
        tokens, positions, missing, qkv_weight, out_weight, up_weight, down_weight, norm_gains
    )
    gain = gain[:, : 2 * width // 128].reshape(2, 2, width)
    share = width // DP
    gain = lax.dynamic_slice_in_dim(gain, lax.axis_index("dp") * share, share, axis=2)
    return (
        loss[0, 0],
        token_grads,
        grads[:, :, hidden + width :].astype(F32),
        grads[:, :, hidden : hidden + width].astype(F32),
        grads[:, :, :hidden].astype(F32),
        down.astype(F32),
        gain,
    )


def lead_dot(left, right):
    return lax.dot_general(
        left, right, (((0,), (0,)), ((), ())), preferred_element_type=jnp.float32
    )


def tail_dot(left, right):
    return lax.dot_general(
        left, right, (((1,), (1,)), ((), ())), preferred_element_type=jnp.float32
    )


def norm_gain(values, gain):
    centre = values - jnp.mean(values, axis=-1, keepdims=True)
    spread = jnp.mean(centre * centre, axis=-1, keepdims=True)
    return centre * lax.rsqrt(spread + eps_norm) * gain


def unit_rows(pooled):
    return pooled * lax.rsqrt(jnp.sum(pooled * pooled, axis=1, keepdims=True) + eps_norm)


def gelu_exact(values):
    return jax.nn.gelu(values, approximate=False)


def alibi_bias(positions):
    grid_rows = (positions // GRID_W).astype(jnp.float32)
    grid_cols = (positions % GRID_W).astype(jnp.float32)
    row_gap = grid_rows[:, :, None] - grid_rows[:, None, :]
    col_gap = grid_cols[:, :, None] - grid_cols[:, None, :]
    distance = jnp.sqrt(row_gap * row_gap + col_gap * col_gap)
    slopes = jnp.exp2(-8.0 * (jnp.arange(HEADS) + 1).astype(jnp.float32) / HEADS)
    return -slopes[None, :, None, None] * distance[:, None, :, :]


def log_total(logits, valid_cols, valid_rows):
    row_max = jnp.max(logits, axis=1, keepdims=True)
    summed = jnp.sum(valid_cols[None, :] * jnp.exp(logits - row_max), axis=1) + (1.0 - valid_rows)
    return row_max[:, 0] + jnp.log(summed)


def row_grads(logits, log_sums, valid_rows, valid_cols, match, total_items):
    soft = valid_cols[None, :] * jnp.exp(logits - log_sums[:, None])
    return (valid_rows[:, None] / (2.0 * total_items) * (soft - match)).astype(jnp.bfloat16)


def block_forward(token_rows, alibi_terms, qkv_weight, out_weight, up_weight, down_weight, gains):
    row_count, model_width = token_rows.shape
    images, patches = (alibi_terms.shape[0], alibi_terms.shape[2])
    head_dim = model_width // HEADS
    score_scale = head_dim ** (-0.5)
    start_rows = token_rows.astype(jnp.float32)
    normed_one = norm_gain(start_rows, gains[0]).astype(jnp.bfloat16)
    projected = jnp.dot(normed_one, qkv_weight, preferred_element_type=jnp.float32).astype(
        jnp.bfloat16
    )
    queries = projected[:, :model_width].reshape(images, patches, HEADS, head_dim)
    key_rows = projected[:, model_width : 2 * model_width].reshape(images, patches, HEADS, head_dim)
    value_rows = projected[:, 2 * model_width :].reshape(images, patches, HEADS, head_dim)
    scores = jnp.einsum("iqhd,ikhd->ihqk", queries, key_rows, preferred_element_type=jnp.float32)
    attn_probs = jax.nn.softmax(scores * score_scale + alibi_terms, axis=-1)
    probs_low = attn_probs.astype(jnp.bfloat16)
    attended = jnp.einsum(
        "ihqk,ikhd->iqhd", probs_low, value_rows, preferred_element_type=jnp.float32
    )
    attended = attended.reshape(row_count, model_width).astype(jnp.bfloat16)
    residual = start_rows + jnp.dot(attended, out_weight, preferred_element_type=jnp.float32)
    normed_two = norm_gain(residual, gains[1]).astype(jnp.bfloat16)
    hidden_pre = jnp.dot(normed_two, up_weight, preferred_element_type=jnp.float32)
    active = gelu_exact(hidden_pre).astype(jnp.bfloat16)
    out_rows = residual + jnp.dot(active, down_weight, preferred_element_type=jnp.float32)
    saved = (
        start_rows,
        normed_one,
        projected,
        attn_probs,
        probs_low,
        attended,
        residual,
        normed_two,
        hidden_pre,
        active,
    )
    return (out_rows, saved)


def block_backward(grad_rows, saved, qkv_weight, out_weight, up_weight, down_weight, gains):
    (
        start_rows,
        normed_one,
        projected,
        attn_probs,
        probs_low,
        attended,
        residual,
        normed_two,
        hidden_pre,
        active,
    ) = saved
    images, head_count, patches = (attn_probs.shape[0], attn_probs.shape[1], attn_probs.shape[2])
    row_count, model_width = grad_rows.shape
    head_dim = model_width // head_count
    score_scale = head_dim ** (-0.5)
    down_in = grad_rows.astype(jnp.bfloat16)
    grad_down = lead_dot(active, down_in)
    grad_active = tail_dot(down_in, down_weight)
    _, gelu_back = jax.vjp(gelu_exact, hidden_pre)
    grad_hidden = gelu_back(grad_active)[0].astype(jnp.bfloat16)
    grad_up = lead_dot(normed_two, grad_hidden)
    grad_h_two = tail_dot(grad_hidden, up_weight)
    _, norm_two_back = jax.vjp(norm_gain, residual, gains[1])
    grad_mid, gain_two = norm_two_back(grad_h_two)
    grad_residual = grad_rows + grad_mid
    attn_in = grad_residual.astype(jnp.bfloat16)
    grad_out = lead_dot(attended, attn_in)
    grad_att = (
        tail_dot(attn_in, out_weight)
        .astype(jnp.bfloat16)
        .reshape(images, patches, head_count, head_dim)
    )
    queries = projected[:, :model_width].reshape(images, patches, head_count, head_dim)
    key_rows = projected[:, model_width : 2 * model_width].reshape(
        images, patches, head_count, head_dim
    )
    value_rows = projected[:, 2 * model_width :].reshape(images, patches, head_count, head_dim)
    grad_values = jnp.einsum(
        "ihqk,iqhd->ikhd", probs_low, grad_att, preferred_element_type=jnp.float32
    )
    grad_probs = jnp.einsum(
        "iqhd,ikhd->ihqk", grad_att, value_rows, preferred_element_type=jnp.float32
    )
    grad_scores = attn_probs * (
        grad_probs - jnp.sum(grad_probs * attn_probs, axis=-1, keepdims=True)
    )
    grad_scores = grad_scores.astype(jnp.bfloat16)
    grad_queries = (
        jnp.einsum("ihqk,ikhd->iqhd", grad_scores, key_rows, preferred_element_type=jnp.float32)
        * score_scale
    )
    grad_keys = (
        jnp.einsum("ihqk,iqhd->ikhd", grad_scores, queries, preferred_element_type=jnp.float32)
        * score_scale
    )
    grad_proj = jnp.concatenate(
        [
            grad_queries.reshape(row_count, model_width),
            grad_keys.reshape(row_count, model_width),
            grad_values.reshape(row_count, model_width),
        ],
        axis=1,
    ).astype(jnp.bfloat16)
    grad_qkv = lead_dot(normed_one, grad_proj)
    grad_h_one = tail_dot(grad_proj, qkv_weight)
    _, norm_one_back = jax.vjp(norm_gain, start_rows, gains[0])
    grad_first, gain_one = norm_one_back(grad_h_one)
    weight_grads = (grad_qkv, grad_out, grad_up, grad_down, jnp.stack([gain_one, gain_two]))
    return (grad_residual + grad_first, weight_grads)


def local(tokens, positions, missing, qkv_weight, out_weight, up_weight, down_weight, norm_gains):
    own_images = positions.shape[0]
    model_width = tokens.shape[2]
    patches = tokens.shape[1] // own_images
    first_row = lax.axis_index(("dp", "rep")) * own_images
    alibi_terms = alibi_bias(positions)
    saved_list = []
    pooled_list = []
    normed = []
    for modality in range(2):
        out_rows, saved = block_forward(
            tokens[modality],
            alibi_terms,
            qkv_weight[modality],
            out_weight[modality],
            up_weight[modality],
            down_weight[modality],
            norm_gains[modality],
        )
        pooled = jnp.sum(out_rows.reshape(own_images, patches, model_width), axis=1)
        saved_list.append(saved)
        pooled_list.append(pooled)
        normed.append(unit_rows(pooled).astype(jnp.bfloat16))
    valid_all = 1.0 - missing.astype(jnp.float32)
    total_items = float(missing.shape[0])
    valid_own = lax.dynamic_slice_in_dim(valid_all, first_row, own_images)
    radar_all, optic_all = (
        lax.all_gather(normed[0], ("dp", "rep"), axis=0, tiled=True),
        lax.all_gather(normed[1], ("dp", "rep"), axis=0, tiled=True),
    )
    images_all = radar_all.shape[0]
    match_own = (
        lax.broadcasted_iota(jnp.int32, (own_images, images_all), 0) + first_row
        == lax.broadcasted_iota(jnp.int32, (own_images, images_all), 1)
    ).astype(jnp.float32)
    logits_r = tail_dot(normed[0], optic_all) * inv_temp
    logits_o = tail_dot(normed[1], radar_all) * inv_temp
    lse_r = log_total(logits_r, valid_all, valid_own)
    lse_o = log_total(logits_o, valid_all, valid_own)
    item_terms = valid_own * (
        lse_r
        - jnp.sum(logits_r * match_own, axis=1)
        + lse_o
        - jnp.sum(logits_o * match_own, axis=1)
    )
    grad_lr = row_grads(logits_r, lse_r, valid_own, valid_all, match_own, total_items)
    grad_lo = row_grads(logits_o, lse_o, valid_own, valid_all, match_own, total_items)
    grad_ur = jnp.dot(grad_lr, optic_all, preferred_element_type=jnp.float32) * inv_temp
    grad_uo = jnp.dot(grad_lo, radar_all, preferred_element_type=jnp.float32) * inv_temp
    summed_terms = lax.psum(jnp.sum(item_terms), ("dp", "rep"))
    loss_value = summed_terms / (2.0 * total_items)
    share_o = lead_dot(grad_lr, normed[0]) * inv_temp
    share_r = lead_dot(grad_lo, normed[1]) * inv_temp
    back_r, back_o = (
        lax.psum_scatter(share_r, ("dp", "rep"), scatter_dimension=0, tiled=True),
        lax.psum_scatter(share_o, ("dp", "rep"), scatter_dimension=0, tiled=True),
    )
    grad_ur = grad_ur + back_r
    grad_uo = grad_uo + back_o
    grad_units = (grad_ur, grad_uo)
    token_list = []
    block_grads = []
    for modality in range(2):
        _, unit_back = jax.vjp(unit_rows, pooled_list[modality])
        grad_pooled = unit_back(grad_units[modality])[0]
        grad_rows = jnp.broadcast_to(grad_pooled[:, None, :], (own_images, patches, model_width))
        grad_rows = grad_rows.reshape(own_images * patches, model_width)
        grad_tokens, weight_grads = block_backward(
            grad_rows,
            saved_list[modality],
            qkv_weight[modality],
            out_weight[modality],
            up_weight[modality],
            down_weight[modality],
            norm_gains[modality],
        )
        token_list.append(grad_tokens)
        block_grads.append(list(weight_grads))
    stacked = [jnp.stack([block_grads[0][slot], block_grads[1][slot]]) for slot in range(5)]
    shares = (
        lax.psum_scatter(stacked[0], "dp", scatter_dimension=1, tiled=True),
        lax.psum_scatter(stacked[1], "dp", scatter_dimension=1, tiled=True),
        lax.psum_scatter(stacked[2], "dp", scatter_dimension=1, tiled=True),
        lax.psum_scatter(stacked[3], "dp", scatter_dimension=1, tiled=True),
        lax.psum_scatter(stacked[4], "dp", scatter_dimension=2, tiled=True),
    )
    summed = (
        lax.psum(shares[0].astype(jnp.bfloat16), "rep").astype(jnp.float32),
        lax.psum(shares[1].astype(jnp.bfloat16), "rep").astype(jnp.float32),
        lax.psum(shares[2].astype(jnp.bfloat16), "rep").astype(jnp.float32),
        lax.psum(shares[3].astype(jnp.bfloat16), "rep").astype(jnp.float32),
        lax.psum(shares[4].astype(jnp.bfloat16), "rep").astype(jnp.float32),
    )
    stacked = list(summed)
    token_grads = jnp.stack(token_list)
    return (loss_value, token_grads, stacked[0], stacked[1], stacked[2], stacked[3], stacked[4])


def solution(mesh):
    in_specs = (P(None, ("dp", "rep"), None), P(("dp", "rep"), None), P(), P(), P(), P(), P(), P())
    out_specs = (
        P(),
        P(None, ("dp", "rep"), None),
        P(None, "dp", None),
        P(None, "dp", None),
        P(None, "dp", None),
        P(None, "dp", None),
        P(None, None, "dp"),
    )
    one_kernel = mesh.shape["dp"] == DP and mesh.shape["rep"] == REP
    step = fused if one_kernel else local
    return jax.shard_map(step, mesh=mesh, in_specs=in_specs, out_specs=out_specs, check_vma=False)
```

```python
import functools

import jax
import jax.numpy as jnp
from jax import lax
from jax.experimental import pallas as pl
from jax.experimental.pallas import tpu as pltpu
from jax.sharding import PartitionSpec as P

HEADS = 12
GRID_W = 12
MESH = pl.DeviceIdType.MESH
F32 = jnp.float32
BF16 = jnp.bfloat16

eps_norm = 1e-06
inv_temp = 32.0
SQRT_HALF = 0.7071067811865476
INV_SQRT_TWO_PI = 0.3989422804014327
HALF_LOG2_E = -0.7213475204444817

DP = 8
REP = 4
CHUNK = 256


def nt_dot(left, right):
    return lax.dot_general(left, right, (((1,), (1,)), ((), ())), preferred_element_type=F32)


def tn_dot(left, right):
    return lax.dot_general(left, right, (((0,), (0,)), ((), ())), preferred_element_type=F32)


def nn_dot(left, right):
    return jnp.dot(left, right, preferred_element_type=F32)


def normalized(values):
    centre = values - jnp.mean(values, axis=-1, keepdims=True)
    scale = lax.rsqrt(jnp.mean(centre * centre, axis=-1, keepdims=True) + eps_norm)
    return centre * scale, scale


def gelu_and_slope(values):
    cdf = 0.5 + 0.5 * lax.erf(values * SQRT_HALF)
    return values * cdf, cdf + values * (jnp.exp2(values * values * HALF_LOG2_E) * INV_SQRT_TWO_PI)


S_TOK, S_POS, S_A, S_AX, S_B, S_BX, S_G, S_GX = 0, 1, 2, 18, 19, 35, 36, 52
S_HT, S_GB, S_TG = 53, 65, 73
S_Y = 74


def layer_kernel(
    tokens, positions_h, missing_h, wqkv_h, wout_h, wup_h, wdown_h, gains_h,
    grad_out, down_out, token_out, gain_out, loss_out,
    positions, missing, gains, gain_stage, loss_stage, wqkv, wout, wup, wdown, tok, posb, h_one, proj, probs, att, resid, h_two, slope,
    asum, rsum, pool, msg_a, recv_a, msg_b, send_b, recv_b, recv_b2, units, downs, downs_lo, ga, gp_own,
    h_t, ht, gbuf, gatt, gh, gacc, recv_g, gx_send, gx_recv, as_mat, down_stage,
    ysend, keep, yrecv, ring_a, ring_b,
    load_sem, out_sem, ss, rs,
):
    width = h_one.shape[1]
    hidden = wup.shape[1]
    rows = h_one.shape[0]
    half = rows // 2
    patches = half // 2
    pairs = HEADS // 2
    lanes = 128
    pieces = width // lanes
    items = missing.shape[1]
    n_wide = hidden // width
    n_blocks = n_wide + 4
    per_block = width // CHUNK
    n_chunks = n_blocks * per_block
    score_scale = (width // HEADS) ** -0.5

    S_OI, S_II, S_IO, S_X = (S_Y + n_chunks * n for n in range(1, 5))

    dp = lax.axis_index("dp")
    z = lax.axis_index("rep")
    c = dp % 2
    x = (dp // 2) % 2
    y = dp // 4
    yz = y * 4 + z

    def at(yy, xx, cc, zz):
        return (yy * 4 + xx * 2 + cc, zz)

    core_dev = at(y, x, 1 - c, z)
    x_dev = at(y, 1 - x, c, z)
    y_dev = at(1 - y, x, c, z)
    inner = jnp.logical_and(z >= 1, z <= 2)
    outer = jnp.logical_not(inner)
    high = z // 2
    inner_peer = at(y, x, c, 3 - z)
    outer_peer = at(y, x, c, 3 * high)
    inward_peer = at(y, x, c, 1 + high)

    def others():
        for k in range(1, 16):
            yield k, y ^ (k & 1), x ^ ((k >> 1) & 1), (z + (k >> 2)) % 4

    def rc(src, dst, idx, dev):
        return pltpu.make_async_remote_copy(
            src_ref=src, dst_ref=dst, send_sem=ss.at[idx], recv_sem=rs.at[idx],
            device_id=dev, device_id_type=MESH,
        )

    def own_rows(xx):
        return pl.ds(pl.multiple_of(xx * half, half), half)

    barrier = pltpu.get_barrier_semaphore()
    for k, yy, xx, zz in others():
        pl.semaphore_signal(barrier, inc=1, device_id=at(yy, xx, c, zz), device_id_type=MESH)
    pl.semaphore_signal(barrier, inc=1, device_id=core_dev, device_id_type=MESH)
    early = [
        (positions_h, positions), (tokens.at[x], tok.at[own_rows(x)]), (gains_h.at[x], gains), (wqkv_h.at[x], wqkv),
        (missing_h, missing),
    ]
    late = [(wout_h.at[x], wout), (wup_h.at[x], wup), (wdown_h.at[x], wdown)]
    loads = [pltpu.make_async_copy(src, dst, load_sem.at[n]) for n, (src, dst) in enumerate(early + late)]
    for load in loads[: len(early)]:
        load.start()
    load_pos, load_tok, load_gains, load_qkv, load_missing, load_out, load_up, load_down = loads
    posb[x] = jnp.zeros((8, lanes), F32)
    asum[...] = jnp.zeros_like(asum)
    rsum[...] = jnp.zeros_like(rsum)
    pool[...] = jnp.zeros_like(pool)
    gacc[...] = jnp.zeros_like(gacc)

    load_pos.wait()
    cells = positions[...].astype(F32)
    cell_rows = jnp.floor((cells + 0.5) * (1.0 / GRID_W))
    cell_cols = cells - GRID_W * cell_rows
    posb[x, 0:2, 0:patches] = cell_rows
    posb[x, 2:4, 0:patches] = cell_cols

    pl.semaphore_wait(barrier, 16)
    tok_send = rc(tokens.at[1 - x], tok.at[own_rows(x)], S_TOK, x_dev)
    pos_send = rc(posb.at[x], posb.at[x], S_POS, x_dev)
    tok_send.start()
    pos_send.start()

    low_lanes = lax.broadcasted_iota(jnp.int32, (patches, lanes), 1) < lanes // 2
    mask_low = low_lanes.astype(F32).astype(BF16)
    mask_high = (1.0 - low_lanes.astype(F32)).astype(BF16)

    def two_heads(values):
        return jnp.concatenate([values * mask_low, values * mask_high], axis=0)

    def fold_heads(values):
        return jnp.where(low_lanes, values[:patches], values[patches:])

    def img_rows(i):
        return pl.ds(pl.multiple_of(i * patches, patches), patches)

    load_tok.wait()
    load_gains.wait()
    gain_one = gains[0:1, :]
    gain_two = gains[1:2, :]

    def attention(xx):
        def image(j, carry):
            r = img_rows(xx * 2 + j)
            cr = jnp.broadcast_to(posb[xx, pl.ds(j, 1), :], (lanes, lanes))
            cc = jnp.broadcast_to(posb[xx, pl.ds(j + 2, 1), :], (lanes, lanes))
            row_gap = cr.T - cr
            col_gap = cc.T - cc
            dist = jnp.sqrt(row_gap * row_gap + col_gap * col_gap)[:patches, :patches]
            for p in range(pairs):
                q = two_heads(proj[r, p * lanes : (p + 1) * lanes])
                k = proj[r, width + p * lanes : width + (p + 1) * lanes]
                v = proj[r, 2 * width + p * lanes : 2 * width + (p + 1) * lanes]
                slopes = [2.0 ** (-8.0 * (2 * p + h + 1) / HEADS) for h in range(2)]
                alibi = jnp.concatenate([dist * -slopes[0], dist * -slopes[1]], axis=0)
                s = nt_dot(q, k) * score_scale + alibi
                e = jnp.exp(s - jnp.max(s, axis=-1, keepdims=True))
                prob = e * (1.0 / jnp.sum(e, axis=-1, keepdims=True))
                probs[(xx * 2 + j) * pairs + p] = prob
                att[r, p * lanes : (p + 1) * lanes] = fold_heads(nn_dot(prob.astype(BF16), v)).astype(BF16)
            return carry

        lax.fori_loop(0, 2, image, 0)

    def wide(j):
        return pl.ds(pl.multiple_of(j * width, width), width)

    def add_pool(j, on):
        a = asum[:, wide(j)] * on
        a_high = a.astype(BF16).astype(F32)
        both = jnp.concatenate([a_high, a - a_high], axis=0).astype(BF16)
        pool[...] += nn_dot(both, wdown[wide(j), :])

    for step in range(2):
        xx = x if step == 0 else 1 - x
        where = own_rows(xx)
        if step == 1:
            tok_send.wait_recv()
            pos_send.wait_recv()
        for j in range(2):
            r = img_rows(xx * 2 + j)
            n, _ = normalized(tok[r, :].astype(F32))
            h_one[r, :] = (n * gain_one).astype(BF16)
        if step == 0:
            load_qkv.wait()
            load_out.start()
            load_up.start()
            load_down.start()
        for n in range(3):
            cols = slice(n * width, (n + 1) * width)
            proj[where, cols] = nn_dot(h_one[where, :], wqkv[:, cols]).astype(BF16)
        attention(xx)
        if step == 0:
            load_out.wait()
        resid[where, :] = tok[where, :].astype(F32) + nn_dot(att[where, :], wout[...])
        for j in range(2):
            i = xx * 2 + j
            r = img_rows(i)
            v = resid[r, :]
            rsum[pl.ds(i, 1), :] = jnp.sum(v, axis=0, keepdims=True)
            n, _ = normalized(v)
            h_two[r, :] = (n * gain_two).astype(BF16)
        if step == 0:
            load_up.wait()
        else:
            load_down.wait()

        def feed(j, carry, where=where, xx=xx, step=step):
            for n in range(width // 256):
                cols = pl.ds(pl.multiple_of(j * width + n * 256, 256), 256)
                pre = nn_dot(h_two[where, :], wup[:, cols])
                act, slp = gelu_and_slope(pre)
                slope[where, cols] = slp.astype(BF16)
                act = act.astype(BF16).astype(F32)
                for i in range(2):
                    asum[pl.ds(xx * 2 + i, 1), cols] = jnp.sum(act[i * patches : (i + 1) * patches], axis=0, keepdims=True)
            if step == 1:
                add_pool(jnp.maximum(j - 1, 0), (j > 0).astype(F32))
            return carry

        lax.fori_loop(0, n_wide, feed, 0)
    add_pool(n_wide - 1, 1.0)

    pooled = rsum[...] + pool[0:8, :] + pool[8:16, :]
    s_own = lax.rsqrt(jnp.sum(pooled * pooled, axis=1, keepdims=True) + eps_norm)
    unit = pooled * s_own
    for q in range(pieces):
        msg_a[4 * q : 4 * q + 4, :] = unit[0:4, q * lanes : (q + 1) * lanes]
    s_high = s_own.astype(BF16).astype(F32)
    msg_a[24:28, :] = jnp.broadcast_to(s_high[0:4], (4, lanes))
    msg_a[28:32, :] = jnp.broadcast_to((s_own - s_high)[0:4], (4, lanes))
    recv_a[c, x, yz] = msg_a[...].astype(BF16)
    a_copies = []
    for k, yy, xx, zz in others():
        a_copies.append(rc(recv_a.at[c, x, yz], recv_a.at[c, x, yz], S_A + k, at(yy, xx, c, zz)))
        a_copies[-1].start()

    ht_copies = []
    for w, src in enumerate((h_two, att, h_one)):
        h_t[w] = src[...].T
        for rel in range(2):
            yy = y if rel == 1 else 1 - y
            for xx in range(2):
                base = yy * (width // 2) + xx * (width // 4)
                mine = pl.ds(pl.multiple_of(base + c * (width // 8), width // 8), width // 8)
                theirs = pl.ds(pl.multiple_of(base + (1 - c) * (width // 8), width // 8), width // 8)
                lo = (rel * 2 + xx) * (width // 8)
                ht[w, lo : lo + width // 8, 0:rows] = h_t[w, mine, :]
                ht_copies.append(
                    rc(
                        h_t.at[w, theirs, :],
                        ht.at[w, pl.ds(lo, width // 8), pl.ds(rows, rows)],
                        S_HT + w * 4 + rel * 2 + xx,
                        core_dev,
                    )
                )
                ht_copies[-1].start()

    n_sel = 8 * 32
    sel_row = lax.broadcasted_iota(jnp.int32, (n_sel, n_sel), 0)
    sel_col = lax.broadcasted_iota(jnp.int32, (n_sel, n_sel), 1)
    pick = ((sel_row >> 2) & 7) * 32 + (sel_row >> 5) * 4 + (sel_row & 3)
    select_a = (sel_col == pick).astype(F32).astype(BF16)

    p_i = lax.broadcasted_iota(jnp.int32, (items, items), 0)
    q_i = lax.broadcasted_iota(jnp.int32, (items, items), 1)
    place = ((((p_i >> 4) & 1) * 4 + ((p_i >> 1) & 1) * 2 + (p_i >> 5)) * 4 + ((p_i >> 2) & 3)) * 2 + (p_i & 1)
    eye = (p_i == q_i).astype(F32)
    load_missing.wait()
    v_nat = 1.0 - missing[...].astype(F32)
    v_col = jnp.sum((q_i == place).astype(F32) * v_nat, axis=1, keepdims=True)
    v_row = jnp.sum(eye * v_col, axis=0, keepdims=True)

    for cp in a_copies:
        cp.wait_recv()
    ax_copy = rc(recv_a.at[c], recv_a.at[c], S_AX, core_dev)
    ax_copy.start()
    ax_copy.wait_recv()

    scales = [[None, None], [None, None]]
    for core in range(2):
        for m in range(2):
            got = nn_dot(select_a, recv_a[core, m].reshape(n_sel, lanes))
            for q in range(pieces):
                units[m, core * 32 : core * 32 + 32, q * lanes : (q + 1) * lanes] = got[q * 32 : q * 32 + 32].astype(BF16)
            scales[m][core] = got[6 * 32 : 7 * 32] + got[7 * 32 :]
    scale_cols = [jnp.concatenate(scales[m], axis=0)[:, 0:1] for m in range(2)]

    u_r, u_o = units[0], units[1]
    logits = nt_dot(u_r, u_o) * inv_temp
    top_r = jnp.max(logits, axis=1, keepdims=True)
    lse_r = top_r + jnp.log(jnp.sum(v_row * jnp.exp(logits - top_r), axis=1, keepdims=True) + (1.0 - v_col))
    top_o = jnp.max(logits, axis=0, keepdims=True)
    lse_o = top_o + jnp.log(jnp.sum(v_col * jnp.exp(logits - top_o), axis=0, keepdims=True) + (1.0 - v_row))
    diag = logits * eye
    terms_r = v_col * (lse_r - jnp.sum(diag, axis=1, keepdims=True))
    terms_o = v_row * (lse_o - jnp.sum(diag, axis=0, keepdims=True))
    loss = (jnp.sum(terms_r, axis=0, keepdims=True) + jnp.sum(terms_o, axis=1, keepdims=True)) / (2.0 * items)
    loss_stage[...] = jnp.broadcast_to(loss, loss_stage.shape)
    loss_copy = pltpu.make_async_copy(loss_stage, loss_out, load_sem.at[8])
    loss_copy.start()
    grad_r = (v_col / (2.0 * items) * (v_row * jnp.exp(logits - lse_r) - eye)).astype(BF16)
    grad_ot = (v_row / (2.0 * items) * (v_col * jnp.exp(logits - lse_o) - eye)).astype(BF16)
    grad_u = [
        (nn_dot(grad_r, u_o) + nn_dot(grad_ot, u_o)) * inv_temp,
        (tn_dot(grad_r, u_r) + tn_dot(grad_ot, u_r)) * inv_temp,
    ]
    for m in range(2):
        u = units[m].astype(F32)
        g = grad_u[m]
        gp = scale_cols[m] * (g - u * jnp.sum(u * g, axis=1, keepdims=True))
        high_part = gp.astype(BF16)
        downs[m] = high_part
        downs_lo[m] = (gp - high_part.astype(F32)).astype(BF16)
    own_r = lax.broadcasted_iota(jnp.int32, (16, items), 0)
    own_c = lax.broadcasted_iota(jnp.int32, (16, items), 1)
    mine = jnp.logical_and(own_r < 4, own_c == c * 32 + yz * 4 + own_r).astype(F32).astype(BF16)
    down_own = nn_dot(mine, downs[x])
    gp_own[...] = (down_own + nn_dot(mine, downs_lo[x]))[0:8]
    down_own = down_own.astype(BF16)

    def y_copy(k):
        return rc(ysend.at[k], yrecv.at[k], S_Y + k, y_dev)

    def oi_copy(k):
        return rc(keep.at[k], ring_a.at[k], S_OI + k, inward_peer)

    def ii_copy(k):
        return rc(ring_a.at[k], ring_b.at[k], S_II + k, inner_peer)

    def io_copy(k):
        return rc(ring_b.at[k], ring_a.at[k], S_IO + k, outer_peer)

    def out_cols(k):
        return pl.ds(pl.multiple_of(k * CHUNK, CHUNK), CHUNK)

    quarter = width // 8

    def x_copy(k):
        return rc(
            yrecv.at[k, pl.ds(pl.multiple_of((1 - x) * quarter, quarter), quarter), :],
            grad_out.at[x, :, out_cols(k)], S_X + k, x_dev,
        )

    def here_copy(k):
        return pltpu.make_async_copy(
            yrecv.at[k, pl.ds(pl.multiple_of(x * quarter, quarter), quarter), :],
            grad_out.at[x, :, out_cols(k)], out_sem.at[k],
        )

    def step_y(k):
        y_copy(k).wait_recv()
        keep[k] = (keep[k].astype(F32) + yrecv[k].astype(F32)).astype(BF16)

        @pl.when(outer)
        def _():
            oi_copy(k).start()

    def step_a(k):
        @pl.when(inner)
        def _():
            oi_copy(k).wait_recv()
            ring_a[k] = (ring_a[k].astype(F32) + keep[k].astype(F32)).astype(BF16)
            ii_copy(k).start()

    def step_b(k):
        @pl.when(inner)
        def _():
            ii_copy(k).wait_recv()
            got = ring_b[k].astype(F32)
            ring_b[k] = (got + keep[k].astype(F32)).astype(BF16)
            io_copy(k).start()
            yrecv[k] = (got + ring_a[k].astype(F32)).astype(BF16)
            x_copy(k).start()
            here_copy(k).start()

    def step_c(k):
        @pl.when(outer)
        def _():
            io_copy(k).wait_recv()
            yrecv[k] = (keep[k].astype(F32) + ring_a[k].astype(F32)).astype(BF16)
            x_copy(k).start()
            here_copy(k).start()

    def comm(t):
        for lag, step in ((0, step_y), (2, step_a), (4, step_b), (6, step_c)):
            @pl.when(jnp.logical_and(t >= lag, t < n_chunks + lag))
            def _(step=step, lag=lag):
                step(t - lag)

    def gb_copy(j):
        return rc(gbuf.at[j, pl.ds(0, rows), :], gbuf.at[j, pl.ds(rows, rows), :], S_GB + j, core_dev)

    def wgrad(j, w):
        gb_copy(j).wait_recv()
        for n in range(per_block):
            both = nn_dot(ht[w], gbuf[j, :, n * CHUNK : (n + 1) * CHUNK])
            k = j * per_block + n
            ysend[k] = both[:half].astype(BF16)
            y_copy(k).start()
            keep[k] = both[half:].astype(BF16)

    for cp in ht_copies[:4]:
        cp.wait_recv()

    def back_hidden(j, carry):
        cols = pl.ds(pl.multiple_of(j * width, width), width)
        ga[...] = nt_dot(down_own, wdown[cols, :])
        for i in range(4):
            r = slice(i * patches, (i + 1) * patches)
            gbuf[j, r, :] = (ga[i : i + 1, :] * slope[r, cols].astype(F32)).astype(BF16)
        gb_copy(j).start()

        @pl.when(j > 0)
        def _():
            wgrad(j - 1, 0)

        return carry

    lax.fori_loop(0, n_wide, back_hidden, 0)
    wgrad(n_wide - 1, 0)

    msg_b[...] = jnp.zeros_like(msg_b)
    for block in range(DP):
        for q in range(3):
            lo = block * 3 * lanes + q * lanes
            msg_b[block, 4 * q : 4 * q + 4, :] = asum[0:4, lo : lo + lanes]
    for block in range(DP):
        send_b[block // 2, block % 2] = msg_b[block].astype(BF16)
    recv_b[x, yz] = send_b[y * 2 + x]
    b_copies = []
    for k, yy, xx, zz in others():
        b_copies.append(rc(send_b.at[yy * 2 + xx], recv_b.at[x, yz], S_B + k, at(yy, xx, c, zz)))
        b_copies[-1].start()


    gh[...] = jnp.zeros_like(gh)

    def back_up(j, carry):
        cols = pl.ds(pl.multiple_of(j * width, width), width)
        gh[...] += nt_dot(gbuf[j, 0:rows, :], wup[:, cols])
        return carry

    lax.fori_loop(0, n_wide, back_up, 0)
    comm(0)

    for i in range(4):
        r = slice(i * patches, (i + 1) * patches)
        n, s = normalized(resid[r, :])
        gy = gh[r, :]
        gacc[1:2, :] += jnp.sum(gy * n, axis=0, keepdims=True)
        gyg = gy * gain_two
        grad = s * (gyg - jnp.mean(gyg, axis=-1, keepdims=True) - n * jnp.mean(gyg * n, axis=-1, keepdims=True))
        grad = grad + gp_own[i : i + 1, :]
        resid[r, :] = grad
        gbuf[n_wide, r, :] = grad.astype(BF16)
    gb_copy(n_wide).start()
    comm(1)
    gatt[...] = nt_dot(gbuf[n_wide, 0:rows, :], wout[...]).astype(BF16)
    for cp in ht_copies[4:8]:
        cp.wait_recv()
    wgrad(n_wide, 1)
    comm(2)

    def back_attention(i, carry):
        r = img_rows(i)
        for p in range(pairs):
            cols = slice(p * lanes, (p + 1) * lanes)
            q = two_heads(proj[r, cols])
            k = proj[r, width + p * lanes : width + (p + 1) * lanes]
            v = proj[r, 2 * width + p * lanes : 2 * width + (p + 1) * lanes]
            da = two_heads(gatt[r, cols])
            prob = probs[i * pairs + p]
            dprob = nt_dot(da, v)
            ds = prob * (dprob - jnp.sum(dprob * prob, axis=-1, keepdims=True))
            ds = ds.astype(BF16)
            gbuf[n_wide + 3, r, cols] = tn_dot(prob.astype(BF16), da).astype(BF16)
            gbuf[n_wide + 1, r, cols] = (fold_heads(nn_dot(ds, k)) * score_scale).astype(BF16)
            gbuf[n_wide + 2, r, cols] = (tn_dot(ds, q) * score_scale).astype(BF16)
        comm(3 + i)
        return carry

    lax.fori_loop(0, 4, back_attention, 0)
    for n in range(3):
        gb_copy(n_wide + 1 + n).start()
    gh[...] = jnp.zeros_like(gh)

    def back_proj(n, carry):
        cols = pl.ds(pl.multiple_of(n * width, width), width)
        gh[...] += nt_dot(gbuf[n_wide + 1 + n, 0:rows, :], wqkv[:, cols])
        comm(9 + n)
        return carry

    for cp in ht_copies[8:12]:
        cp.wait_recv()
    wgrad(n_wide + 1, 2)
    comm(7)
    wgrad(n_wide + 2, 2)
    comm(8)
    wgrad(n_wide + 3, 2)
    lax.fori_loop(0, 3, back_proj, 0)

    for i in range(4):
        r = slice(i * patches, (i + 1) * patches)
        n, s = normalized(tok[r, :].astype(F32))
        gy = gh[r, :]
        gacc[0:1, :] += jnp.sum(gy * n, axis=0, keepdims=True)
        gyg = gy * gain_one
        grad = s * (gyg - jnp.mean(gyg, axis=-1, keepdims=True) - n * jnp.mean(gyg * n, axis=-1, keepdims=True))
        tok[r, :] = (resid[r, :] + grad).astype(BF16)
    tg_copy = rc(tok.at[own_rows(1 - x)], token_out.at[x], S_TG, x_dev)
    tg_copy.start()
    tg_here = pltpu.make_async_copy(tok.at[own_rows(x)], token_out.at[x], load_sem.at[9])
    tg_here.start()

    gx_send[...] = jnp.zeros_like(gx_send)
    for n in range(2):
        for q in range(pieces):
            row = n * pieces + q
            gx_send[0, row : row + 1, :] = gacc[n : n + 1, q * lanes : (q + 1) * lanes]
    recv_g[x, yz] = gx_send[0]
    g_copies = []
    for k, yy, xx, zz in others():
        g_copies.append(rc(recv_g.at[x, yz], recv_g.at[x, yz], S_G + k, at(yy, xx, c, zz)))
        g_copies[-1].start()
    comm(12)

    for cp in b_copies:
        cp.wait_recv()
    bx_copy = rc(recv_b.at[:, :, 1 - c], recv_b2, S_BX, core_dev)
    bx_copy.start()
    sb_row = lax.broadcasted_iota(jnp.int32, (96, 128), 0)
    sb_col = lax.broadcasted_iota(jnp.int32, (96, 128), 1)
    pick_b = ((sb_row >> 2) & 7) * 16 + (sb_row >> 5) * 4 + (sb_row & 3)
    select_b = (sb_col == pick_b).astype(F32).astype(BF16)
    comm(13)
    bx_copy.wait_recv()
    for m in range(2):
        for src, cc in ((recv_b[m, :, c], c), (recv_b2[m], 1 - c)):
            got = nn_dot(select_b, src.reshape(128, lanes)).astype(BF16)
            to = pl.ds(pl.multiple_of(cc * 32, 32), 32)
            for q in range(3):
                as_mat[to, q * lanes : (q + 1) * lanes] = got[q * 32 : (q + 1) * 32]
        down_stage[m] = tn_dot(as_mat[...], downs[m]).astype(BF16)
    down_copy = pltpu.make_async_copy(down_stage, down_out, load_sem.at[10])
    down_copy.start()
    comm(14)

    for cp in g_copies:
        cp.wait_recv()
    for m in range(2):
        total = recv_g[m, 0]
        for n in range(1, 8):
            total = total + recv_g[m, n]
        gx_send[m] = total
    gx_copy = rc(gx_send, gx_recv, S_GX, core_dev)
    gx_copy.start()

    def drain(t, carry):
        comm(t)
        return carry

    lax.fori_loop(15, n_chunks + 6, drain, 0)
    gx_copy.wait_recv()
    total = gx_send[...] + gx_recv[...]
    for m in range(2):
        flat = jnp.concatenate(
            [jnp.concatenate([total[m, n * pieces + q : n * pieces + q + 1] for q in range(pieces)], axis=1) for n in range(2)],
            axis=0,
        )
        share = width // DP
        own = flat[:, 0:share]
        for d in range(1, DP):
            own = jnp.where(dp == d, flat[:, d * share : (d + 1) * share], own)
        gain_stage[m, 0:2, 0:share] = own
    gain_copy = pltpu.make_async_copy(gain_stage, gain_out, load_sem.at[11])
    gain_copy.start()

    def finish(k, carry):
        y_copy(k).wait_send()
        here_copy(k).wait()
        x_copy(k).wait()

        @pl.when(outer)
        def _():
            oi_copy(k).wait_send()

        @pl.when(inner)
        def _():
            ii_copy(k).wait_send()
            io_copy(k).wait_send()

        return carry

    lax.fori_loop(0, n_chunks, finish, 0)
    for cp in a_copies + b_copies + ht_copies + g_copies + [tok_send, pos_send, ax_copy, bx_copy, gx_copy]:
        cp.wait_send()
    for j in range(n_blocks):
        gb_copy(j).wait_send()
    tg_copy.wait()
    tg_here.wait()
    down_copy.wait()
    loss_copy.wait()
    gain_copy.wait()


def layer_call(tokens, positions, missing, wqkv, wout, wup, wdown, gains):
    own, patches = positions.shape
    width = tokens.shape[2]
    hidden = wup.shape[2]
    rows = 2 * own * patches
    items = missing.shape[0]
    n_blocks = hidden // width + 4
    n_chunks = n_blocks * (width // CHUNK)
    piece = (n_chunks, width // 4, CHUNK)
    vm = pltpu.VMEM
    any_spec = pl.BlockSpec(memory_space=pl.ANY)
    n_sems = S_Y + 5 * n_chunks
    scratch = [
        vm((own, patches), jnp.int32), vm((1, items), jnp.int32), vm((2, width), F32), vm((2, 8, 128), F32), vm((8, 128), F32),
        vm((width, 3 * width), BF16), vm((width, width), BF16), vm((width, hidden), BF16), vm((hidden, width), BF16),
        vm((rows, width), BF16),
        vm((2, 8, 128), F32),
        vm((rows, width), BF16),
        vm((rows, 3 * width), BF16),
        vm((4 * (HEADS // 2), 2 * patches, patches), F32),
        vm((rows, width), BF16),
        vm((rows, width), F32),
        vm((rows, width), BF16),
        vm((rows, hidden), BF16),
        vm((8, hidden), F32),
        vm((8, width), F32),
        vm((16, width), F32),
        vm((32, 128), F32),
        vm((2, 2, 8, 32, 128), BF16),
        vm((8, 16, 128), F32),
        vm((4, 2, 16, 128), BF16),
        vm((2, 8, 2, 16, 128), BF16),
        vm((2, 8, 16, 128), BF16),
        vm((2, items, width), BF16),
        vm((2, items, width), BF16),
        vm((2, items, width), BF16),
        vm((16, width), F32),
        vm((8, width), F32),
        vm((3, width, rows), BF16),
        vm((3, width // 2, 2 * rows), BF16),
        vm((n_blocks, 2 * rows, width), BF16),
        vm((rows, width), BF16),
        vm((rows, width), F32),
        vm((8, width), F32),
        vm((2, 8, 16, 128), F32),
        vm((2, 16, 128), F32),
        vm((2, 16, 128), F32),
        vm((items, hidden // DP), BF16),
        vm((2, hidden // DP, width), BF16),
        vm(piece, BF16), vm(piece, BF16), vm(piece, BF16), vm(piece, BF16), vm(piece, BF16),
        pltpu.SemaphoreType.DMA((12,)),
        pltpu.SemaphoreType.DMA((n_chunks,)),
        pltpu.SemaphoreType.DMA((n_sems,)),
        pltpu.SemaphoreType.DMA((n_sems,)),
    ]
    return pl.pallas_call(
        layer_kernel,
        out_shape=(
            jax.ShapeDtypeStruct((2, width // DP, n_chunks * CHUNK), BF16),
            jax.ShapeDtypeStruct((2, hidden // DP, width), BF16),
            jax.ShapeDtypeStruct((2, own * patches, width), BF16),
            jax.ShapeDtypeStruct((2, 8, 128), F32),
            jax.ShapeDtypeStruct((8, 128), F32),
        ),
        in_specs=[any_spec] * 8,
        out_specs=(any_spec,) * 5,
        scratch_shapes=scratch,
        compiler_params=pltpu.CompilerParams(
            collective_id=0, has_side_effects=True, vmem_limit_bytes=62 * 2**20
        ),
    )(tokens, positions, missing.reshape(1, items), wqkv, wout, wup, wdown, gains)


def widen_kernel(
    grads, down, tok, gain, loss, qkv_o, out_o, up_o, down_o, tok_o, gain_o, loss_o,
    grads_v, down_v, tok_v, gain_v, loss_v, qkv_v, out_v, up_v, down_w, tok_w, in_sem, out_sem,
):
    hidden, width = up_v.shape[2], out_v.shape[2]
    spans = ((0, hidden, up_v, up_o), (hidden, width, out_v, out_o), (hidden + width, 3 * width, qkv_v, qkv_o))
    moves = [(loss, loss_v, None, None, None), (gain, gain_v, None, None, None)]
    for m in range(2):
        moves.append((tok.at[m], tok_v.at[m], tok_w.at[m], tok_o.at[m], None))
        moves.append((down.at[m], down_v.at[m], down_w.at[m], down_o.at[m], None))
        for lo, size, wide_v, wide_o in spans:
            moves.append(
                (grads.at[m, :, pl.ds(lo, size)], grads_v.at[m, :, pl.ds(lo, size)], wide_v.at[m], wide_o.at[m], None)
            )
    ins = [pltpu.make_async_copy(move[0], move[1], in_sem.at[n]) for n, move in enumerate(moves)]
    for cp in ins:
        cp.start()
    outs = []
    for n, (_, narrow, wide, dst, _) in enumerate(moves):
        ins[n].wait()
        if dst is None:
            continue
        wide[...] = narrow[...].astype(F32)
        outs.append(pltpu.make_async_copy(wide, dst, out_sem.at[n]))
        outs[-1].start()
    loss_o[...] = loss_v[0:1, 0:1]
    gain_o[...] = gain_v[:, 0:2, 0 : gain_o.shape[2]]
    for cp in outs:
        cp.wait()


def widen_call(grads, down, tok, gain, loss, width, hidden):
    vm = pltpu.VMEM
    any_spec = pl.BlockSpec(memory_space=pl.ANY)
    vmem_spec = pl.BlockSpec(memory_space=pltpu.VMEM)
    rows = width // DP
    shapes = ((2, rows, 3 * width), (2, rows, width), (2, rows, hidden), down.shape, tok.shape)
    return pl.pallas_call(
        widen_kernel,
        out_shape=tuple(jax.ShapeDtypeStruct(shape, F32) for shape in shapes + ((2, 2, rows), (1, 1))),
        in_specs=[any_spec] * 5,
        out_specs=(any_spec,) * 5 + (vmem_spec,) * 2,
        scratch_shapes=[vm(v.shape, v.dtype) for v in (grads, down, tok, gain, loss)]
        + [vm(shape, F32) for shape in shapes]
        + [pltpu.SemaphoreType.DMA((16,)), pltpu.SemaphoreType.DMA((16,))],
        compiler_params=pltpu.CompilerParams(vmem_limit_bytes=62 * 2**20),
    )(grads, down, tok, gain, loss)


def fused(tokens, positions, missing, qkv_weight, out_weight, up_weight, down_weight, norm_gains):
    grads, down, tok, gain, loss = layer_call(
        tokens, positions, missing, qkv_weight, out_weight, up_weight, down_weight, norm_gains
    )
    qkv, out, up, down, tok, gain, loss = widen_call(
        grads, down, tok, gain, loss, tokens.shape[2], up_weight.shape[2]
    )
    return (loss.reshape(()), tok, qkv, out, up, down, gain)


def lead_dot(left, right):
    return lax.dot_general(
        left, right, (((0,), (0,)), ((), ())), preferred_element_type=jnp.float32
    )


def tail_dot(left, right):
    return lax.dot_general(
        left, right, (((1,), (1,)), ((), ())), preferred_element_type=jnp.float32
    )


def norm_gain(values, gain):
    centre = values - jnp.mean(values, axis=-1, keepdims=True)
    spread = jnp.mean(centre * centre, axis=-1, keepdims=True)
    return centre * lax.rsqrt(spread + eps_norm) * gain


def unit_rows(pooled):
    return pooled * lax.rsqrt(jnp.sum(pooled * pooled, axis=1, keepdims=True) + eps_norm)


def gelu_exact(values):
    return jax.nn.gelu(values, approximate=False)


def alibi_bias(positions):
    grid_rows = (positions // GRID_W).astype(jnp.float32)
    grid_cols = (positions % GRID_W).astype(jnp.float32)
    row_gap = grid_rows[:, :, None] - grid_rows[:, None, :]
    col_gap = grid_cols[:, :, None] - grid_cols[:, None, :]
    distance = jnp.sqrt(row_gap * row_gap + col_gap * col_gap)
    slopes = jnp.exp2(-8.0 * (jnp.arange(HEADS) + 1).astype(jnp.float32) / HEADS)
    return -slopes[None, :, None, None] * distance[:, None, :, :]


def log_total(logits, valid_cols, valid_rows):
    row_max = jnp.max(logits, axis=1, keepdims=True)
    summed = jnp.sum(valid_cols[None, :] * jnp.exp(logits - row_max), axis=1) + (1.0 - valid_rows)
    return row_max[:, 0] + jnp.log(summed)


def row_grads(logits, log_sums, valid_rows, valid_cols, match, total_items):
    soft = valid_cols[None, :] * jnp.exp(logits - log_sums[:, None])
    return (valid_rows[:, None] / (2.0 * total_items) * (soft - match)).astype(jnp.bfloat16)


def block_forward(token_rows, alibi_terms, qkv_weight, out_weight, up_weight, down_weight, gains):
    row_count, model_width = token_rows.shape
    images, patches = (alibi_terms.shape[0], alibi_terms.shape[2])
    head_dim = model_width // HEADS
    score_scale = head_dim ** (-0.5)
    start_rows = token_rows.astype(jnp.float32)
    normed_one = norm_gain(start_rows, gains[0]).astype(jnp.bfloat16)
    projected = jnp.dot(normed_one, qkv_weight, preferred_element_type=jnp.float32).astype(
        jnp.bfloat16
    )
    queries = projected[:, :model_width].reshape(images, patches, HEADS, head_dim)
    key_rows = projected[:, model_width : 2 * model_width].reshape(images, patches, HEADS, head_dim)
    value_rows = projected[:, 2 * model_width :].reshape(images, patches, HEADS, head_dim)
    scores = jnp.einsum("iqhd,ikhd->ihqk", queries, key_rows, preferred_element_type=jnp.float32)
    attn_probs = jax.nn.softmax(scores * score_scale + alibi_terms, axis=-1)
    probs_low = attn_probs.astype(jnp.bfloat16)
    attended = jnp.einsum(
        "ihqk,ikhd->iqhd", probs_low, value_rows, preferred_element_type=jnp.float32
    )
    attended = attended.reshape(row_count, model_width).astype(jnp.bfloat16)
    residual = start_rows + jnp.dot(attended, out_weight, preferred_element_type=jnp.float32)
    normed_two = norm_gain(residual, gains[1]).astype(jnp.bfloat16)
    hidden_pre = jnp.dot(normed_two, up_weight, preferred_element_type=jnp.float32)
    active = gelu_exact(hidden_pre).astype(jnp.bfloat16)
    out_rows = residual + jnp.dot(active, down_weight, preferred_element_type=jnp.float32)
    saved = (
        start_rows,
        normed_one,
        projected,
        attn_probs,
        probs_low,
        attended,
        residual,
        normed_two,
        hidden_pre,
        active,
    )
    return (out_rows, saved)


def block_backward(grad_rows, saved, qkv_weight, out_weight, up_weight, down_weight, gains):
    (
        start_rows,
        normed_one,
        projected,
        attn_probs,
        probs_low,
        attended,
        residual,
        normed_two,
        hidden_pre,
        active,
    ) = saved
    images, head_count, patches = (attn_probs.shape[0], attn_probs.shape[1], attn_probs.shape[2])
    row_count, model_width = grad_rows.shape
    head_dim = model_width // head_count
    score_scale = head_dim ** (-0.5)
    down_in = grad_rows.astype(jnp.bfloat16)
    grad_down = lead_dot(active, down_in)
    grad_active = tail_dot(down_in, down_weight)
    _, gelu_back = jax.vjp(gelu_exact, hidden_pre)
    grad_hidden = gelu_back(grad_active)[0].astype(jnp.bfloat16)
    grad_up = lead_dot(normed_two, grad_hidden)
    grad_h_two = tail_dot(grad_hidden, up_weight)
    _, norm_two_back = jax.vjp(norm_gain, residual, gains[1])
    grad_mid, gain_two = norm_two_back(grad_h_two)
    grad_residual = grad_rows + grad_mid
    attn_in = grad_residual.astype(jnp.bfloat16)
    grad_out = lead_dot(attended, attn_in)
    grad_att = (
        tail_dot(attn_in, out_weight)
        .astype(jnp.bfloat16)
        .reshape(images, patches, head_count, head_dim)
    )
    queries = projected[:, :model_width].reshape(images, patches, head_count, head_dim)
    key_rows = projected[:, model_width : 2 * model_width].reshape(
        images, patches, head_count, head_dim
    )
    value_rows = projected[:, 2 * model_width :].reshape(images, patches, head_count, head_dim)
    grad_values = jnp.einsum(
        "ihqk,iqhd->ikhd", probs_low, grad_att, preferred_element_type=jnp.float32
    )
    grad_probs = jnp.einsum(
        "iqhd,ikhd->ihqk", grad_att, value_rows, preferred_element_type=jnp.float32
    )
    grad_scores = attn_probs * (
        grad_probs - jnp.sum(grad_probs * attn_probs, axis=-1, keepdims=True)
    )
    grad_scores = grad_scores.astype(jnp.bfloat16)
    grad_queries = (
        jnp.einsum("ihqk,ikhd->iqhd", grad_scores, key_rows, preferred_element_type=jnp.float32)
        * score_scale
    )
    grad_keys = (
        jnp.einsum("ihqk,iqhd->ikhd", grad_scores, queries, preferred_element_type=jnp.float32)
        * score_scale
    )
    grad_proj = jnp.concatenate(
        [
            grad_queries.reshape(row_count, model_width),
            grad_keys.reshape(row_count, model_width),
            grad_values.reshape(row_count, model_width),
        ],
        axis=1,
    ).astype(jnp.bfloat16)
    grad_qkv = lead_dot(normed_one, grad_proj)
    grad_h_one = tail_dot(grad_proj, qkv_weight)
    _, norm_one_back = jax.vjp(norm_gain, start_rows, gains[0])
    grad_first, gain_one = norm_one_back(grad_h_one)
    weight_grads = (grad_qkv, grad_out, grad_up, grad_down, jnp.stack([gain_one, gain_two]))
    return (grad_residual + grad_first, weight_grads)


def local(tokens, positions, missing, qkv_weight, out_weight, up_weight, down_weight, norm_gains):
    own_images = positions.shape[0]
    model_width = tokens.shape[2]
    patches = tokens.shape[1] // own_images
    first_row = lax.axis_index(("dp", "rep")) * own_images
    alibi_terms = alibi_bias(positions)
    saved_list = []
    pooled_list = []
    normed = []
    for modality in range(2):
        out_rows, saved = block_forward(
            tokens[modality],
            alibi_terms,
            qkv_weight[modality],
            out_weight[modality],
            up_weight[modality],
            down_weight[modality],
            norm_gains[modality],
        )
        pooled = jnp.sum(out_rows.reshape(own_images, patches, model_width), axis=1)
        saved_list.append(saved)
        pooled_list.append(pooled)
        normed.append(unit_rows(pooled).astype(jnp.bfloat16))
    valid_all = 1.0 - missing.astype(jnp.float32)
    total_items = float(missing.shape[0])
    valid_own = lax.dynamic_slice_in_dim(valid_all, first_row, own_images)
    radar_all, optic_all = (
        lax.all_gather(normed[0], ("dp", "rep"), axis=0, tiled=True),
        lax.all_gather(normed[1], ("dp", "rep"), axis=0, tiled=True),
    )
    images_all = radar_all.shape[0]
    match_own = (
        lax.broadcasted_iota(jnp.int32, (own_images, images_all), 0) + first_row
        == lax.broadcasted_iota(jnp.int32, (own_images, images_all), 1)
    ).astype(jnp.float32)
    logits_r = tail_dot(normed[0], optic_all) * inv_temp
    logits_o = tail_dot(normed[1], radar_all) * inv_temp
    lse_r = log_total(logits_r, valid_all, valid_own)
    lse_o = log_total(logits_o, valid_all, valid_own)
    item_terms = valid_own * (
        lse_r
        - jnp.sum(logits_r * match_own, axis=1)
        + lse_o
        - jnp.sum(logits_o * match_own, axis=1)
    )
    grad_lr = row_grads(logits_r, lse_r, valid_own, valid_all, match_own, total_items)
    grad_lo = row_grads(logits_o, lse_o, valid_own, valid_all, match_own, total_items)
    grad_ur = jnp.dot(grad_lr, optic_all, preferred_element_type=jnp.float32) * inv_temp
    grad_uo = jnp.dot(grad_lo, radar_all, preferred_element_type=jnp.float32) * inv_temp
    summed_terms = lax.psum(jnp.sum(item_terms), ("dp", "rep"))
    loss_value = summed_terms / (2.0 * total_items)
    share_o = lead_dot(grad_lr, normed[0]) * inv_temp
    share_r = lead_dot(grad_lo, normed[1]) * inv_temp
    back_r, back_o = (
        lax.psum_scatter(share_r, ("dp", "rep"), scatter_dimension=0, tiled=True),
        lax.psum_scatter(share_o, ("dp", "rep"), scatter_dimension=0, tiled=True),
    )
    grad_ur = grad_ur + back_r
    grad_uo = grad_uo + back_o
    grad_units = (grad_ur, grad_uo)
    token_list = []
    block_grads = []
    for modality in range(2):
        _, unit_back = jax.vjp(unit_rows, pooled_list[modality])
        grad_pooled = unit_back(grad_units[modality])[0]
        grad_rows = jnp.broadcast_to(grad_pooled[:, None, :], (own_images, patches, model_width))
        grad_rows = grad_rows.reshape(own_images * patches, model_width)
        grad_tokens, weight_grads = block_backward(
            grad_rows,
            saved_list[modality],
            qkv_weight[modality],
            out_weight[modality],
            up_weight[modality],
            down_weight[modality],
            norm_gains[modality],
        )
        token_list.append(grad_tokens)
        block_grads.append(list(weight_grads))
    stacked = [jnp.stack([block_grads[0][slot], block_grads[1][slot]]) for slot in range(5)]
    shares = (
        lax.psum_scatter(stacked[0], "dp", scatter_dimension=1, tiled=True),
        lax.psum_scatter(stacked[1], "dp", scatter_dimension=1, tiled=True),
        lax.psum_scatter(stacked[2], "dp", scatter_dimension=1, tiled=True),
        lax.psum_scatter(stacked[3], "dp", scatter_dimension=1, tiled=True),
        lax.psum_scatter(stacked[4], "dp", scatter_dimension=2, tiled=True),
    )
    summed = (
        lax.psum(shares[0].astype(jnp.bfloat16), "rep").astype(jnp.float32),
        lax.psum(shares[1].astype(jnp.bfloat16), "rep").astype(jnp.float32),
        lax.psum(shares[2].astype(jnp.bfloat16), "rep").astype(jnp.float32),
        lax.psum(shares[3].astype(jnp.bfloat16), "rep").astype(jnp.float32),
        lax.psum(shares[4].astype(jnp.bfloat16), "rep").astype(jnp.float32),
    )
    stacked = list(summed)
    token_grads = jnp.stack(token_list)
    return (loss_value, token_grads, stacked[0], stacked[1], stacked[2], stacked[3], stacked[4])


def solution(mesh):
    in_specs = (P(None, ("dp", "rep"), None), P(("dp", "rep"), None), P(), P(), P(), P(), P(), P())
    out_specs = (
        P(),
        P(None, ("dp", "rep"), None),
        P(None, "dp", None),
        P(None, "dp", None),
        P(None, "dp", None),
        P(None, "dp", None),
        P(None, None, "dp"),
    )
    one_kernel = mesh.shape["dp"] == DP and mesh.shape["rep"] == REP
    step = fused if one_kernel else local
    return jax.shard_map(step, mesh=mesh, in_specs=in_specs, out_specs=out_specs, check_vma=False)
```

```python
import functools

import jax
import jax.numpy as jnp
from jax import lax
from jax.experimental import pallas as pl
from jax.experimental.pallas import tpu as pltpu
from jax.sharding import PartitionSpec as P

HEADS = 12
GRID_W = 12
MESH = pl.DeviceIdType.MESH
F32 = jnp.float32
BF16 = jnp.bfloat16

eps_norm = 1e-06
inv_temp = 32.0
SQRT_HALF = 0.7071067811865476
INV_SQRT_TWO_PI = 0.3989422804014327
HALF_LOG2_E = -0.7213475204444817

DP = 8
REP = 4
CHUNK = 256


def nt_dot(left, right):
    return lax.dot_general(left, right, (((1,), (1,)), ((), ())), preferred_element_type=F32)


def tn_dot(left, right):
    return lax.dot_general(left, right, (((0,), (0,)), ((), ())), preferred_element_type=F32)


def nn_dot(left, right):
    return jnp.dot(left, right, preferred_element_type=F32)


def normalized(values):
    centre = values - jnp.mean(values, axis=-1, keepdims=True)
    scale = lax.rsqrt(jnp.mean(centre * centre, axis=-1, keepdims=True) + eps_norm)
    return centre * scale, scale


def gelu_and_slope(values):
    cdf = 0.5 + 0.5 * lax.erf(values * SQRT_HALF)
    return values * cdf, cdf + values * (jnp.exp2(values * values * HALF_LOG2_E) * INV_SQRT_TWO_PI)


S_TOK, S_POS, S_A, S_AX, S_B, S_BX, S_G, S_GX = 0, 1, 2, 18, 19, 35, 36, 52
S_HT, S_GB, S_TG = 53, 65, 73
S_Y = 74


def layer_kernel(
    tokens, positions_h, missing_h, wqkv_h, wout_h, wup_h, wdown_h, gains_h,
    grad_out, down_out, token_out, gain_out, loss_out,
    positions, missing, gains, wqkv, wout, wup, wdown, tok, posb, h_one, proj, probs, att, resid, h_two, slope,
    asum, rsum, pool, msg_a, recv_a, msg_b, send_b, recv_b, recv_b2, units, downs, downs_lo, ga, gp_own,
    h_t, ht, gbuf, gatt, gh, gacc, recv_g, gx_send, gx_recv, as_mat,
    ysend, keep, yrecv, ring_a, ring_b,
    load_sem, out_sem, ss, rs,
):
    width = h_one.shape[1]
    hidden = wup.shape[1]
    rows = h_one.shape[0]
    half = rows // 2
    patches = half // 2
    pairs = HEADS // 2
    lanes = 128
    pieces = width // lanes
    items = missing.shape[1]
    n_wide = hidden // width
    n_blocks = n_wide + 4
    per_block = width // CHUNK
    n_chunks = n_blocks * per_block
    score_scale = (width // HEADS) ** -0.5

    S_OI, S_II, S_IO, S_X = (S_Y + n_chunks * n for n in range(1, 5))

    dp = lax.axis_index("dp")
    z = lax.axis_index("rep")
    c = dp % 2
    x = (dp // 2) % 2
    y = dp // 4
    yz = y * 4 + z

    def at(yy, xx, cc, zz):
        return (yy * 4 + xx * 2 + cc, zz)

    core_dev = at(y, x, 1 - c, z)
    x_dev = at(y, 1 - x, c, z)
    y_dev = at(1 - y, x, c, z)
    inner = jnp.logical_and(z >= 1, z <= 2)
    outer = jnp.logical_not(inner)
    high = z // 2
    inner_peer = at(y, x, c, 3 - z)
    outer_peer = at(y, x, c, 3 * high)
    inward_peer = at(y, x, c, 1 + high)

    def others():
        for k in range(1, 16):
            yield k, y ^ (k & 1), x ^ ((k >> 1) & 1), (z + (k >> 2)) % 4

    def rc(src, dst, idx, dev):
        return pltpu.make_async_remote_copy(
            src_ref=src, dst_ref=dst, send_sem=ss.at[idx], recv_sem=rs.at[idx],
            device_id=dev, device_id_type=MESH,
        )

    def own_rows(xx):
        return pl.ds(pl.multiple_of(xx * half, half), half)

    barrier = pltpu.get_barrier_semaphore()
    for k, yy, xx, zz in others():
        pl.semaphore_signal(barrier, inc=1, device_id=at(yy, xx, c, zz), device_id_type=MESH)
    pl.semaphore_signal(barrier, inc=1, device_id=core_dev, device_id_type=MESH)
    early = [
        (positions_h, positions), (tokens.at[x], tok.at[own_rows(x)]), (gains_h.at[x], gains), (wqkv_h.at[x], wqkv),
        (missing_h, missing),
    ]
    late = [(wout_h.at[x], wout), (wup_h.at[x], wup), (wdown_h.at[x], wdown)]
    loads = [pltpu.make_async_copy(src, dst, load_sem.at[n]) for n, (src, dst) in enumerate(early + late)]
    for load in loads[: len(early)]:
        load.start()
    load_pos, load_tok, load_gains, load_qkv, load_missing, load_out, load_up, load_down = loads
    posb[x] = jnp.zeros((8, lanes), F32)
    asum[...] = jnp.zeros_like(asum)
    rsum[...] = jnp.zeros_like(rsum)
    pool[...] = jnp.zeros_like(pool)
    gacc[...] = jnp.zeros_like(gacc)

    load_pos.wait()
    cells = positions[...].astype(F32)
    cell_rows = jnp.floor((cells + 0.5) * (1.0 / GRID_W))
    cell_cols = cells - GRID_W * cell_rows
    posb[x, 0:2, 0:patches] = cell_rows
    posb[x, 2:4, 0:patches] = cell_cols

    pl.semaphore_wait(barrier, 16)
    tok_send = rc(tokens.at[1 - x], tok.at[own_rows(x)], S_TOK, x_dev)
    pos_send = rc(posb.at[x], posb.at[x], S_POS, x_dev)
    tok_send.start()
    pos_send.start()

    low_lanes = lax.broadcasted_iota(jnp.int32, (patches, lanes), 1) < lanes // 2
    mask_low = low_lanes.astype(F32).astype(BF16)
    mask_high = (1.0 - low_lanes.astype(F32)).astype(BF16)

    def two_heads(values):
        return jnp.concatenate([values * mask_low, values * mask_high], axis=0)

    def fold_heads(values):
        return jnp.where(low_lanes, values[:patches], values[patches:])

    def img_rows(i):
        return pl.ds(pl.multiple_of(i * patches, patches), patches)

    load_tok.wait()
    load_gains.wait()
    gain_one = gains[0:1, :]
    gain_two = gains[1:2, :]

    def attention(xx):
        def image(j, carry):
            r = img_rows(xx * 2 + j)
            cr = jnp.broadcast_to(posb[xx, pl.ds(j, 1), :], (lanes, lanes))
            cc = jnp.broadcast_to(posb[xx, pl.ds(j + 2, 1), :], (lanes, lanes))
            row_gap = cr.T - cr
            col_gap = cc.T - cc
            dist = jnp.sqrt(row_gap * row_gap + col_gap * col_gap)[:patches, :patches]
            raw = []
            for p in range(pairs):
                q = two_heads(proj[r, p * lanes : (p + 1) * lanes])
                raw.append(nt_dot(q, proj[r, width + p * lanes : width + (p + 1) * lanes]))
            soft = []
            for p in range(pairs):
                slopes = [2.0 ** (-8.0 * (2 * p + h + 1) / HEADS) for h in range(2)]
                alibi = jnp.concatenate([dist * -slopes[0], dist * -slopes[1]], axis=0)
                s = raw[p] * score_scale + alibi
                e = jnp.exp(s - jnp.max(s, axis=-1, keepdims=True))
                prob = e * (1.0 / jnp.sum(e, axis=-1, keepdims=True))
                probs[(xx * 2 + j) * pairs + p] = prob
                soft.append(prob.astype(BF16))
            for p in range(pairs):
                v = proj[r, 2 * width + p * lanes : 2 * width + (p + 1) * lanes]
                att[r, p * lanes : (p + 1) * lanes] = fold_heads(nn_dot(soft[p], v)).astype(BF16)
            return carry

        lax.fori_loop(0, 2, image, 0)

    def wide(j):
        return pl.ds(pl.multiple_of(j * width, width), width)

    def add_pool(j, on):
        a = asum[:, wide(j)] * on
        a_high = a.astype(BF16).astype(F32)
        both = jnp.concatenate([a_high, a - a_high], axis=0).astype(BF16)
        pool[...] += nn_dot(both, wdown[wide(j), :])

    for step in range(2):
        xx = x if step == 0 else 1 - x
        where = own_rows(xx)
        if step == 1:
            tok_send.wait_recv()
            pos_send.wait_recv()
        for j in range(2):
            r = img_rows(xx * 2 + j)
            n, _ = normalized(tok[r, :].astype(F32))
            h_one[r, :] = (n * gain_one).astype(BF16)
        if step == 0:
            load_qkv.wait()
            load_out.start()
            load_up.start()
            load_down.start()
        for n in range(3):
            cols = slice(n * width, (n + 1) * width)
            proj[where, cols] = nn_dot(h_one[where, :], wqkv[:, cols]).astype(BF16)
        attention(xx)
        if step == 0:
            load_out.wait()
        resid[where, :] = tok[where, :].astype(F32) + nn_dot(att[where, :], wout[...])
        for j in range(2):
            i = xx * 2 + j
            r = img_rows(i)
            v = resid[r, :]
            rsum[pl.ds(i, 1), :] = jnp.sum(v, axis=0, keepdims=True)
            n, _ = normalized(v)
            h_two[r, :] = (n * gain_two).astype(BF16)
        if step == 0:
            load_up.wait()
        else:
            load_down.wait()

        def feed(j, carry, where=where, xx=xx, step=step):
            for n in range(width // 256):
                cols = pl.ds(pl.multiple_of(j * width + n * 256, 256), 256)
                pre = nn_dot(h_two[where, :], wup[:, cols])
                act, slp = gelu_and_slope(pre)
                slope[where, cols] = slp.astype(BF16)
                act = act.astype(BF16).astype(F32)
                for i in range(2):
                    asum[pl.ds(xx * 2 + i, 1), cols] = jnp.sum(act[i * patches : (i + 1) * patches], axis=0, keepdims=True)
            if step == 1:
                add_pool(jnp.maximum(j - 1, 0), (j > 0).astype(F32))
            return carry

        lax.fori_loop(0, n_wide, feed, 0)
    add_pool(n_wide - 1, 1.0)

    pooled = rsum[...] + pool[0:8, :] + pool[8:16, :]
    s_own = lax.rsqrt(jnp.sum(pooled * pooled, axis=1, keepdims=True) + eps_norm)
    unit = pooled * s_own
    for q in range(pieces):
        msg_a[4 * q : 4 * q + 4, :] = unit[0:4, q * lanes : (q + 1) * lanes]
    s_high = s_own.astype(BF16).astype(F32)
    msg_a[24:28, :] = jnp.broadcast_to(s_high[0:4], (4, lanes))
    msg_a[28:32, :] = jnp.broadcast_to((s_own - s_high)[0:4], (4, lanes))
    recv_a[c, x, yz] = msg_a[...].astype(BF16)
    a_copies = []
    for k, yy, xx, zz in others():
        a_copies.append(rc(recv_a.at[c, x, yz], recv_a.at[c, x, yz], S_A + k, at(yy, xx, c, zz)))
        a_copies[-1].start()

    msg_b[...] = jnp.zeros_like(msg_b)
    for block in range(DP):
        for q in range(3):
            lo = block * 3 * lanes + q * lanes
            msg_b[block, 4 * q : 4 * q + 4, :] = asum[0:4, lo : lo + lanes]
    for block in range(DP):
        send_b[block // 2, block % 2] = msg_b[block].astype(BF16)
    recv_b[x, yz] = send_b[y * 2 + x]
    ht_copies = []
    for w, src in enumerate((h_two, att, h_one)):
        h_t[w] = src[...].T
        for rel in range(2):
            yy = y if rel == 1 else 1 - y
            for xx in range(2):
                base = yy * (width // 2) + xx * (width // 4)
                mine = pl.ds(pl.multiple_of(base + c * (width // 8), width // 8), width // 8)
                theirs = pl.ds(pl.multiple_of(base + (1 - c) * (width // 8), width // 8), width // 8)
                lo = (rel * 2 + xx) * (width // 8)
                ht[w, lo : lo + width // 8, 0:rows] = h_t[w, mine, :]
                ht_copies.append(
                    rc(
                        h_t.at[w, theirs, :],
                        ht.at[w, pl.ds(lo, width // 8), pl.ds(rows, rows)],
                        S_HT + w * 4 + rel * 2 + xx,
                        core_dev,
                    )
                )
                ht_copies[-1].start()

    n_sel = 8 * 32
    sel_row = lax.broadcasted_iota(jnp.int32, (n_sel, n_sel), 0)
    sel_col = lax.broadcasted_iota(jnp.int32, (n_sel, n_sel), 1)
    pick = ((sel_row >> 2) & 7) * 32 + (sel_row >> 5) * 4 + (sel_row & 3)
    select_a = (sel_col == pick).astype(F32).astype(BF16)

    p_i = lax.broadcasted_iota(jnp.int32, (items, items), 0)
    q_i = lax.broadcasted_iota(jnp.int32, (items, items), 1)
    place = ((((p_i >> 4) & 1) * 4 + ((p_i >> 1) & 1) * 2 + (p_i >> 5)) * 4 + ((p_i >> 2) & 3)) * 2 + (p_i & 1)
    eye = (p_i == q_i).astype(F32)
    load_missing.wait()
    v_nat = 1.0 - missing[...].astype(F32)
    v_col = jnp.sum((q_i == place).astype(F32) * v_nat, axis=1, keepdims=True)
    v_row = jnp.sum(eye * v_col, axis=0, keepdims=True)

    for cp in a_copies:
        cp.wait_recv()
    ax_copy = rc(recv_a.at[c], recv_a.at[c], S_AX, core_dev)
    ax_copy.start()
    b_copies = []
    for k, yy, xx, zz in others():
        b_copies.append(rc(send_b.at[yy * 2 + xx], recv_b.at[x, yz], S_B + k, at(yy, xx, c, zz)))
        b_copies[-1].start()
    ax_copy.wait_recv()

    scales = [[None, None], [None, None]]
    for core in range(2):
        for m in range(2):
            got = nn_dot(select_a, recv_a[core, m].reshape(n_sel, lanes))
            for q in range(pieces):
                units[m, core * 32 : core * 32 + 32, q * lanes : (q + 1) * lanes] = got[q * 32 : q * 32 + 32].astype(BF16)
            scales[m][core] = got[6 * 32 : 7 * 32] + got[7 * 32 :]
    scale_cols = [jnp.concatenate(scales[m], axis=0)[:, 0:1] for m in range(2)]

    u_r, u_o = units[0], units[1]
    logits = nt_dot(u_r, u_o) * inv_temp
    top_r = jnp.max(logits, axis=1, keepdims=True)
    lse_r = top_r + jnp.log(jnp.sum(v_row * jnp.exp(logits - top_r), axis=1, keepdims=True) + (1.0 - v_col))
    top_o = jnp.max(logits, axis=0, keepdims=True)
    lse_o = top_o + jnp.log(jnp.sum(v_col * jnp.exp(logits - top_o), axis=0, keepdims=True) + (1.0 - v_row))
    diag = logits * eye
    terms_r = v_col * (lse_r - jnp.sum(diag, axis=1, keepdims=True))
    terms_o = v_row * (lse_o - jnp.sum(diag, axis=0, keepdims=True))
    loss = (jnp.sum(terms_r, axis=0, keepdims=True) + jnp.sum(terms_o, axis=1, keepdims=True)) / (2.0 * items)
    loss_out[...] = jnp.broadcast_to(loss, loss_out.shape)
    grad_r = (v_col / (2.0 * items) * (v_row * jnp.exp(logits - lse_r) - eye)).astype(BF16)
    grad_ot = (v_row / (2.0 * items) * (v_col * jnp.exp(logits - lse_o) - eye)).astype(BF16)
    grad_u = [
        (nn_dot(grad_r, u_o) + nn_dot(grad_ot, u_o)) * inv_temp,
        (tn_dot(grad_r, u_r) + tn_dot(grad_ot, u_r)) * inv_temp,
    ]
    for m in range(2):
        u = units[m].astype(F32)
        g = grad_u[m]
        gp = scale_cols[m] * (g - u * jnp.sum(u * g, axis=1, keepdims=True))
        high_part = gp.astype(BF16)
        downs[m] = high_part
        downs_lo[m] = (gp - high_part.astype(F32)).astype(BF16)
    own_r = lax.broadcasted_iota(jnp.int32, (16, items), 0)
    own_c = lax.broadcasted_iota(jnp.int32, (16, items), 1)
    mine = jnp.logical_and(own_r < 4, own_c == c * 32 + yz * 4 + own_r).astype(F32).astype(BF16)
    down_own = nn_dot(mine, downs[x])
    gp_own[...] = (down_own + nn_dot(mine, downs_lo[x]))[0:8]
    down_own = down_own.astype(BF16)

    def y_copy(k):
        return rc(ysend.at[k], yrecv.at[k], S_Y + k, y_dev)

    def oi_copy(k):
        return rc(keep.at[k], ring_a.at[k], S_OI + k, inward_peer)

    def ii_copy(k):
        return rc(ring_a.at[k], ring_b.at[k], S_II + k, inner_peer)

    def io_copy(k):
        return rc(ring_b.at[k], ring_a.at[k], S_IO + k, outer_peer)

    def out_cols(k):
        return pl.ds(pl.multiple_of(k * CHUNK, CHUNK), CHUNK)

    quarter = width // 8

    def x_copy(k):
        return rc(
            yrecv.at[k, pl.ds(pl.multiple_of((1 - x) * quarter, quarter), quarter), :],
            grad_out.at[x, :, out_cols(k)], S_X + k, x_dev,
        )

    def here_copy(k):
        return pltpu.make_async_copy(
            yrecv.at[k, pl.ds(pl.multiple_of(x * quarter, quarter), quarter), :],
            grad_out.at[x, :, out_cols(k)], out_sem.at[k],
        )

    def step_y(k):
        y_copy(k).wait_recv()
        keep[k] = (keep[k].astype(F32) + yrecv[k].astype(F32)).astype(BF16)

        @pl.when(outer)
        def _():
            oi_copy(k).start()

    def step_a(k):
        @pl.when(inner)
        def _():
            oi_copy(k).wait_recv()
            ring_a[k] = (ring_a[k].astype(F32) + keep[k].astype(F32)).astype(BF16)
            ii_copy(k).start()

    def step_b(k):
        @pl.when(inner)
        def _():
            ii_copy(k).wait_recv()
            got = ring_b[k].astype(F32)
            ring_b[k] = (got + keep[k].astype(F32)).astype(BF16)
            io_copy(k).start()
            yrecv[k] = (got + ring_a[k].astype(F32)).astype(BF16)
            x_copy(k).start()
            here_copy(k).start()

    def step_c(k):
        @pl.when(outer)
        def _():
            io_copy(k).wait_recv()
            yrecv[k] = (keep[k].astype(F32) + ring_a[k].astype(F32)).astype(BF16)
            x_copy(k).start()
            here_copy(k).start()

    def comm(t):
        for lag, step in ((0, step_y), (2, step_a), (4, step_b), (6, step_c)):
            @pl.when(jnp.logical_and(t >= lag, t < n_chunks + lag))
            def _(step=step, lag=lag):
                step(t - lag)

    def gb_copy(j):
        return rc(gbuf.at[j, pl.ds(0, rows), :], gbuf.at[j, pl.ds(rows, rows), :], S_GB + j, core_dev)

    def wgrad(j, w):
        gb_copy(j).wait_recv()
        for n in range(per_block):
            both = nn_dot(ht[w], gbuf[j, :, n * CHUNK : (n + 1) * CHUNK])
            k = j * per_block + n
            ysend[k] = both[:half].astype(BF16)
            y_copy(k).start()
            keep[k] = both[half:].astype(BF16)

    for cp in ht_copies[:4]:
        cp.wait_recv()

    def back_hidden(j, carry):
        cols = pl.ds(pl.multiple_of(j * width, width), width)
        ga[...] = nt_dot(down_own, wdown[cols, :])
        for i in range(4):
            r = slice(i * patches, (i + 1) * patches)
            gbuf[j, r, :] = (ga[i : i + 1, :] * slope[r, cols].astype(F32)).astype(BF16)
        gb_copy(j).start()

        @pl.when(j > 0)
        def _():
            wgrad(j - 1, 0)

        return carry

    lax.fori_loop(0, n_wide, back_hidden, 0)
    wgrad(n_wide - 1, 0)
    comm(0)

    gh[...] = jnp.zeros_like(gh)

    def back_up(j, carry):
        cols = pl.ds(pl.multiple_of(j * width, width), width)
        gh[...] += nt_dot(gbuf[j, 0:rows, :], wup[:, cols])

        @pl.when(j == 2)
        def _():
            comm(1)

        return carry

    lax.fori_loop(0, n_wide, back_up, 0)

    for i in range(4):
        r = slice(i * patches, (i + 1) * patches)
        n, s = normalized(resid[r, :])
        gy = gh[r, :]
        gacc[1:2, :] += jnp.sum(gy * n, axis=0, keepdims=True)
        gyg = gy * gain_two
        grad = s * (gyg - jnp.mean(gyg, axis=-1, keepdims=True) - n * jnp.mean(gyg * n, axis=-1, keepdims=True))
        grad = grad + gp_own[i : i + 1, :]
        resid[r, :] = grad
        gbuf[n_wide, r, :] = grad.astype(BF16)
    gb_copy(n_wide).start()
    gatt[...] = nt_dot(gbuf[n_wide, 0:rows, :], wout[...]).astype(BF16)
    comm(2)
    for cp in ht_copies[4:8]:
        cp.wait_recv()
    wgrad(n_wide, 1)

    def back_attention(i, carry):
        r = img_rows(i)
        das, dps, dss = [], [], []
        for p in range(pairs):
            da = two_heads(gatt[r, p * lanes : (p + 1) * lanes])
            das.append(da)
            dps.append(nt_dot(da, proj[r, 2 * width + p * lanes : 2 * width + (p + 1) * lanes]))
        for p in range(pairs):
            cols = slice(p * lanes, (p + 1) * lanes)
            prob = probs[i * pairs + p]
            dss.append((prob * (dps[p] - jnp.sum(dps[p] * prob, axis=-1, keepdims=True))).astype(BF16))
            gbuf[n_wide + 3, r, cols] = tn_dot(prob.astype(BF16), das[p]).astype(BF16)
        for p in range(pairs):
            cols = slice(p * lanes, (p + 1) * lanes)
            q = two_heads(proj[r, cols])
            k = proj[r, width + p * lanes : width + (p + 1) * lanes]
            gbuf[n_wide + 1, r, cols] = (fold_heads(nn_dot(dss[p], k)) * score_scale).astype(BF16)
            gbuf[n_wide + 2, r, cols] = (tn_dot(dss[p], q) * score_scale).astype(BF16)
        comm(3 + i)
        return carry

    lax.fori_loop(0, 4, back_attention, 0)
    for n in range(3):
        gb_copy(n_wide + 1 + n).start()
    gh[...] = jnp.zeros_like(gh)

    def back_proj(n, carry):
        cols = pl.ds(pl.multiple_of(n * width, width), width)
        gh[...] += nt_dot(gbuf[n_wide + 1 + n, 0:rows, :], wqkv[:, cols])
        return carry

    lax.fori_loop(0, 3, back_proj, 0)
    comm(7)

    for i in range(4):
        r = slice(i * patches, (i + 1) * patches)
        n, s = normalized(tok[r, :].astype(F32))
        gy = gh[r, :]
        gacc[0:1, :] += jnp.sum(gy * n, axis=0, keepdims=True)
        gyg = gy * gain_one
        grad = s * (gyg - jnp.mean(gyg, axis=-1, keepdims=True) - n * jnp.mean(gyg * n, axis=-1, keepdims=True))
        tok[r, :] = (resid[r, :] + grad).astype(BF16)
    tg_copy = rc(tok.at[own_rows(1 - x)], token_out.at[x], S_TG, x_dev)
    tg_copy.start()
    tg_here = pltpu.make_async_copy(tok.at[own_rows(x)], token_out.at[x], load_sem.at[9])
    tg_here.start()

    comm(8)
    for cp in ht_copies[8:12]:
        cp.wait_recv()
    for n in range(3):
        wgrad(n_wide + 1 + n, 2)
        comm(9 + n)

    gx_send[...] = jnp.zeros_like(gx_send)
    for n in range(2):
        for q in range(pieces):
            row = n * pieces + q
            gx_send[0, row : row + 1, :] = gacc[n : n + 1, q * lanes : (q + 1) * lanes]
    recv_g[x, yz] = gx_send[0]
    g_copies = []
    for k, yy, xx, zz in others():
        g_copies.append(rc(recv_g.at[x, yz], recv_g.at[x, yz], S_G + k, at(yy, xx, c, zz)))
        g_copies[-1].start()
    comm(12)

    for cp in b_copies:
        cp.wait_recv()
    bx_copy = rc(recv_b.at[:, :, 1 - c], recv_b2, S_BX, core_dev)
    bx_copy.start()
    sb_row = lax.broadcasted_iota(jnp.int32, (96, 128), 0)
    sb_col = lax.broadcasted_iota(jnp.int32, (96, 128), 1)
    pick_b = ((sb_row >> 2) & 7) * 16 + (sb_row >> 5) * 4 + (sb_row & 3)
    select_b = (sb_col == pick_b).astype(F32).astype(BF16)
    comm(13)
    bx_copy.wait_recv()
    for m in range(2):
        for src, cc in ((recv_b[m, :, c], c), (recv_b2[m], 1 - c)):
            got = nn_dot(select_b, src.reshape(128, lanes)).astype(BF16)
            to = pl.ds(pl.multiple_of(cc * 32, 32), 32)
            for q in range(3):
                as_mat[to, q * lanes : (q + 1) * lanes] = got[q * 32 : (q + 1) * 32]
        down_out[m] = tn_dot(as_mat[...], downs[m]).astype(BF16)
    comm(14)

    def drain(t, carry):
        comm(t)
        return carry

    lax.fori_loop(15, n_chunks + 3, drain, 0)
    for cp in g_copies:
        cp.wait_recv()
    for m in range(2):
        total = recv_g[m, 0]
        for n in range(1, 8):
            total = total + recv_g[m, n]
        gx_send[m] = total
    gx_copy = rc(gx_send, gx_recv, S_GX, core_dev)
    gx_copy.start()
    lax.fori_loop(n_chunks + 3, n_chunks + 6, drain, 0)
    gx_copy.wait_recv()
    total = gx_send[...] + gx_recv[...]
    for m in range(2):
        flat = jnp.concatenate(
            [jnp.concatenate([total[m, n * pieces + q : n * pieces + q + 1] for q in range(pieces)], axis=1) for n in range(2)],
            axis=0,
        )
        share = width // DP
        own = flat[:, 0:share]
        for d in range(1, DP):
            own = jnp.where(dp == d, flat[:, d * share : (d + 1) * share], own)
        gain_out[m, 0:2, 0:share] = own

    def finish(k, carry):
        y_copy(k).wait_send()
        here_copy(k).wait()
        x_copy(k).wait()

        @pl.when(outer)
        def _():
            oi_copy(k).wait_send()

        @pl.when(inner)
        def _():
            ii_copy(k).wait_send()
            io_copy(k).wait_send()

        return carry

    lax.fori_loop(0, n_chunks, finish, 0)
    for cp in a_copies + b_copies + ht_copies + g_copies + [tok_send, pos_send, ax_copy, bx_copy, gx_copy]:
        cp.wait_send()
    for j in range(n_blocks):
        gb_copy(j).wait_send()
    tg_copy.wait()
    tg_here.wait()


def layer_call(tokens, positions, missing, wqkv, wout, wup, wdown, gains):
    own, patches = positions.shape
    width = tokens.shape[2]
    hidden = wup.shape[2]
    rows = 2 * own * patches
    items = missing.shape[0]
    n_blocks = hidden // width + 4
    n_chunks = n_blocks * (width // CHUNK)
    piece = (n_chunks, width // 4, CHUNK)
    vm = pltpu.VMEM
    any_spec = pl.BlockSpec(memory_space=pl.ANY)
    n_sems = S_Y + 5 * n_chunks
    scratch = [
        vm((own, patches), jnp.int32), vm((1, items), jnp.int32), vm((2, width), F32),
        vm((width, 3 * width), BF16), vm((width, width), BF16), vm((width, hidden), BF16), vm((hidden, width), BF16),
        vm((rows, width), BF16),
        vm((2, 8, 128), F32),
        vm((rows, width), BF16),
        vm((rows, 3 * width), BF16),
        vm((4 * (HEADS // 2), 2 * patches, patches), F32),
        vm((rows, width), BF16),
        vm((rows, width), F32),
        vm((rows, width), BF16),
        vm((rows, hidden), BF16),
        vm((8, hidden), F32),
        vm((8, width), F32),
        vm((16, width), F32),
        vm((32, 128), F32),
        vm((2, 2, 8, 32, 128), BF16),
        vm((8, 16, 128), F32),
        vm((4, 2, 16, 128), BF16),
        vm((2, 8, 2, 16, 128), BF16),
        vm((2, 8, 16, 128), BF16),
        vm((2, items, width), BF16),
        vm((2, items, width), BF16),
        vm((2, items, width), BF16),
        vm((16, width), F32),
        vm((8, width), F32),
        vm((3, width, rows), BF16),
        vm((3, width // 2, 2 * rows), BF16),
        vm((n_blocks, 2 * rows, width), BF16),
        vm((rows, width), BF16),
        vm((rows, width), F32),
        vm((8, width), F32),
        vm((2, 8, 16, 128), F32),
        vm((2, 16, 128), F32),
        vm((2, 16, 128), F32),
        vm((items, hidden // DP), BF16),
        vm(piece, BF16), vm(piece, BF16), vm(piece, BF16), vm(piece, BF16), vm(piece, BF16),
        pltpu.SemaphoreType.DMA((12,)),
        pltpu.SemaphoreType.DMA((n_chunks,)),
        pltpu.SemaphoreType.DMA((n_sems,)),
        pltpu.SemaphoreType.DMA((n_sems,)),
    ]
    return pl.pallas_call(
        layer_kernel,
        out_shape=(
            vm((2, width // DP, n_chunks * CHUNK), BF16), vm((2, hidden // DP, width), BF16),
            vm((2, own * patches, width), BF16), vm((2, 8, 128), F32), vm((8, 128), F32),
        ),
        in_specs=[any_spec] * 8,
        out_specs=(pl.BlockSpec(memory_space=pltpu.VMEM),) * 5,
        scratch_shapes=scratch,
        compiler_params=pltpu.CompilerParams(
            collective_id=0, has_side_effects=True, vmem_limit_bytes=58 * 2**20
        ),
    )(tokens, positions, missing.reshape(1, items), wqkv, wout, wup, wdown, gains)


def widen_kernel(
    grads, down, tok, gain, loss, qkv_o, out_o, up_o, down_o, tok_o, gain_o, loss_o, qkv_v, out_v, up_v, down_v, tok_v, sem
):
    hidden, width = up_v.shape[2], out_v.shape[2]
    outs = []

    def send(value, wide, dst):
        wide[...] = value.astype(F32)
        outs.append(pltpu.make_async_copy(wide, dst, sem.at[len(outs)]))
        outs[-1].start()

    for m in range(2):
        send(tok[m], tok_v.at[m], tok_o.at[m])
        send(down[m], down_v.at[m], down_o.at[m])
        for lo, size, wide, dst in (
            (0, hidden, up_v, up_o), (hidden, width, out_v, out_o), (hidden + width, 3 * width, qkv_v, qkv_o)
        ):
            send(grads[m, :, lo : lo + size], wide.at[m], dst.at[m])
    loss_o[...] = loss[0:1, 0:1]
    gain_o[...] = gain[:, 0:2, 0 : gain_o.shape[2]]
    for cp in outs:
        cp.wait()


def widen_call(grads, down, tok, gain, loss, width, hidden):
    vm = pltpu.VMEM
    vmem_spec = pl.BlockSpec(memory_space=pltpu.VMEM)
    rows = width // DP
    shapes = ((2, rows, 3 * width), (2, rows, width), (2, rows, hidden), down.shape, tok.shape)
    ins = [pltpu.with_memory_space_constraint(v, pltpu.VMEM) for v in (grads, down, tok, gain, loss)]
    return pl.pallas_call(
        widen_kernel,
        out_shape=tuple(jax.ShapeDtypeStruct(shape, F32) for shape in shapes + ((2, 2, rows), (1, 1))),
        in_specs=[vmem_spec] * 5,
        out_specs=(pl.BlockSpec(memory_space=pl.ANY),) * 5 + (vmem_spec,) * 2,
        scratch_shapes=[vm(shape, F32) for shape in shapes] + [pltpu.SemaphoreType.DMA((10,))],
        compiler_params=pltpu.CompilerParams(vmem_limit_bytes=40 * 2**20),
    )(*ins)


def fused(tokens, positions, missing, qkv_weight, out_weight, up_weight, down_weight, norm_gains):
    grads, down, tok, gain, loss = layer_call(
        tokens, positions, missing, qkv_weight, out_weight, up_weight, down_weight, norm_gains
    )
    qkv, out, up, down, tok, gain, loss = widen_call(
        grads, down, tok, gain, loss, tokens.shape[2], up_weight.shape[2]
    )
    return (loss.reshape(()), tok, qkv, out, up, down, gain)


def lead_dot(left, right):
    return lax.dot_general(
        left, right, (((0,), (0,)), ((), ())), preferred_element_type=jnp.float32
    )


def tail_dot(left, right):
    return lax.dot_general(
        left, right, (((1,), (1,)), ((), ())), preferred_element_type=jnp.float32
    )


def norm_gain(values, gain):
    centre = values - jnp.mean(values, axis=-1, keepdims=True)
    spread = jnp.mean(centre * centre, axis=-1, keepdims=True)
    return centre * lax.rsqrt(spread + eps_norm) * gain


def unit_rows(pooled):
    return pooled * lax.rsqrt(jnp.sum(pooled * pooled, axis=1, keepdims=True) + eps_norm)


def gelu_exact(values):
    return jax.nn.gelu(values, approximate=False)


def alibi_bias(positions):
    grid_rows = (positions // GRID_W).astype(jnp.float32)
    grid_cols = (positions % GRID_W).astype(jnp.float32)
    row_gap = grid_rows[:, :, None] - grid_rows[:, None, :]
    col_gap = grid_cols[:, :, None] - grid_cols[:, None, :]
    distance = jnp.sqrt(row_gap * row_gap + col_gap * col_gap)
    slopes = jnp.exp2(-8.0 * (jnp.arange(HEADS) + 1).astype(jnp.float32) / HEADS)
    return -slopes[None, :, None, None] * distance[:, None, :, :]


def log_total(logits, valid_cols, valid_rows):
    row_max = jnp.max(logits, axis=1, keepdims=True)
    summed = jnp.sum(valid_cols[None, :] * jnp.exp(logits - row_max), axis=1) + (1.0 - valid_rows)
    return row_max[:, 0] + jnp.log(summed)


def row_grads(logits, log_sums, valid_rows, valid_cols, match, total_items):
    soft = valid_cols[None, :] * jnp.exp(logits - log_sums[:, None])
    return (valid_rows[:, None] / (2.0 * total_items) * (soft - match)).astype(jnp.bfloat16)


def block_forward(token_rows, alibi_terms, qkv_weight, out_weight, up_weight, down_weight, gains):
    row_count, model_width = token_rows.shape
    images, patches = (alibi_terms.shape[0], alibi_terms.shape[2])
    head_dim = model_width // HEADS
    score_scale = head_dim ** (-0.5)
    start_rows = token_rows.astype(jnp.float32)
    normed_one = norm_gain(start_rows, gains[0]).astype(jnp.bfloat16)
    projected = jnp.dot(normed_one, qkv_weight, preferred_element_type=jnp.float32).astype(
        jnp.bfloat16
    )
    queries = projected[:, :model_width].reshape(images, patches, HEADS, head_dim)
    key_rows = projected[:, model_width : 2 * model_width].reshape(images, patches, HEADS, head_dim)
    value_rows = projected[:, 2 * model_width :].reshape(images, patches, HEADS, head_dim)
    scores = jnp.einsum("iqhd,ikhd->ihqk", queries, key_rows, preferred_element_type=jnp.float32)
    attn_probs = jax.nn.softmax(scores * score_scale + alibi_terms, axis=-1)
    probs_low = attn_probs.astype(jnp.bfloat16)
    attended = jnp.einsum(
        "ihqk,ikhd->iqhd", probs_low, value_rows, preferred_element_type=jnp.float32
    )
    attended = attended.reshape(row_count, model_width).astype(jnp.bfloat16)
    residual = start_rows + jnp.dot(attended, out_weight, preferred_element_type=jnp.float32)
    normed_two = norm_gain(residual, gains[1]).astype(jnp.bfloat16)
    hidden_pre = jnp.dot(normed_two, up_weight, preferred_element_type=jnp.float32)
    active = gelu_exact(hidden_pre).astype(jnp.bfloat16)
    out_rows = residual + jnp.dot(active, down_weight, preferred_element_type=jnp.float32)
    saved = (
        start_rows,
        normed_one,
        projected,
        attn_probs,
        probs_low,
        attended,
        residual,
        normed_two,
        hidden_pre,
        active,
    )
    return (out_rows, saved)


def block_backward(grad_rows, saved, qkv_weight, out_weight, up_weight, down_weight, gains):
    (
        start_rows,
        normed_one,
        projected,
        attn_probs,
        probs_low,
        attended,
        residual,
        normed_two,
        hidden_pre,
        active,
    ) = saved
    images, head_count, patches = (attn_probs.shape[0], attn_probs.shape[1], attn_probs.shape[2])
    row_count, model_width = grad_rows.shape
    head_dim = model_width // head_count
    score_scale = head_dim ** (-0.5)
    down_in = grad_rows.astype(jnp.bfloat16)
    grad_down = lead_dot(active, down_in)
    grad_active = tail_dot(down_in, down_weight)
    _, gelu_back = jax.vjp(gelu_exact, hidden_pre)
    grad_hidden = gelu_back(grad_active)[0].astype(jnp.bfloat16)
    grad_up = lead_dot(normed_two, grad_hidden)
    grad_h_two = tail_dot(grad_hidden, up_weight)
    _, norm_two_back = jax.vjp(norm_gain, residual, gains[1])
    grad_mid, gain_two = norm_two_back(grad_h_two)
    grad_residual = grad_rows + grad_mid
    attn_in = grad_residual.astype(jnp.bfloat16)
    grad_out = lead_dot(attended, attn_in)
    grad_att = (
        tail_dot(attn_in, out_weight)
        .astype(jnp.bfloat16)
        .reshape(images, patches, head_count, head_dim)
    )
    queries = projected[:, :model_width].reshape(images, patches, head_count, head_dim)
    key_rows = projected[:, model_width : 2 * model_width].reshape(
        images, patches, head_count, head_dim
    )
    value_rows = projected[:, 2 * model_width :].reshape(images, patches, head_count, head_dim)
    grad_values = jnp.einsum(
        "ihqk,iqhd->ikhd", probs_low, grad_att, preferred_element_type=jnp.float32
    )
    grad_probs = jnp.einsum(
        "iqhd,ikhd->ihqk", grad_att, value_rows, preferred_element_type=jnp.float32
    )
    grad_scores = attn_probs * (
        grad_probs - jnp.sum(grad_probs * attn_probs, axis=-1, keepdims=True)
    )
    grad_scores = grad_scores.astype(jnp.bfloat16)
    grad_queries = (
        jnp.einsum("ihqk,ikhd->iqhd", grad_scores, key_rows, preferred_element_type=jnp.float32)
        * score_scale
    )
    grad_keys = (
        jnp.einsum("ihqk,iqhd->ikhd", grad_scores, queries, preferred_element_type=jnp.float32)
        * score_scale
    )
    grad_proj = jnp.concatenate(
        [
            grad_queries.reshape(row_count, model_width),
            grad_keys.reshape(row_count, model_width),
            grad_values.reshape(row_count, model_width),
        ],
        axis=1,
    ).astype(jnp.bfloat16)
    grad_qkv = lead_dot(normed_one, grad_proj)
    grad_h_one = tail_dot(grad_proj, qkv_weight)
    _, norm_one_back = jax.vjp(norm_gain, start_rows, gains[0])
    grad_first, gain_one = norm_one_back(grad_h_one)
    weight_grads = (grad_qkv, grad_out, grad_up, grad_down, jnp.stack([gain_one, gain_two]))
    return (grad_residual + grad_first, weight_grads)


def local(tokens, positions, missing, qkv_weight, out_weight, up_weight, down_weight, norm_gains):
    own_images = positions.shape[0]
    model_width = tokens.shape[2]
    patches = tokens.shape[1] // own_images
    first_row = lax.axis_index(("dp", "rep")) * own_images
    alibi_terms = alibi_bias(positions)
    saved_list = []
    pooled_list = []
    normed = []
    for modality in range(2):
        out_rows, saved = block_forward(
            tokens[modality],
            alibi_terms,
            qkv_weight[modality],
            out_weight[modality],
            up_weight[modality],
            down_weight[modality],
            norm_gains[modality],
        )
        pooled = jnp.sum(out_rows.reshape(own_images, patches, model_width), axis=1)
        saved_list.append(saved)
        pooled_list.append(pooled)
        normed.append(unit_rows(pooled).astype(jnp.bfloat16))
    valid_all = 1.0 - missing.astype(jnp.float32)
    total_items = float(missing.shape[0])
    valid_own = lax.dynamic_slice_in_dim(valid_all, first_row, own_images)
    radar_all, optic_all = (
        lax.all_gather(normed[0], ("dp", "rep"), axis=0, tiled=True),
        lax.all_gather(normed[1], ("dp", "rep"), axis=0, tiled=True),
    )
    images_all = radar_all.shape[0]
    match_own = (
        lax.broadcasted_iota(jnp.int32, (own_images, images_all), 0) + first_row
        == lax.broadcasted_iota(jnp.int32, (own_images, images_all), 1)
    ).astype(jnp.float32)
    logits_r = tail_dot(normed[0], optic_all) * inv_temp
    logits_o = tail_dot(normed[1], radar_all) * inv_temp
    lse_r = log_total(logits_r, valid_all, valid_own)
    lse_o = log_total(logits_o, valid_all, valid_own)
    item_terms = valid_own * (
        lse_r
        - jnp.sum(logits_r * match_own, axis=1)
        + lse_o
        - jnp.sum(logits_o * match_own, axis=1)
    )
    grad_lr = row_grads(logits_r, lse_r, valid_own, valid_all, match_own, total_items)
    grad_lo = row_grads(logits_o, lse_o, valid_own, valid_all, match_own, total_items)
    grad_ur = jnp.dot(grad_lr, optic_all, preferred_element_type=jnp.float32) * inv_temp
    grad_uo = jnp.dot(grad_lo, radar_all, preferred_element_type=jnp.float32) * inv_temp
    summed_terms = lax.psum(jnp.sum(item_terms), ("dp", "rep"))
    loss_value = summed_terms / (2.0 * total_items)
    share_o = lead_dot(grad_lr, normed[0]) * inv_temp
    share_r = lead_dot(grad_lo, normed[1]) * inv_temp
    back_r, back_o = (
        lax.psum_scatter(share_r, ("dp", "rep"), scatter_dimension=0, tiled=True),
        lax.psum_scatter(share_o, ("dp", "rep"), scatter_dimension=0, tiled=True),
    )
    grad_ur = grad_ur + back_r
    grad_uo = grad_uo + back_o
    grad_units = (grad_ur, grad_uo)
    token_list = []
    block_grads = []
    for modality in range(2):
        _, unit_back = jax.vjp(unit_rows, pooled_list[modality])
        grad_pooled = unit_back(grad_units[modality])[0]
        grad_rows = jnp.broadcast_to(grad_pooled[:, None, :], (own_images, patches, model_width))
        grad_rows = grad_rows.reshape(own_images * patches, model_width)
        grad_tokens, weight_grads = block_backward(
            grad_rows,
            saved_list[modality],
            qkv_weight[modality],
            out_weight[modality],
            up_weight[modality],
            down_weight[modality],
            norm_gains[modality],
        )
        token_list.append(grad_tokens)
        block_grads.append(list(weight_grads))
    stacked = [jnp.stack([block_grads[0][slot], block_grads[1][slot]]) for slot in range(5)]
    shares = (
        lax.psum_scatter(stacked[0], "dp", scatter_dimension=1, tiled=True),
        lax.psum_scatter(stacked[1], "dp", scatter_dimension=1, tiled=True),
        lax.psum_scatter(stacked[2], "dp", scatter_dimension=1, tiled=True),
        lax.psum_scatter(stacked[3], "dp", scatter_dimension=1, tiled=True),
        lax.psum_scatter(stacked[4], "dp", scatter_dimension=2, tiled=True),
    )
    summed = (
        lax.psum(shares[0].astype(jnp.bfloat16), "rep").astype(jnp.float32),
        lax.psum(shares[1].astype(jnp.bfloat16), "rep").astype(jnp.float32),
        lax.psum(shares[2].astype(jnp.bfloat16), "rep").astype(jnp.float32),
        lax.psum(shares[3].astype(jnp.bfloat16), "rep").astype(jnp.float32),
        lax.psum(shares[4].astype(jnp.bfloat16), "rep").astype(jnp.float32),
    )
    stacked = list(summed)
    token_grads = jnp.stack(token_list)
    return (loss_value, token_grads, stacked[0], stacked[1], stacked[2], stacked[3], stacked[4])


def solution(mesh):
    in_specs = (P(None, ("dp", "rep"), None), P(("dp", "rep"), None), P(), P(), P(), P(), P(), P())
    out_specs = (
        P(),
        P(None, ("dp", "rep"), None),
        P(None, "dp", None),
        P(None, "dp", None),
        P(None, "dp", None),
        P(None, "dp", None),
        P(None, None, "dp"),
    )
    one_kernel = mesh.shape["dp"] == DP and mesh.shape["rep"] == REP
    step = fused if one_kernel else local
    return jax.shard_map(step, mesh=mesh, in_specs=in_specs, out_specs=out_specs, check_vma=False)
```

```python
import functools

import jax
import jax.numpy as jnp
from jax import lax
from jax.experimental import pallas as pl
from jax.experimental.pallas import tpu as pltpu
from jax.sharding import PartitionSpec as P

HEADS = 12
GRID_W = 12
MESH = pl.DeviceIdType.MESH
F32 = jnp.float32
BF16 = jnp.bfloat16

eps_norm = 1e-06
inv_temp = 32.0
SQRT_HALF = 0.7071067811865476
INV_SQRT_TWO_PI = 0.3989422804014327
HALF_LOG2_E = -0.7213475204444817

DP = 8
REP = 4
CHUNK = 256


def nt_dot(left, right):
    return lax.dot_general(left, right, (((1,), (1,)), ((), ())), preferred_element_type=F32)


def tn_dot(left, right):
    return lax.dot_general(left, right, (((0,), (0,)), ((), ())), preferred_element_type=F32)


def nn_dot(left, right):
    return jnp.dot(left, right, preferred_element_type=F32)


def normalized(values):
    centre = values - jnp.mean(values, axis=-1, keepdims=True)
    scale = lax.rsqrt(jnp.mean(centre * centre, axis=-1, keepdims=True) + eps_norm)
    return centre * scale, scale


def gelu_and_slope(values):
    cdf = 0.5 + 0.5 * lax.erf(values * SQRT_HALF)
    return values * cdf, cdf + values * (jnp.exp2(values * values * HALF_LOG2_E) * INV_SQRT_TWO_PI)


S_TOK, S_POS, S_A, S_AX, S_B, S_BX, S_G, S_GX = 0, 1, 2, 18, 19, 35, 36, 52
S_HT, S_GB, S_TG = 53, 65, 73
S_Y = 74


def layer_kernel(
    tokens, positions_h, missing_h, wqkv_h, wout_h, wup_h, wdown_h, gains_h,
    grad_out, down_out, token_out, gain_out, loss_out,
    positions, missing, gains, wqkv, wout, wup, wdown, tok, posb, h_one, proj, probs, att, resid, h_two, slope,
    asum, rsum, pool, msg_a, recv_a, msg_b, send_b, recv_b, recv_b2, units, downs, downs_lo, ga, gp_own,
    h_t, ht, gbuf, gatt, gh, gacc, gsum, as_mat,
    ysend, keep, yrecv, ring_a, ring_b,
    load_sem, out_sem, ss, rs,
):
    width = h_one.shape[1]
    hidden = wup.shape[1]
    rows = h_one.shape[0]
    half = rows // 2
    patches = half // 2
    pairs = HEADS // 2
    lanes = 128
    pieces = width // lanes
    items = missing.shape[1]
    n_wide = hidden // width
    n_blocks = n_wide + 4
    per_block = width // CHUNK
    n_chunks = n_blocks * per_block
    score_scale = (width // HEADS) ** -0.5

    S_OI, S_II, S_IO, S_X = (S_Y + n_chunks * n for n in range(1, 5))

    dp = lax.axis_index("dp")
    z = lax.axis_index("rep")
    c = dp % 2
    x = (dp // 2) % 2
    y = dp // 4
    yz = y * 4 + z

    def at(yy, xx, cc, zz):
        return (yy * 4 + xx * 2 + cc, zz)

    core_dev = at(y, x, 1 - c, z)
    x_dev = at(y, 1 - x, c, z)
    y_dev = at(1 - y, x, c, z)
    inner = jnp.logical_and(z >= 1, z <= 2)
    outer = jnp.logical_not(inner)
    high = z // 2
    inner_peer = at(y, x, c, 3 - z)
    outer_peer = at(y, x, c, 3 * high)
    inward_peer = at(y, x, c, 1 + high)

    def others():
        for k in range(1, 16):
            yield k, y ^ (k & 1), x ^ ((k >> 1) & 1), (z + (k >> 2)) % 4

    def rc(src, dst, idx, dev):
        return pltpu.make_async_remote_copy(
            src_ref=src, dst_ref=dst, send_sem=ss.at[idx], recv_sem=rs.at[idx],
            device_id=dev, device_id_type=MESH,
        )

    def own_rows(xx):
        return pl.ds(pl.multiple_of(xx * half, half), half)

    barrier = pltpu.get_barrier_semaphore()
    for k, yy, xx, zz in others():
        pl.semaphore_signal(barrier, inc=1, device_id=at(yy, xx, c, zz), device_id_type=MESH)
    pl.semaphore_signal(barrier, inc=1, device_id=core_dev, device_id_type=MESH)
    early = [
        (positions_h, positions), (tokens.at[x], tok.at[own_rows(x)]), (gains_h.at[x], gains), (wqkv_h.at[x], wqkv),
        (missing_h, missing),
    ]
    late = [(wout_h.at[x], wout), (wup_h.at[x], wup), (wdown_h.at[x], wdown)]
    loads = [pltpu.make_async_copy(src, dst, load_sem.at[n]) for n, (src, dst) in enumerate(early + late)]
    for load in loads[: len(early)]:
        load.start()
    load_pos, load_tok, load_gains, load_qkv, load_missing, load_out, load_up, load_down = loads
    posb[x] = jnp.zeros((8, lanes), F32)
    asum[...] = jnp.zeros_like(asum)
    rsum[...] = jnp.zeros_like(rsum)
    pool[...] = jnp.zeros_like(pool)
    gacc[...] = jnp.zeros_like(gacc)

    load_pos.wait()
    cells = positions[...].astype(F32)
    cell_rows = jnp.floor((cells + 0.5) * (1.0 / GRID_W))
    cell_cols = cells - GRID_W * cell_rows
    posb[x, 0:2, 0:patches] = cell_rows
    posb[x, 2:4, 0:patches] = cell_cols

    pl.semaphore_wait(barrier, 16)
    tok_send = rc(tokens.at[1 - x], tok.at[own_rows(x)], S_TOK, x_dev)
    pos_send = rc(posb.at[x], posb.at[x], S_POS, x_dev)
    tok_send.start()
    pos_send.start()

    low_lanes = lax.broadcasted_iota(jnp.int32, (patches, lanes), 1) < lanes // 2
    mask_low = low_lanes.astype(F32).astype(BF16)
    mask_high = (1.0 - low_lanes.astype(F32)).astype(BF16)

    def two_heads(values):
        return jnp.concatenate([values * mask_low, values * mask_high], axis=0)

    def fold_heads(values):
        return jnp.where(low_lanes, values[:patches], values[patches:])

    def img_rows(i):
        return pl.ds(pl.multiple_of(i * patches, patches), patches)

    load_tok.wait()
    load_gains.wait()
    gain_one = gains[0:1, :]
    gain_two = gains[1:2, :]

    def attention(xx):
        def image(j, carry):
            r = img_rows(xx * 2 + j)
            cr = jnp.broadcast_to(posb[xx, pl.ds(j, 1), :], (lanes, lanes))
            cc = jnp.broadcast_to(posb[xx, pl.ds(j + 2, 1), :], (lanes, lanes))
            row_gap = cr.T - cr
            col_gap = cc.T - cc
            dist = jnp.sqrt(row_gap * row_gap + col_gap * col_gap)[:patches, :patches]
            raw = []
            for p in range(pairs):
                q = two_heads(proj[r, p * lanes : (p + 1) * lanes])
                raw.append(nt_dot(q, proj[r, width + p * lanes : width + (p + 1) * lanes]))
            soft = []
            for p in range(pairs):
                slopes = [2.0 ** (-8.0 * (2 * p + h + 1) / HEADS) for h in range(2)]
                alibi = jnp.concatenate([dist * -slopes[0], dist * -slopes[1]], axis=0)
                s = raw[p] * score_scale + alibi
                e = jnp.exp(s - jnp.max(s, axis=-1, keepdims=True))
                prob = e * (1.0 / jnp.sum(e, axis=-1, keepdims=True))
                probs[(xx * 2 + j) * pairs + p] = prob
                soft.append(prob.astype(BF16))
            for p in range(pairs):
                v = proj[r, 2 * width + p * lanes : 2 * width + (p + 1) * lanes]
                att[r, p * lanes : (p + 1) * lanes] = fold_heads(nn_dot(soft[p], v)).astype(BF16)
            return carry

        lax.fori_loop(0, 2, image, 0)

    def wide(j):
        return pl.ds(pl.multiple_of(j * width, width), width)

    def add_pool(j, on):
        a = asum[:, wide(j)] * on
        a_high = a.astype(BF16).astype(F32)
        both = jnp.concatenate([a_high, a - a_high], axis=0).astype(BF16)
        pool[...] += nn_dot(both, wdown[wide(j), :])

    for step in range(2):
        xx = x if step == 0 else 1 - x
        where = own_rows(xx)
        if step == 1:
            tok_send.wait_recv()
            pos_send.wait_recv()
        for j in range(2):
            r = img_rows(xx * 2 + j)
            n, _ = normalized(tok[r, :].astype(F32))
            h_one[r, :] = (n * gain_one).astype(BF16)
        if step == 0:
            load_qkv.wait()
            load_out.start()
            load_up.start()
            load_down.start()
        for n in range(3):
            cols = slice(n * width, (n + 1) * width)
            proj[where, cols] = nn_dot(h_one[where, :], wqkv[:, cols]).astype(BF16)
        attention(xx)
        if step == 0:
            load_out.wait()
        resid[where, :] = tok[where, :].astype(F32) + nn_dot(att[where, :], wout[...])
        for j in range(2):
            i = xx * 2 + j
            r = img_rows(i)
            v = resid[r, :]
            rsum[pl.ds(i, 1), :] = jnp.sum(v, axis=0, keepdims=True)
            n, _ = normalized(v)
            h_two[r, :] = (n * gain_two).astype(BF16)
        if step == 0:
            load_up.wait()
        else:
            load_down.wait()

        def feed(j, carry, where=where, xx=xx, step=step):
            for n in range(width // 256):
                cols = pl.ds(pl.multiple_of(j * width + n * 256, 256), 256)
                pre = nn_dot(h_two[where, :], wup[:, cols])
                act, slp = gelu_and_slope(pre)
                slope[where, cols] = slp.astype(BF16)
                act = act.astype(BF16).astype(F32)
                for i in range(2):
                    asum[pl.ds(xx * 2 + i, 1), cols] = jnp.sum(act[i * patches : (i + 1) * patches], axis=0, keepdims=True)
            if step == 1:
                add_pool(jnp.maximum(j - 1, 0), (j > 0).astype(F32))
            return carry

        lax.fori_loop(0, n_wide, feed, 0)
    add_pool(n_wide - 1, 1.0)

    pooled = rsum[...] + pool[0:8, :] + pool[8:16, :]
    s_own = lax.rsqrt(jnp.sum(pooled * pooled, axis=1, keepdims=True) + eps_norm)
    unit = pooled * s_own
    for q in range(pieces):
        msg_a[4 * q : 4 * q + 4, :] = unit[0:4, q * lanes : (q + 1) * lanes]
    s_high = s_own.astype(BF16).astype(F32)
    msg_a[24:28, :] = jnp.broadcast_to(s_high[0:4], (4, lanes))
    msg_a[28:32, :] = jnp.broadcast_to((s_own - s_high)[0:4], (4, lanes))
    recv_a[c, x, yz] = msg_a[...].astype(BF16)
    a_copies = []
    for k, yy, xx, zz in others():
        a_copies.append(rc(recv_a.at[c, x, yz], recv_a.at[c, x, yz], S_A + k, at(yy, xx, c, zz)))
        a_copies[-1].start()

    msg_b[...] = jnp.zeros_like(msg_b)
    for block in range(DP):
        for q in range(3):
            lo = block * 3 * lanes + q * lanes
            msg_b[block, 4 * q : 4 * q + 4, :] = asum[0:4, lo : lo + lanes]
    for block in range(DP):
        send_b[block // 2, block % 2] = msg_b[block].astype(BF16)
    recv_b[x, yz] = send_b[y * 2 + x]
    ht_copies = []
    for w, src in enumerate((h_two, att, h_one)):
        h_t[w] = src[...].T
        for rel in range(2):
            yy = y if rel == 1 else 1 - y
            for xx in range(2):
                base = yy * (width // 2) + xx * (width // 4)
                mine = pl.ds(pl.multiple_of(base + c * (width // 8), width // 8), width // 8)
                theirs = pl.ds(pl.multiple_of(base + (1 - c) * (width // 8), width // 8), width // 8)
                lo = (rel * 2 + xx) * (width // 8)
                ht[w, lo : lo + width // 8, 0:rows] = h_t[w, mine, :]
                ht_copies.append(
                    rc(
                        h_t.at[w, theirs, :],
                        ht.at[w, pl.ds(lo, width // 8), pl.ds(rows, rows)],
                        S_HT + w * 4 + rel * 2 + xx,
                        core_dev,
                    )
                )
                ht_copies[-1].start()

    n_sel = 8 * 32
    sel_row = lax.broadcasted_iota(jnp.int32, (n_sel, n_sel), 0)
    sel_col = lax.broadcasted_iota(jnp.int32, (n_sel, n_sel), 1)
    pick = ((sel_row >> 2) & 7) * 32 + (sel_row >> 5) * 4 + (sel_row & 3)
    select_a = (sel_col == pick).astype(F32).astype(BF16)

    p_i = lax.broadcasted_iota(jnp.int32, (items, items), 0)
    q_i = lax.broadcasted_iota(jnp.int32, (items, items), 1)
    place = ((((p_i >> 4) & 1) * 4 + ((p_i >> 1) & 1) * 2 + (p_i >> 5)) * 4 + ((p_i >> 2) & 3)) * 2 + (p_i & 1)
    eye = (p_i == q_i).astype(F32)
    load_missing.wait()
    v_nat = 1.0 - missing[...].astype(F32)
    v_col = jnp.sum((q_i == place).astype(F32) * v_nat, axis=1, keepdims=True)
    v_row = jnp.sum(eye * v_col, axis=0, keepdims=True)

    for cp in a_copies:
        cp.wait_recv()
    ax_copy = rc(recv_a.at[c], recv_a.at[c], S_AX, core_dev)
    ax_copy.start()
    b_copies = []
    for k, yy, xx, zz in others():
        b_copies.append(rc(send_b.at[yy * 2 + xx], recv_b.at[x, yz], S_B + k, at(yy, xx, c, zz)))
        b_copies[-1].start()
    ax_copy.wait_recv()

    scales = [[None, None], [None, None]]
    for core in range(2):
        for m in range(2):
            got = nn_dot(select_a, recv_a[core, m].reshape(n_sel, lanes))
            for q in range(pieces):
                units[m, core * 32 : core * 32 + 32, q * lanes : (q + 1) * lanes] = got[q * 32 : q * 32 + 32].astype(BF16)
            scales[m][core] = got[6 * 32 : 7 * 32] + got[7 * 32 :]
    scale_cols = [jnp.concatenate(scales[m], axis=0)[:, 0:1] for m in range(2)]

    u_r, u_o = units[0], units[1]
    logits = nt_dot(u_r, u_o) * inv_temp
    top_r = jnp.max(logits, axis=1, keepdims=True)
    lse_r = top_r + jnp.log(jnp.sum(v_row * jnp.exp(logits - top_r), axis=1, keepdims=True) + (1.0 - v_col))
    top_o = jnp.max(logits, axis=0, keepdims=True)
    lse_o = top_o + jnp.log(jnp.sum(v_col * jnp.exp(logits - top_o), axis=0, keepdims=True) + (1.0 - v_row))
    diag = logits * eye
    terms_r = v_col * (lse_r - jnp.sum(diag, axis=1, keepdims=True))
    terms_o = v_row * (lse_o - jnp.sum(diag, axis=0, keepdims=True))
    loss = (jnp.sum(terms_r, axis=0, keepdims=True) + jnp.sum(terms_o, axis=1, keepdims=True)) / (2.0 * items)
    loss_out[...] = jnp.broadcast_to(loss, loss_out.shape)
    grad_r = (v_col / (2.0 * items) * (v_row * jnp.exp(logits - lse_r) - eye)).astype(BF16)
    grad_ot = (v_row / (2.0 * items) * (v_col * jnp.exp(logits - lse_o) - eye)).astype(BF16)
    grad_u = [
        (nn_dot(grad_r, u_o) + nn_dot(grad_ot, u_o)) * inv_temp,
        (tn_dot(grad_r, u_r) + tn_dot(grad_ot, u_r)) * inv_temp,
    ]
    for m in range(2):
        u = units[m].astype(F32)
        g = grad_u[m]
        gp = scale_cols[m] * (g - u * jnp.sum(u * g, axis=1, keepdims=True))
        high_part = gp.astype(BF16)
        downs[m] = high_part
        downs_lo[m] = (gp - high_part.astype(F32)).astype(BF16)
    own_r = lax.broadcasted_iota(jnp.int32, (16, items), 0)
    own_c = lax.broadcasted_iota(jnp.int32, (16, items), 1)
    mine = jnp.logical_and(own_r < 4, own_c == c * 32 + yz * 4 + own_r).astype(F32).astype(BF16)
    down_own = nn_dot(mine, downs[x])
    gp_own[...] = (down_own + nn_dot(mine, downs_lo[x]))[0:8]
    down_own = down_own.astype(BF16)

    def y_copy(k):
        return rc(ysend.at[k], yrecv.at[k], S_Y + k, y_dev)

    def oi_copy(k):
        return rc(keep.at[k], ring_a.at[k], S_OI + k, inward_peer)

    def ii_copy(k):
        return rc(ring_a.at[k], ring_b.at[k], S_II + k, inner_peer)

    def io_copy(k):
        return rc(ring_b.at[k], ring_a.at[k], S_IO + k, outer_peer)

    def out_cols(k):
        return pl.ds(pl.multiple_of(k * CHUNK, CHUNK), CHUNK)

    quarter = width // 8

    def x_copy(k):
        return rc(
            yrecv.at[k, pl.ds(pl.multiple_of((1 - x) * quarter, quarter), quarter), :],
            grad_out.at[x, :, out_cols(k)], S_X + k, x_dev,
        )

    def here_copy(k):
        return pltpu.make_async_copy(
            yrecv.at[k, pl.ds(pl.multiple_of(x * quarter, quarter), quarter), :],
            grad_out.at[x, :, out_cols(k)], out_sem.at[k],
        )

    def step_y(k):
        y_copy(k).wait_recv()
        keep[k] = (keep[k].astype(F32) + yrecv[k].astype(F32)).astype(BF16)

        @pl.when(outer)
        def _():
            oi_copy(k).start()

    def step_a(k):
        @pl.when(inner)
        def _():
            oi_copy(k).wait_recv()
            ring_a[k] = (ring_a[k].astype(F32) + keep[k].astype(F32)).astype(BF16)
            ii_copy(k).start()

    def step_b(k):
        @pl.when(inner)
        def _():
            ii_copy(k).wait_recv()
            got = ring_b[k].astype(F32)
            ring_b[k] = (got + keep[k].astype(F32)).astype(BF16)
            io_copy(k).start()
            yrecv[k] = (got + ring_a[k].astype(F32)).astype(BF16)
            x_copy(k).start()
            here_copy(k).start()

    def step_c(k):
        @pl.when(outer)
        def _():
            io_copy(k).wait_recv()
            yrecv[k] = (keep[k].astype(F32) + ring_a[k].astype(F32)).astype(BF16)
            x_copy(k).start()
            here_copy(k).start()

    def comm(t):
        for lag, step in ((0, step_y), (2, step_a), (4, step_b), (6, step_c)):
            @pl.when(jnp.logical_and(t >= lag, t < n_chunks + lag))
            def _(step=step, lag=lag):
                step(t - lag)

    def gb_copy(j):
        return rc(gbuf.at[j, pl.ds(0, rows), :], gbuf.at[j, pl.ds(rows, rows), :], S_GB + j, core_dev)

    def wgrad(j, w):
        gb_copy(j).wait_recv()
        for n in range(per_block):
            both = nn_dot(ht[w], gbuf[j, :, n * CHUNK : (n + 1) * CHUNK])
            k = j * per_block + n
            ysend[k] = both[:half].astype(BF16)
            y_copy(k).start()
            keep[k] = both[half:].astype(BF16)

    for cp in ht_copies[:4]:
        cp.wait_recv()

    def back_hidden(j, carry):
        cols = pl.ds(pl.multiple_of(j * width, width), width)
        ga[...] = nt_dot(down_own, wdown[cols, :])
        for i in range(4):
            r = slice(i * patches, (i + 1) * patches)
            gbuf[j, r, :] = (ga[i : i + 1, :] * slope[r, cols].astype(F32)).astype(BF16)
        gb_copy(j).start()

        @pl.when(j > 0)
        def _():
            wgrad(j - 1, 0)

        return carry

    lax.fori_loop(0, n_wide, back_hidden, 0)
    wgrad(n_wide - 1, 0)
    comm(0)

    gh[...] = jnp.zeros_like(gh)

    def back_up(j, carry):
        cols = pl.ds(pl.multiple_of(j * width, width), width)
        gh[...] += nt_dot(gbuf[j, 0:rows, :], wup[:, cols])

        @pl.when(j == 2)
        def _():
            comm(1)

        return carry

    lax.fori_loop(0, n_wide, back_up, 0)

    for i in range(4):
        r = slice(i * patches, (i + 1) * patches)
        n, s = normalized(resid[r, :])
        gy = gh[r, :]
        gacc[1:2, :] += jnp.sum(gy * n, axis=0, keepdims=True)
        gyg = gy * gain_two
        grad = s * (gyg - jnp.mean(gyg, axis=-1, keepdims=True) - n * jnp.mean(gyg * n, axis=-1, keepdims=True))
        grad = grad + gp_own[i : i + 1, :]
        resid[r, :] = grad
        gbuf[n_wide, r, :] = grad.astype(BF16)
    gb_copy(n_wide).start()
    gatt[...] = nt_dot(gbuf[n_wide, 0:rows, :], wout[...]).astype(BF16)
    comm(2)
    for cp in ht_copies[4:8]:
        cp.wait_recv()
    wgrad(n_wide, 1)

    def back_attention(i, carry):
        r = img_rows(i)
        das, dps, dss = [], [], []
        for p in range(pairs):
            da = two_heads(gatt[r, p * lanes : (p + 1) * lanes])
            das.append(da)
            dps.append(nt_dot(da, proj[r, 2 * width + p * lanes : 2 * width + (p + 1) * lanes]))
        for p in range(pairs):
            cols = slice(p * lanes, (p + 1) * lanes)
            prob = probs[i * pairs + p]
            dss.append((prob * (dps[p] - jnp.sum(dps[p] * prob, axis=-1, keepdims=True))).astype(BF16))
            gbuf[n_wide + 3, r, cols] = tn_dot(prob.astype(BF16), das[p]).astype(BF16)
        for p in range(pairs):
            cols = slice(p * lanes, (p + 1) * lanes)
            q = two_heads(proj[r, cols])
            k = proj[r, width + p * lanes : width + (p + 1) * lanes]
            gbuf[n_wide + 1, r, cols] = (fold_heads(nn_dot(dss[p], k)) * score_scale).astype(BF16)
            gbuf[n_wide + 2, r, cols] = (tn_dot(dss[p], q) * score_scale).astype(BF16)
        comm(3 + i)
        return carry

    lax.fori_loop(0, 4, back_attention, 0)
    for n in range(3):
        gb_copy(n_wide + 1 + n).start()
    gh[...] = jnp.zeros_like(gh)

    def back_proj(n, carry):
        cols = pl.ds(pl.multiple_of(n * width, width), width)
        gh[...] += nt_dot(gbuf[n_wide + 1 + n, 0:rows, :], wqkv[:, cols])
        return carry

    lax.fori_loop(0, 3, back_proj, 0)
    comm(7)

    for i in range(4):
        r = slice(i * patches, (i + 1) * patches)
        n, s = normalized(tok[r, :].astype(F32))
        gy = gh[r, :]
        gacc[0:1, :] += jnp.sum(gy * n, axis=0, keepdims=True)
        gyg = gy * gain_one
        grad = s * (gyg - jnp.mean(gyg, axis=-1, keepdims=True) - n * jnp.mean(gyg * n, axis=-1, keepdims=True))
        tok[r, :] = (resid[r, :] + grad).astype(BF16)
    tg_copy = rc(tok.at[own_rows(1 - x)], token_out.at[x], S_TG, x_dev)
    tg_copy.start()
    tg_here = pltpu.make_async_copy(tok.at[own_rows(x)], token_out.at[x], load_sem.at[9])
    tg_here.start()

    def gain_copy(src, dst, n, dev):
        return rc(gsum.at[src], gsum.at[dst], S_G + n, dev)

    g_core = gain_copy(0, 1, 0, core_dev)
    g_y = gain_copy(2, 3, 1, y_dev)
    g_oi = gain_copy(4, 5, 2, inward_peer)
    g_ii = gain_copy(6, 7, 3, inner_peer)
    g_io = gain_copy(8, 9, 4, outer_peer)
    g_x = gain_copy(10, 11, 5, x_dev)
    gsum[0] = jnp.zeros_like(gsum[0])
    for n in range(2):
        for q in range(pieces):
            row = n * pieces + q
            gsum[0, row : row + 1, :] = gacc[n : n + 1, q * lanes : (q + 1) * lanes]
    g_core.start()

    def gain_y():
        g_core.wait_recv()
        gsum[2] = gsum[0] + gsum[1]
        g_y.start()

    def gain_oi():
        g_y.wait_recv()
        gsum[4] = gsum[2] + gsum[3]

        @pl.when(outer)
        def _():
            g_oi.start()

    def gain_ii():
        @pl.when(inner)
        def _():
            g_oi.wait_recv()
            gsum[6] = gsum[5] + gsum[4]
            g_ii.start()

    def gain_io():
        @pl.when(inner)
        def _():
            g_ii.wait_recv()
            gsum[8] = gsum[7] + gsum[4]
            g_io.start()
            gsum[10] = gsum[7] + gsum[6]
            g_x.start()

    def gain_x():
        @pl.when(outer)
        def _():
            g_io.wait_recv()
            gsum[10] = gsum[4] + gsum[9]
            g_x.start()

    comm(8)
    for cp in ht_copies[8:12]:
        cp.wait_recv()
    for n in range(3):
        wgrad(n_wide + 1 + n, 2)
        if n == 0:
            gain_y()
        comm(9 + n)

    comm(12)

    for cp in b_copies:
        cp.wait_recv()
    bx_copy = rc(recv_b.at[:, :, 1 - c], recv_b2, S_BX, core_dev)
    bx_copy.start()
    sb_row = lax.broadcasted_iota(jnp.int32, (96, 128), 0)
    sb_col = lax.broadcasted_iota(jnp.int32, (96, 128), 1)
    pick_b = ((sb_row >> 2) & 7) * 16 + (sb_row >> 5) * 4 + (sb_row & 3)
    select_b = (sb_col == pick_b).astype(F32).astype(BF16)
    comm(13)
    bx_copy.wait_recv()
    for m in range(2):
        for src, cc in ((recv_b[m, :, c], c), (recv_b2[m], 1 - c)):
            got = nn_dot(select_b, src.reshape(128, lanes)).astype(BF16)
            to = pl.ds(pl.multiple_of(cc * 32, 32), 32)
            for q in range(3):
                as_mat[to, q * lanes : (q + 1) * lanes] = got[q * 32 : (q + 1) * 32]
        down_out[m] = tn_dot(as_mat[...], downs[m]).astype(BF16)
    comm(14)

    def drain(t, carry):
        comm(t)
        return carry

    lax.fori_loop(15, 20, drain, 0)
    gain_oi()
    lax.fori_loop(20, 22, drain, 0)
    gain_ii()
    lax.fori_loop(22, n_chunks, drain, 0)
    gain_io()
    lax.fori_loop(n_chunks, n_chunks + 2, drain, 0)
    gain_x()
    lax.fori_loop(n_chunks + 2, n_chunks + 6, drain, 0)
    g_x.wait_recv()
    for m, n in ((x, 10), (1 - x, 11)):
        total = gsum[n]
        flat = jnp.concatenate(
            [jnp.concatenate([total[r * pieces + q : r * pieces + q + 1] for q in range(pieces)], axis=1) for r in range(2)],
            axis=0,
        )
        share = width // DP
        own = flat[:, 0:share]
        for d in range(1, DP):
            own = jnp.where(dp == d, flat[:, d * share : (d + 1) * share], own)
        gain_out[m, 0:2, 0:share] = own

    def finish(k, carry):
        y_copy(k).wait_send()
        here_copy(k).wait()
        x_copy(k).wait()

        @pl.when(outer)
        def _():
            oi_copy(k).wait_send()

        @pl.when(inner)
        def _():
            ii_copy(k).wait_send()
            io_copy(k).wait_send()

        return carry

    lax.fori_loop(0, n_chunks, finish, 0)
    for cp in a_copies + b_copies + ht_copies + [tok_send, pos_send, ax_copy, bx_copy, g_core, g_y, g_x]:
        cp.wait_send()

    @pl.when(outer)
    def _():
        g_oi.wait_send()

    @pl.when(inner)
    def _():
        g_ii.wait_send()
        g_io.wait_send()

    for j in range(n_blocks):
        gb_copy(j).wait_send()
    tg_copy.wait()
    tg_here.wait()


def layer_call(tokens, positions, missing, wqkv, wout, wup, wdown, gains):
    own, patches = positions.shape
    width = tokens.shape[2]
    hidden = wup.shape[2]
    rows = 2 * own * patches
    items = missing.shape[0]
    n_blocks = hidden // width + 4
    n_chunks = n_blocks * (width // CHUNK)
    piece = (n_chunks, width // 4, CHUNK)
    vm = pltpu.VMEM
    any_spec = pl.BlockSpec(memory_space=pl.ANY)
    n_sems = S_Y + 5 * n_chunks
    scratch = [
        vm((own, patches), jnp.int32), vm((1, items), jnp.int32), vm((2, width), F32),
        vm((width, 3 * width), BF16), vm((width, width), BF16), vm((width, hidden), BF16), vm((hidden, width), BF16),
        vm((rows, width), BF16),
        vm((2, 8, 128), F32),
        vm((rows, width), BF16),
        vm((rows, 3 * width), BF16),
        vm((4 * (HEADS // 2), 2 * patches, patches), F32),
        vm((rows, width), BF16),
        vm((rows, width), F32),
        vm((rows, width), BF16),
        vm((rows, hidden), BF16),
        vm((8, hidden), F32),
        vm((8, width), F32),
        vm((16, width), F32),
        vm((32, 128), F32),
        vm((2, 2, 8, 32, 128), BF16),
        vm((8, 16, 128), F32),
        vm((4, 2, 16, 128), BF16),
        vm((2, 8, 2, 16, 128), BF16),
        vm((2, 8, 16, 128), BF16),
        vm((2, items, width), BF16),
        vm((2, items, width), BF16),
        vm((2, items, width), BF16),
        vm((16, width), F32),
        vm((8, width), F32),
        vm((3, width, rows), BF16),
        vm((3, width // 2, 2 * rows), BF16),
        vm((n_blocks, 2 * rows, width), BF16),
        vm((rows, width), BF16),
        vm((rows, width), F32),
        vm((8, width), F32),
        vm((12, 16, 128), F32),
        vm((items, hidden // DP), BF16),
        vm(piece, BF16), vm(piece, BF16), vm(piece, BF16), vm(piece, BF16), vm(piece, BF16),
        pltpu.SemaphoreType.DMA((12,)),
        pltpu.SemaphoreType.DMA((n_chunks,)),
        pltpu.SemaphoreType.DMA((n_sems,)),
        pltpu.SemaphoreType.DMA((n_sems,)),
    ]
    return pl.pallas_call(
        layer_kernel,
        out_shape=(
            vm((2, width // DP, n_chunks * CHUNK), BF16), vm((2, hidden // DP, width), BF16),
            vm((2, own * patches, width), BF16), vm((2, 8, 128), F32), vm((8, 128), F32),
        ),
        in_specs=[any_spec] * 8,
        out_specs=(pl.BlockSpec(memory_space=pltpu.VMEM),) * 5,
        scratch_shapes=scratch,
        compiler_params=pltpu.CompilerParams(
            collective_id=0, has_side_effects=True, vmem_limit_bytes=58 * 2**20
        ),
    )(tokens, positions, missing.reshape(1, items), wqkv, wout, wup, wdown, gains)


def widen_kernel(
    grads, down, tok, gain, loss, qkv_o, out_o, up_o, down_o, tok_o, gain_o, loss_o, qkv_v, out_v, up_v, down_v, tok_v, sem
):
    hidden, width = up_v.shape[2], out_v.shape[2]
    outs = []

    def send(value, wide, dst):
        wide[...] = value.astype(F32)
        outs.append(pltpu.make_async_copy(wide, dst, sem.at[len(outs)]))
        outs[-1].start()

    for m in range(2):
        send(tok[m], tok_v.at[m], tok_o.at[m])
        send(down[m], down_v.at[m], down_o.at[m])
        for lo, size, wide, dst in (
            (0, hidden, up_v, up_o), (hidden, width, out_v, out_o), (hidden + width, 3 * width, qkv_v, qkv_o)
        ):
            send(grads[m, :, lo : lo + size], wide.at[m], dst.at[m])
    loss_o[...] = loss[0:1, 0:1]
    gain_o[...] = gain[:, 0:2, 0 : gain_o.shape[2]]
    for cp in outs:
        cp.wait()


def widen_call(grads, down, tok, gain, loss, width, hidden):
    vm = pltpu.VMEM
    vmem_spec = pl.BlockSpec(memory_space=pltpu.VMEM)
    rows = width // DP
    shapes = ((2, rows, 3 * width), (2, rows, width), (2, rows, hidden), down.shape, tok.shape)
    ins = [pltpu.with_memory_space_constraint(v, pltpu.VMEM) for v in (grads, down, tok, gain, loss)]
    return pl.pallas_call(
        widen_kernel,
        out_shape=tuple(jax.ShapeDtypeStruct(shape, F32) for shape in shapes + ((2, 2, rows), (1, 1))),
        in_specs=[vmem_spec] * 5,
        out_specs=(pl.BlockSpec(memory_space=pl.ANY),) * 5 + (vmem_spec,) * 2,
        scratch_shapes=[vm(shape, F32) for shape in shapes] + [pltpu.SemaphoreType.DMA((10,))],
        compiler_params=pltpu.CompilerParams(vmem_limit_bytes=40 * 2**20),
    )(*ins)


def fused(tokens, positions, missing, qkv_weight, out_weight, up_weight, down_weight, norm_gains):
    grads, down, tok, gain, loss = layer_call(
        tokens, positions, missing, qkv_weight, out_weight, up_weight, down_weight, norm_gains
    )
    qkv, out, up, down, tok, gain, loss = widen_call(
        grads, down, tok, gain, loss, tokens.shape[2], up_weight.shape[2]
    )
    return (loss.reshape(()), tok, qkv, out, up, down, gain)


def lead_dot(left, right):
    return lax.dot_general(
        left, right, (((0,), (0,)), ((), ())), preferred_element_type=jnp.float32
    )


def tail_dot(left, right):
    return lax.dot_general(
        left, right, (((1,), (1,)), ((), ())), preferred_element_type=jnp.float32
    )


def norm_gain(values, gain):
    centre = values - jnp.mean(values, axis=-1, keepdims=True)
    spread = jnp.mean(centre * centre, axis=-1, keepdims=True)
    return centre * lax.rsqrt(spread + eps_norm) * gain


def unit_rows(pooled):
    return pooled * lax.rsqrt(jnp.sum(pooled * pooled, axis=1, keepdims=True) + eps_norm)


def gelu_exact(values):
    return jax.nn.gelu(values, approximate=False)


def alibi_bias(positions):
    grid_rows = (positions // GRID_W).astype(jnp.float32)
    grid_cols = (positions % GRID_W).astype(jnp.float32)
    row_gap = grid_rows[:, :, None] - grid_rows[:, None, :]
    col_gap = grid_cols[:, :, None] - grid_cols[:, None, :]
    distance = jnp.sqrt(row_gap * row_gap + col_gap * col_gap)
    slopes = jnp.exp2(-8.0 * (jnp.arange(HEADS) + 1).astype(jnp.float32) / HEADS)
    return -slopes[None, :, None, None] * distance[:, None, :, :]


def log_total(logits, valid_cols, valid_rows):
    row_max = jnp.max(logits, axis=1, keepdims=True)
    summed = jnp.sum(valid_cols[None, :] * jnp.exp(logits - row_max), axis=1) + (1.0 - valid_rows)
    return row_max[:, 0] + jnp.log(summed)


def row_grads(logits, log_sums, valid_rows, valid_cols, match, total_items):
    soft = valid_cols[None, :] * jnp.exp(logits - log_sums[:, None])
    return (valid_rows[:, None] / (2.0 * total_items) * (soft - match)).astype(jnp.bfloat16)


def block_forward(token_rows, alibi_terms, qkv_weight, out_weight, up_weight, down_weight, gains):
    row_count, model_width = token_rows.shape
    images, patches = (alibi_terms.shape[0], alibi_terms.shape[2])
    head_dim = model_width // HEADS
    score_scale = head_dim ** (-0.5)
    start_rows = token_rows.astype(jnp.float32)
    normed_one = norm_gain(start_rows, gains[0]).astype(jnp.bfloat16)
    projected = jnp.dot(normed_one, qkv_weight, preferred_element_type=jnp.float32).astype(
        jnp.bfloat16
    )
    queries = projected[:, :model_width].reshape(images, patches, HEADS, head_dim)
    key_rows = projected[:, model_width : 2 * model_width].reshape(images, patches, HEADS, head_dim)
    value_rows = projected[:, 2 * model_width :].reshape(images, patches, HEADS, head_dim)
    scores = jnp.einsum("iqhd,ikhd->ihqk", queries, key_rows, preferred_element_type=jnp.float32)
    attn_probs = jax.nn.softmax(scores * score_scale + alibi_terms, axis=-1)
    probs_low = attn_probs.astype(jnp.bfloat16)
    attended = jnp.einsum(
        "ihqk,ikhd->iqhd", probs_low, value_rows, preferred_element_type=jnp.float32
    )
    attended = attended.reshape(row_count, model_width).astype(jnp.bfloat16)
    residual = start_rows + jnp.dot(attended, out_weight, preferred_element_type=jnp.float32)
    normed_two = norm_gain(residual, gains[1]).astype(jnp.bfloat16)
    hidden_pre = jnp.dot(normed_two, up_weight, preferred_element_type=jnp.float32)
    active = gelu_exact(hidden_pre).astype(jnp.bfloat16)
    out_rows = residual + jnp.dot(active, down_weight, preferred_element_type=jnp.float32)
    saved = (
        start_rows,
        normed_one,
        projected,
        attn_probs,
        probs_low,
        attended,
        residual,
        normed_two,
        hidden_pre,
        active,
    )
    return (out_rows, saved)


def block_backward(grad_rows, saved, qkv_weight, out_weight, up_weight, down_weight, gains):
    (
        start_rows,
        normed_one,
        projected,
        attn_probs,
        probs_low,
        attended,
        residual,
        normed_two,
        hidden_pre,
        active,
    ) = saved
    images, head_count, patches = (attn_probs.shape[0], attn_probs.shape[1], attn_probs.shape[2])
    row_count, model_width = grad_rows.shape
    head_dim = model_width // head_count
    score_scale = head_dim ** (-0.5)
    down_in = grad_rows.astype(jnp.bfloat16)
    grad_down = lead_dot(active, down_in)
    grad_active = tail_dot(down_in, down_weight)
    _, gelu_back = jax.vjp(gelu_exact, hidden_pre)
    grad_hidden = gelu_back(grad_active)[0].astype(jnp.bfloat16)
    grad_up = lead_dot(normed_two, grad_hidden)
    grad_h_two = tail_dot(grad_hidden, up_weight)
    _, norm_two_back = jax.vjp(norm_gain, residual, gains[1])
    grad_mid, gain_two = norm_two_back(grad_h_two)
    grad_residual = grad_rows + grad_mid
    attn_in = grad_residual.astype(jnp.bfloat16)
    grad_out = lead_dot(attended, attn_in)
    grad_att = (
        tail_dot(attn_in, out_weight)
        .astype(jnp.bfloat16)
        .reshape(images, patches, head_count, head_dim)
    )
    queries = projected[:, :model_width].reshape(images, patches, head_count, head_dim)
    key_rows = projected[:, model_width : 2 * model_width].reshape(
        images, patches, head_count, head_dim
    )
    value_rows = projected[:, 2 * model_width :].reshape(images, patches, head_count, head_dim)
    grad_values = jnp.einsum(
        "ihqk,iqhd->ikhd", probs_low, grad_att, preferred_element_type=jnp.float32
    )
    grad_probs = jnp.einsum(
        "iqhd,ikhd->ihqk", grad_att, value_rows, preferred_element_type=jnp.float32
    )
    grad_scores = attn_probs * (
        grad_probs - jnp.sum(grad_probs * attn_probs, axis=-1, keepdims=True)
    )
    grad_scores = grad_scores.astype(jnp.bfloat16)
    grad_queries = (
        jnp.einsum("ihqk,ikhd->iqhd", grad_scores, key_rows, preferred_element_type=jnp.float32)
        * score_scale
    )
    grad_keys = (
        jnp.einsum("ihqk,iqhd->ikhd", grad_scores, queries, preferred_element_type=jnp.float32)
        * score_scale
    )
    grad_proj = jnp.concatenate(
        [
            grad_queries.reshape(row_count, model_width),
            grad_keys.reshape(row_count, model_width),
            grad_values.reshape(row_count, model_width),
        ],
        axis=1,
    ).astype(jnp.bfloat16)
    grad_qkv = lead_dot(normed_one, grad_proj)
    grad_h_one = tail_dot(grad_proj, qkv_weight)
    _, norm_one_back = jax.vjp(norm_gain, start_rows, gains[0])
    grad_first, gain_one = norm_one_back(grad_h_one)
    weight_grads = (grad_qkv, grad_out, grad_up, grad_down, jnp.stack([gain_one, gain_two]))
    return (grad_residual + grad_first, weight_grads)


def local(tokens, positions, missing, qkv_weight, out_weight, up_weight, down_weight, norm_gains):
    own_images = positions.shape[0]
    model_width = tokens.shape[2]
    patches = tokens.shape[1] // own_images
    first_row = lax.axis_index(("dp", "rep")) * own_images
    alibi_terms = alibi_bias(positions)
    saved_list = []
    pooled_list = []
    normed = []
    for modality in range(2):
        out_rows, saved = block_forward(
            tokens[modality],
            alibi_terms,
            qkv_weight[modality],
            out_weight[modality],
            up_weight[modality],
            down_weight[modality],
            norm_gains[modality],
        )
        pooled = jnp.sum(out_rows.reshape(own_images, patches, model_width), axis=1)
        saved_list.append(saved)
        pooled_list.append(pooled)
        normed.append(unit_rows(pooled).astype(jnp.bfloat16))
    valid_all = 1.0 - missing.astype(jnp.float32)
    total_items = float(missing.shape[0])
    valid_own = lax.dynamic_slice_in_dim(valid_all, first_row, own_images)
    radar_all, optic_all = (
        lax.all_gather(normed[0], ("dp", "rep"), axis=0, tiled=True),
        lax.all_gather(normed[1], ("dp", "rep"), axis=0, tiled=True),
    )
    images_all = radar_all.shape[0]
    match_own = (
        lax.broadcasted_iota(jnp.int32, (own_images, images_all), 0) + first_row
        == lax.broadcasted_iota(jnp.int32, (own_images, images_all), 1)
    ).astype(jnp.float32)
    logits_r = tail_dot(normed[0], optic_all) * inv_temp
    logits_o = tail_dot(normed[1], radar_all) * inv_temp
    lse_r = log_total(logits_r, valid_all, valid_own)
    lse_o = log_total(logits_o, valid_all, valid_own)
    item_terms = valid_own * (
        lse_r
        - jnp.sum(logits_r * match_own, axis=1)
        + lse_o
        - jnp.sum(logits_o * match_own, axis=1)
    )
    grad_lr = row_grads(logits_r, lse_r, valid_own, valid_all, match_own, total_items)
    grad_lo = row_grads(logits_o, lse_o, valid_own, valid_all, match_own, total_items)
    grad_ur = jnp.dot(grad_lr, optic_all, preferred_element_type=jnp.float32) * inv_temp
    grad_uo = jnp.dot(grad_lo, radar_all, preferred_element_type=jnp.float32) * inv_temp
    summed_terms = lax.psum(jnp.sum(item_terms), ("dp", "rep"))
    loss_value = summed_terms / (2.0 * total_items)
    share_o = lead_dot(grad_lr, normed[0]) * inv_temp
    share_r = lead_dot(grad_lo, normed[1]) * inv_temp
    back_r, back_o = (
        lax.psum_scatter(share_r, ("dp", "rep"), scatter_dimension=0, tiled=True),
        lax.psum_scatter(share_o, ("dp", "rep"), scatter_dimension=0, tiled=True),
    )
    grad_ur = grad_ur + back_r
    grad_uo = grad_uo + back_o
    grad_units = (grad_ur, grad_uo)
    token_list = []
    block_grads = []
    for modality in range(2):
        _, unit_back = jax.vjp(unit_rows, pooled_list[modality])
        grad_pooled = unit_back(grad_units[modality])[0]
        grad_rows = jnp.broadcast_to(grad_pooled[:, None, :], (own_images, patches, model_width))
        grad_rows = grad_rows.reshape(own_images * patches, model_width)
        grad_tokens, weight_grads = block_backward(
            grad_rows,
            saved_list[modality],
            qkv_weight[modality],
            out_weight[modality],
            up_weight[modality],
            down_weight[modality],
            norm_gains[modality],
        )
        token_list.append(grad_tokens)
        block_grads.append(list(weight_grads))
    stacked = [jnp.stack([block_grads[0][slot], block_grads[1][slot]]) for slot in range(5)]
    shares = (
        lax.psum_scatter(stacked[0], "dp", scatter_dimension=1, tiled=True),
        lax.psum_scatter(stacked[1], "dp", scatter_dimension=1, tiled=True),
        lax.psum_scatter(stacked[2], "dp", scatter_dimension=1, tiled=True),
        lax.psum_scatter(stacked[3], "dp", scatter_dimension=1, tiled=True),
        lax.psum_scatter(stacked[4], "dp", scatter_dimension=2, tiled=True),
    )
    summed = (
        lax.psum(shares[0].astype(jnp.bfloat16), "rep").astype(jnp.float32),
        lax.psum(shares[1].astype(jnp.bfloat16), "rep").astype(jnp.float32),
        lax.psum(shares[2].astype(jnp.bfloat16), "rep").astype(jnp.float32),
        lax.psum(shares[3].astype(jnp.bfloat16), "rep").astype(jnp.float32),
        lax.psum(shares[4].astype(jnp.bfloat16), "rep").astype(jnp.float32),
    )
    stacked = list(summed)
    token_grads = jnp.stack(token_list)
    return (loss_value, token_grads, stacked[0], stacked[1], stacked[2], stacked[3], stacked[4])


def solution(mesh):
    in_specs = (P(None, ("dp", "rep"), None), P(("dp", "rep"), None), P(), P(), P(), P(), P(), P())
    out_specs = (
        P(),
        P(None, ("dp", "rep"), None),
        P(None, "dp", None),
        P(None, "dp", None),
        P(None, "dp", None),
        P(None, "dp", None),
        P(None, None, "dp"),
    )
    one_kernel = mesh.shape["dp"] == DP and mesh.shape["rep"] == REP
    step = fused if one_kernel else local
    return jax.shard_map(step, mesh=mesh, in_specs=in_specs, out_specs=out_specs, check_vma=False)
```

```python
import functools

import jax
import jax.numpy as jnp
from jax import lax
from jax.experimental import pallas as pl
from jax.experimental.pallas import tpu as pltpu
from jax.sharding import PartitionSpec as P

HEADS = 12
GRID_W = 12
MESH = pl.DeviceIdType.MESH
F32 = jnp.float32
BF16 = jnp.bfloat16

eps_norm = 1e-06
inv_temp = 32.0
SQRT_HALF = 0.7071067811865476
INV_SQRT_TWO_PI = 0.3989422804014327
HALF_LOG2_E = -0.7213475204444817

DP = 8
REP = 4
CHUNK = 256


def nt_dot(left, right):
    return lax.dot_general(left, right, (((1,), (1,)), ((), ())), preferred_element_type=F32)


def tn_dot(left, right):
    return lax.dot_general(left, right, (((0,), (0,)), ((), ())), preferred_element_type=F32)


def nn_dot(left, right):
    return jnp.dot(left, right, preferred_element_type=F32)


def normalized(values):
    centre = values - jnp.mean(values, axis=-1, keepdims=True)
    scale = lax.rsqrt(jnp.mean(centre * centre, axis=-1, keepdims=True) + eps_norm)
    return centre * scale, scale


def gelu_and_slope(values):
    cdf = 0.5 + 0.5 * lax.erf(values * SQRT_HALF)
    return values * cdf, cdf + values * (jnp.exp2(values * values * HALF_LOG2_E) * INV_SQRT_TWO_PI)


S_TOK, S_POS, S_A, S_AX, S_B, S_BX, S_G, S_GX = 0, 1, 2, 18, 19, 35, 36, 52
S_HT, S_GB, S_TG = 53, 65, 73
S_Y = 74


def layer_kernel(
    tokens, positions_h, missing_h, wqkv_h, wout_h, wup_h, wdown_h, gains_h,
    grad_out, down_out, token_out, gain_out, loss_out,
    positions, missing, gains, wqkv, wout, wup, wdown, tok, posb, h_one, proj, probs, att, resid, h_two, slope,
    asum, rsum, pool, msg_a, recv_a, msg_b, send_b, recv_b, recv_b2, units, downs, downs_lo, ga, gp_own,
    h_t, ht, gbuf, gatt, gh, gacc, gsum, as_mat,
    ysend, keep, yrecv, ring_a, ring_b,
    load_sem, ss, rs,
):
    width = h_one.shape[1]
    hidden = wup.shape[1]
    rows = h_one.shape[0]
    half = rows // 2
    patches = half // 2
    pairs = HEADS // 2
    lanes = 128
    pieces = width // lanes
    items = missing.shape[1]
    n_wide = hidden // width
    n_blocks = n_wide + 4
    per_block = width // CHUNK
    n_chunks = n_blocks * per_block
    score_scale = (width // HEADS) ** -0.5

    S_OI, S_II, S_IO, S_X = (S_Y + n_chunks * n for n in range(1, 5))

    dp = lax.axis_index("dp")
    z = lax.axis_index("rep")
    c = dp % 2
    x = (dp // 2) % 2
    y = dp // 4
    yz = y * 4 + z

    def at(yy, xx, cc, zz):
        return (yy * 4 + xx * 2 + cc, zz)

    core_dev = at(y, x, 1 - c, z)
    x_dev = at(y, 1 - x, c, z)
    y_dev = at(1 - y, x, c, z)
    inner = jnp.logical_and(z >= 1, z <= 2)
    outer = jnp.logical_not(inner)
    high = z // 2
    inner_peer = at(y, x, c, 3 - z)
    outer_peer = at(y, x, c, 3 * high)
    inward_peer = at(y, x, c, 1 + high)

    def others():
        for k in range(1, 16):
            yield k, y ^ (k & 1), x ^ ((k >> 1) & 1), (z + (k >> 2)) % 4

    def rc(src, dst, idx, dev):
        return pltpu.make_async_remote_copy(
            src_ref=src, dst_ref=dst, send_sem=ss.at[idx], recv_sem=rs.at[idx],
            device_id=dev, device_id_type=MESH,
        )

    def own_rows(xx):
        return pl.ds(pl.multiple_of(xx * half, half), half)

    barrier = pltpu.get_barrier_semaphore()
    for k, yy, xx, zz in others():
        pl.semaphore_signal(barrier, inc=1, device_id=at(yy, xx, c, zz), device_id_type=MESH)
    pl.semaphore_signal(barrier, inc=1, device_id=core_dev, device_id_type=MESH)
    early = [
        (positions_h, positions), (tokens.at[x], tok.at[own_rows(x)]), (gains_h.at[x], gains), (wqkv_h.at[x], wqkv),
        (missing_h, missing),
    ]
    late = [(wout_h.at[x], wout), (wup_h.at[x], wup), (wdown_h.at[x], wdown)]
    loads = [pltpu.make_async_copy(src, dst, load_sem.at[n]) for n, (src, dst) in enumerate(early + late)]
    for load in loads[: len(early)]:
        load.start()
    load_pos, load_tok, load_gains, load_qkv, load_missing, load_out, load_up, load_down = loads
    pl.semaphore_wait(barrier, 16)
    tok_send = rc(tokens.at[1 - x], tok.at[own_rows(x)], S_TOK, x_dev)
    tok_send.start()
    posb[x] = jnp.zeros((8, lanes), F32)
    asum[...] = jnp.zeros_like(asum)
    rsum[...] = jnp.zeros_like(rsum)
    pool[...] = jnp.zeros_like(pool)
    gacc[...] = jnp.zeros_like(gacc)

    load_pos.wait()
    cells = positions[...].astype(F32)
    cell_rows = jnp.floor((cells + 0.5) * (1.0 / GRID_W))
    cell_cols = cells - GRID_W * cell_rows
    posb[x, 0:2, 0:patches] = cell_rows
    posb[x, 2:4, 0:patches] = cell_cols

    pos_send = rc(posb.at[x], posb.at[x], S_POS, x_dev)
    pos_send.start()

    low_lanes = lax.broadcasted_iota(jnp.int32, (patches, lanes), 1) < lanes // 2
    mask_low = low_lanes.astype(F32).astype(BF16)
    mask_high = (1.0 - low_lanes.astype(F32)).astype(BF16)

    def two_heads(values):
        return jnp.concatenate([values * mask_low, values * mask_high], axis=0)

    def fold_heads(values):
        return jnp.where(low_lanes, values[:patches], values[patches:])

    def img_rows(i):
        return pl.ds(pl.multiple_of(i * patches, patches), patches)

    load_tok.wait()
    load_gains.wait()
    gain_one = gains[0:1, :]
    gain_two = gains[1:2, :]

    def attention(xx):
        def image(j, carry):
            r = img_rows(xx * 2 + j)
            cr = jnp.broadcast_to(posb[xx, pl.ds(j, 1), :], (lanes, lanes))
            cc = jnp.broadcast_to(posb[xx, pl.ds(j + 2, 1), :], (lanes, lanes))
            row_gap = cr.T - cr
            col_gap = cc.T - cc
            dist = jnp.sqrt(row_gap * row_gap + col_gap * col_gap)[:patches, :patches]
            raw = []
            for p in range(pairs):
                q = two_heads(proj[r, p * lanes : (p + 1) * lanes])
                raw.append(nt_dot(q, proj[r, width + p * lanes : width + (p + 1) * lanes]))
            soft = []
            for p in range(pairs):
                slopes = [2.0 ** (-8.0 * (2 * p + h + 1) / HEADS) for h in range(2)]
                alibi = jnp.concatenate([dist * -slopes[0], dist * -slopes[1]], axis=0)
                s = raw[p] * score_scale + alibi
                e = jnp.exp(s - jnp.max(s, axis=-1, keepdims=True))
                prob = e * (1.0 / jnp.sum(e, axis=-1, keepdims=True))
                probs[(xx * 2 + j) * pairs + p] = prob
                soft.append(prob.astype(BF16))
            for p in range(pairs):
                v = proj[r, 2 * width + p * lanes : 2 * width + (p + 1) * lanes]
                att[r, p * lanes : (p + 1) * lanes] = fold_heads(nn_dot(soft[p], v)).astype(BF16)
            return carry

        lax.fori_loop(0, 2, image, 0, unroll=True)

    def wide(j):
        return pl.ds(pl.multiple_of(j * width, width), width)

    def add_pool(j, on):
        a = asum[:, wide(j)] * on
        a_high = a.astype(BF16).astype(F32)
        both = jnp.concatenate([a_high, a - a_high], axis=0).astype(BF16)
        pool[...] += nn_dot(both, wdown[wide(j), :])

    for step in range(2):
        xx = x if step == 0 else 1 - x
        where = own_rows(xx)
        if step == 1:
            tok_send.wait_recv()
            pos_send.wait_recv()
        for j in range(2):
            r = img_rows(xx * 2 + j)
            n, _ = normalized(tok[r, :].astype(F32))
            h_one[r, :] = (n * gain_one).astype(BF16)
        if step == 0:
            load_qkv.wait()
            load_out.start()
            load_up.start()
            load_down.start()
        for n in range(3):
            cols = slice(n * width, (n + 1) * width)
            proj[where, cols] = nn_dot(h_one[where, :], wqkv[:, cols]).astype(BF16)
        attention(xx)
        if step == 0:
            load_out.wait()
        resid[where, :] = tok[where, :].astype(F32) + nn_dot(att[where, :], wout[...])
        for j in range(2):
            i = xx * 2 + j
            r = img_rows(i)
            v = resid[r, :]
            rsum[pl.ds(i, 1), :] = jnp.sum(v, axis=0, keepdims=True)
            n, _ = normalized(v)
            h_two[r, :] = (n * gain_two).astype(BF16)
        if step == 0:
            load_up.wait()
        else:
            load_down.wait()

        def feed(j, carry, where=where, xx=xx, step=step):
            for n in range(width // 256):
                cols = pl.ds(pl.multiple_of(j * width + n * 256, 256), 256)
                pre = nn_dot(h_two[where, :], wup[:, cols])
                act, slp = gelu_and_slope(pre)
                slope[where, cols] = slp.astype(BF16)
                act = act.astype(BF16).astype(F32)
                for i in range(2):
                    asum[pl.ds(xx * 2 + i, 1), cols] = jnp.sum(act[i * patches : (i + 1) * patches], axis=0, keepdims=True)
            if step == 1:
                add_pool(jnp.maximum(j - 1, 0), (j > 0).astype(F32))
            return carry

        lax.fori_loop(0, n_wide, feed, 0)
    add_pool(n_wide - 1, 1.0)

    pooled = rsum[...] + pool[0:8, :] + pool[8:16, :]
    s_own = lax.rsqrt(jnp.sum(pooled * pooled, axis=1, keepdims=True) + eps_norm)
    unit = pooled * s_own
    for q in range(pieces):
        msg_a[4 * q : 4 * q + 4, :] = unit[0:4, q * lanes : (q + 1) * lanes]
    s_high = s_own.astype(BF16).astype(F32)
    msg_a[24:28, :] = jnp.broadcast_to(s_high[0:4], (4, lanes))
    msg_a[28:32, :] = jnp.broadcast_to((s_own - s_high)[0:4], (4, lanes))
    recv_a[c, x, yz] = msg_a[...].astype(BF16)
    a_copies = []
    for k, yy, xx, zz in others():
        a_copies.append(rc(recv_a.at[c, x, yz], recv_a.at[c, x, yz], S_A + k, at(yy, xx, c, zz)))
        a_copies[-1].start()

    msg_b[...] = jnp.zeros_like(msg_b)
    for block in range(DP):
        for q in range(3):
            lo = block * 3 * lanes + q * lanes
            msg_b[block, 4 * q : 4 * q + 4, :] = asum[0:4, lo : lo + lanes]
    for block in range(DP):
        send_b[block // 2, block % 2] = msg_b[block].astype(BF16)
    recv_b[x, yz] = send_b[y * 2 + x]
    ht_copies = []
    for w, src in enumerate((h_two, att, h_one)):
        h_t[w] = src[...].T
        for rel in range(2):
            yy = y if rel == 1 else 1 - y
            for xx in range(2):
                base = yy * (width // 2) + xx * (width // 4)
                mine = pl.ds(pl.multiple_of(base + c * (width // 8), width // 8), width // 8)
                theirs = pl.ds(pl.multiple_of(base + (1 - c) * (width // 8), width // 8), width // 8)
                lo = (rel * 2 + xx) * (width // 8)
                ht[w, lo : lo + width // 8, 0:rows] = h_t[w, mine, :]
                ht_copies.append(
                    rc(
                        h_t.at[w, theirs, :],
                        ht.at[w, pl.ds(lo, width // 8), pl.ds(rows, rows)],
                        S_HT + w * 4 + rel * 2 + xx,
                        core_dev,
                    )
                )
                ht_copies[-1].start()

    n_sel = 8 * 32
    sel_row = lax.broadcasted_iota(jnp.int32, (n_sel, n_sel), 0)
    sel_col = lax.broadcasted_iota(jnp.int32, (n_sel, n_sel), 1)
    pick = ((sel_row >> 2) & 7) * 32 + (sel_row >> 5) * 4 + (sel_row & 3)
    select_a = (sel_col == pick).astype(F32).astype(BF16)

    p_i = lax.broadcasted_iota(jnp.int32, (items, items), 0)
    q_i = lax.broadcasted_iota(jnp.int32, (items, items), 1)
    place = ((((p_i >> 4) & 1) * 4 + ((p_i >> 1) & 1) * 2 + (p_i >> 5)) * 4 + ((p_i >> 2) & 3)) * 2 + (p_i & 1)
    eye = (p_i == q_i).astype(F32)
    load_missing.wait()
    v_nat = 1.0 - missing[...].astype(F32)
    v_col = jnp.sum((q_i == place).astype(F32) * v_nat, axis=1, keepdims=True)
    v_row = jnp.sum(eye * v_col, axis=0, keepdims=True)

    for cp in a_copies:
        cp.wait_recv()
    ax_copy = rc(recv_a.at[c], recv_a.at[c], S_AX, core_dev)
    ax_copy.start()
    b_copies = []
    for k, yy, xx, zz in others():
        b_copies.append(rc(send_b.at[yy * 2 + xx], recv_b.at[x, yz], S_B + k, at(yy, xx, c, zz)))
        b_copies[-1].start()
    ax_copy.wait_recv()

    scales = [[None, None], [None, None]]
    for core in range(2):
        for m in range(2):
            got = nn_dot(select_a, recv_a[core, m].reshape(n_sel, lanes))
            for q in range(pieces):
                units[m, core * 32 : core * 32 + 32, q * lanes : (q + 1) * lanes] = got[q * 32 : q * 32 + 32].astype(BF16)
            scales[m][core] = got[6 * 32 : 7 * 32] + got[7 * 32 :]
    scale_cols = [jnp.concatenate(scales[m], axis=0)[:, 0:1] for m in range(2)]

    u_r, u_o = units[0], units[1]
    logits = nt_dot(u_r, u_o) * inv_temp
    top_r = jnp.max(logits, axis=1, keepdims=True)
    lse_r = top_r + jnp.log(jnp.sum(v_row * jnp.exp(logits - top_r), axis=1, keepdims=True) + (1.0 - v_col))
    top_o = jnp.max(logits, axis=0, keepdims=True)
    lse_o = top_o + jnp.log(jnp.sum(v_col * jnp.exp(logits - top_o), axis=0, keepdims=True) + (1.0 - v_row))
    diag = logits * eye
    terms_r = v_col * (lse_r - jnp.sum(diag, axis=1, keepdims=True))
    terms_o = v_row * (lse_o - jnp.sum(diag, axis=0, keepdims=True))
    loss = (jnp.sum(terms_r, axis=0, keepdims=True) + jnp.sum(terms_o, axis=1, keepdims=True)) / (2.0 * items)
    loss_out[...] = jnp.broadcast_to(loss, loss_out.shape)
    grad_r = (v_col / (2.0 * items) * (v_row * jnp.exp(logits - lse_r) - eye)).astype(BF16)
    grad_ot = (v_row / (2.0 * items) * (v_col * jnp.exp(logits - lse_o) - eye)).astype(BF16)
    grad_u = [
        (nn_dot(grad_r, u_o) + nn_dot(grad_ot, u_o)) * inv_temp,
        (tn_dot(grad_r, u_r) + tn_dot(grad_ot, u_r)) * inv_temp,
    ]
    for m in range(2):
        u = units[m].astype(F32)
        g = grad_u[m]
        gp = scale_cols[m] * (g - u * jnp.sum(u * g, axis=1, keepdims=True))
        high_part = gp.astype(BF16)
        downs[m] = high_part
        downs_lo[m] = (gp - high_part.astype(F32)).astype(BF16)
    own_r = lax.broadcasted_iota(jnp.int32, (16, items), 0)
    own_c = lax.broadcasted_iota(jnp.int32, (16, items), 1)
    mine = jnp.logical_and(own_r < 4, own_c == c * 32 + yz * 4 + own_r).astype(F32).astype(BF16)
    down_own = nn_dot(mine, downs[x])
    gp_own[...] = (down_own + nn_dot(mine, downs_lo[x]))[0:8]
    down_own = down_own.astype(BF16)

    def y_copy(k):
        return rc(ysend.at[k], yrecv.at[k], S_Y + k, y_dev)

    def oi_copy(k):
        return rc(keep.at[k], ring_a.at[k], S_OI + k, inward_peer)

    def ii_copy(k):
        return rc(ring_a.at[k], ring_b.at[k], S_II + k, inner_peer)

    def io_copy(k):
        return rc(ring_b.at[k], ring_a.at[k], S_IO + k, outer_peer)

    def out_cols(k):
        return pl.ds(pl.multiple_of(k * CHUNK, CHUNK), CHUNK)

    quarter = width // 8

    def x_copy(k):
        return rc(
            yrecv.at[k, pl.ds(pl.multiple_of((1 - x) * quarter, quarter), quarter), :],
            grad_out.at[x, :, out_cols(k)], S_X + k, x_dev,
        )

    def store_here(k):
        here = pl.ds(pl.multiple_of(x * quarter, quarter), quarter)
        grad_out[x, :, out_cols(k)] = yrecv[k, here, :]

    def step_y(k):
        y_copy(k).wait_recv()
        keep[k] = (keep[k].astype(F32) + yrecv[k].astype(F32)).astype(BF16)

        @pl.when(outer)
        def _():
            oi_copy(k).start()

    def step_a(k):
        @pl.when(inner)
        def _():
            oi_copy(k).wait_recv()
            ring_a[k] = (ring_a[k].astype(F32) + keep[k].astype(F32)).astype(BF16)
            ii_copy(k).start()

    def step_b(k):
        @pl.when(inner)
        def _():
            ii_copy(k).wait_recv()
            got = ring_b[k].astype(F32)
            ring_b[k] = (got + keep[k].astype(F32)).astype(BF16)
            io_copy(k).start()
            yrecv[k] = (got + ring_a[k].astype(F32)).astype(BF16)
            x_copy(k).start()
            store_here(k)

    def step_c(k):
        @pl.when(outer)
        def _():
            io_copy(k).wait_recv()
            yrecv[k] = (keep[k].astype(F32) + ring_a[k].astype(F32)).astype(BF16)
            x_copy(k).start()
            store_here(k)

    def comm(t):
        for lag, step in ((0, step_y), (2, step_a), (4, step_b), (6, step_c)):
            @pl.when(jnp.logical_and(t >= lag, t < n_chunks + lag))
            def _(step=step, lag=lag):
                step(t - lag)

    def gb_copy(j):
        return rc(gbuf.at[j, pl.ds(0, rows), :], gbuf.at[j, pl.ds(rows, rows), :], S_GB + j, core_dev)

    def wgrad(j, w):
        gb_copy(j).wait_recv()
        for n in range(per_block):
            both = nn_dot(ht[w], gbuf[j, :, n * CHUNK : (n + 1) * CHUNK])
            k = j * per_block + n
            ysend[k] = both[:half].astype(BF16)
            y_copy(k).start()
            keep[k] = both[half:].astype(BF16)

    for cp in ht_copies[:4]:
        cp.wait_recv()

    def back_hidden(j, carry):
        cols = pl.ds(pl.multiple_of(j * width, width), width)
        ga[...] = nt_dot(down_own, wdown[cols, :])
        for i in range(4):
            r = slice(i * patches, (i + 1) * patches)
            gbuf[j, r, :] = (ga[i : i + 1, :] * slope[r, cols].astype(F32)).astype(BF16)
        gb_copy(j).start()

        @pl.when(j > 0)
        def _():
            wgrad(j - 1, 0)

        return carry

    lax.fori_loop(0, n_wide, back_hidden, 0)
    wgrad(n_wide - 1, 0)
    comm(0)

    gh[...] = jnp.zeros_like(gh)

    def back_up(j, carry):
        cols = pl.ds(pl.multiple_of(j * width, width), width)
        gh[...] += nt_dot(gbuf[j, 0:rows, :], wup[:, cols])

        @pl.when(j == 2)
        def _():
            comm(1)

        return carry

    lax.fori_loop(0, n_wide, back_up, 0)

    for i in range(4):
        r = slice(i * patches, (i + 1) * patches)
        n, s = normalized(resid[r, :])
        gy = gh[r, :]
        gacc[1:2, :] += jnp.sum(gy * n, axis=0, keepdims=True)
        gyg = gy * gain_two
        grad = s * (gyg - jnp.mean(gyg, axis=-1, keepdims=True) - n * jnp.mean(gyg * n, axis=-1, keepdims=True))
        grad = grad + gp_own[i : i + 1, :]
        resid[r, :] = grad
        gbuf[n_wide, r, :] = grad.astype(BF16)
    gb_copy(n_wide).start()
    gatt[...] = nt_dot(gbuf[n_wide, 0:rows, :], wout[...]).astype(BF16)
    comm(2)
    for cp in ht_copies[4:8]:
        cp.wait_recv()
    wgrad(n_wide, 1)

    def back_attention(i, carry):
        r = img_rows(i)
        das, dps, dss = [], [], []
        for p in range(pairs):
            da = two_heads(gatt[r, p * lanes : (p + 1) * lanes])
            das.append(da)
            dps.append(nt_dot(da, proj[r, 2 * width + p * lanes : 2 * width + (p + 1) * lanes]))
        for p in range(pairs):
            cols = slice(p * lanes, (p + 1) * lanes)
            prob = probs[i * pairs + p]
            dss.append((prob * (dps[p] - jnp.sum(dps[p] * prob, axis=-1, keepdims=True))).astype(BF16))
            gbuf[n_wide + 3, r, cols] = tn_dot(prob.astype(BF16), das[p]).astype(BF16)
        for p in range(pairs):
            cols = slice(p * lanes, (p + 1) * lanes)
            q = two_heads(proj[r, cols])
            k = proj[r, width + p * lanes : width + (p + 1) * lanes]
            gbuf[n_wide + 1, r, cols] = (fold_heads(nn_dot(dss[p], k)) * score_scale).astype(BF16)
            gbuf[n_wide + 2, r, cols] = (tn_dot(dss[p], q) * score_scale).astype(BF16)
        comm(3 + i)
        return carry

    lax.fori_loop(0, 4, back_attention, 0)
    for n in range(3):
        gb_copy(n_wide + 1 + n).start()
    gh[...] = jnp.zeros_like(gh)

    def back_proj(n, carry):
        cols = pl.ds(pl.multiple_of(n * width, width), width)
        gh[...] += nt_dot(gbuf[n_wide + 1 + n, 0:rows, :], wqkv[:, cols])
        return carry

    lax.fori_loop(0, 3, back_proj, 0)
    comm(7)

    for i in range(4):
        r = slice(i * patches, (i + 1) * patches)
        n, s = normalized(tok[r, :].astype(F32))
        gy = gh[r, :]
        gacc[0:1, :] += jnp.sum(gy * n, axis=0, keepdims=True)
        gyg = gy * gain_one
        grad = s * (gyg - jnp.mean(gyg, axis=-1, keepdims=True) - n * jnp.mean(gyg * n, axis=-1, keepdims=True))
        tok[r, :] = (resid[r, :] + grad).astype(BF16)
    tg_copy = rc(tok.at[own_rows(1 - x)], token_out.at[x], S_TG, x_dev)
    tg_copy.start()
    tg_here = pltpu.make_async_copy(tok.at[own_rows(x)], token_out.at[x], load_sem.at[9])
    tg_here.start()

    def gain_copy(src, dst, n, dev):
        return rc(gsum.at[src], gsum.at[dst], S_G + n, dev)

    g_core = gain_copy(0, 1, 0, core_dev)
    g_y = gain_copy(2, 3, 1, y_dev)
    g_oi = gain_copy(4, 5, 2, inward_peer)
    g_ii = gain_copy(6, 7, 3, inner_peer)
    g_io = gain_copy(8, 9, 4, outer_peer)
    g_x = gain_copy(10, 11, 5, x_dev)
    gsum[0] = jnp.zeros_like(gsum[0])
    for n in range(2):
        for q in range(pieces):
            row = n * pieces + q
            gsum[0, row : row + 1, :] = gacc[n : n + 1, q * lanes : (q + 1) * lanes]
    g_core.start()

    def gain_y():
        g_core.wait_recv()
        gsum[2] = gsum[0] + gsum[1]
        g_y.start()

    def gain_oi():
        g_y.wait_recv()
        gsum[4] = gsum[2] + gsum[3]

        @pl.when(outer)
        def _():
            g_oi.start()

    def gain_ii():
        @pl.when(inner)
        def _():
            g_oi.wait_recv()
            gsum[6] = gsum[5] + gsum[4]
            g_ii.start()

    def gain_io():
        @pl.when(inner)
        def _():
            g_ii.wait_recv()
            gsum[8] = gsum[7] + gsum[4]
            g_io.start()
            gsum[10] = gsum[7] + gsum[6]
            g_x.start()

    def gain_x():
        @pl.when(outer)
        def _():
            g_io.wait_recv()
            gsum[10] = gsum[4] + gsum[9]
            g_x.start()

    comm(8)
    for cp in ht_copies[8:12]:
        cp.wait_recv()
    for n in range(3):
        wgrad(n_wide + 1 + n, 2)
        if n == 0:
            gain_y()
        comm(9 + n)

    comm(12)

    for cp in b_copies:
        cp.wait_recv()
    bx_copy = rc(recv_b.at[:, :, 1 - c], recv_b2, S_BX, core_dev)
    bx_copy.start()
    sb_row = lax.broadcasted_iota(jnp.int32, (96, 128), 0)
    sb_col = lax.broadcasted_iota(jnp.int32, (96, 128), 1)
    pick_b = ((sb_row >> 2) & 7) * 16 + (sb_row >> 5) * 4 + (sb_row & 3)
    select_b = (sb_col == pick_b).astype(F32).astype(BF16)
    comm(13)
    bx_copy.wait_recv()
    for m in range(2):
        for src, cc in ((recv_b[m, :, c], c), (recv_b2[m], 1 - c)):
            got = nn_dot(select_b, src.reshape(128, lanes)).astype(BF16)
            to = pl.ds(pl.multiple_of(cc * 32, 32), 32)
            for q in range(3):
                as_mat[to, q * lanes : (q + 1) * lanes] = got[q * 32 : (q + 1) * 32]
        down_out[m] = tn_dot(as_mat[...], downs[m]).astype(BF16)
    comm(14)

    def finish(k, carry):
        y_copy(k).wait_send()
        x_copy(k).wait()

        @pl.when(outer)
        def _():
            oi_copy(k).wait_send()

        @pl.when(inner)
        def _():
            ii_copy(k).wait_send()
            io_copy(k).wait_send()

        return carry

    behind = 10

    def drain(t, carry):
        comm(t)
        return finish(t - behind, carry)

    lax.fori_loop(0, 15 - behind, finish, 0)
    lax.fori_loop(15, 20, drain, 0)
    gain_oi()
    lax.fori_loop(20, 22, drain, 0)
    gain_ii()
    lax.fori_loop(22, n_chunks, drain, 0)
    gain_io()
    lax.fori_loop(n_chunks, n_chunks + 2, drain, 0)
    gain_x()
    lax.fori_loop(n_chunks + 2, n_chunks + 6, drain, 0)
    g_x.wait_recv()
    for m, n in ((x, 10), (1 - x, 11)):
        total = gsum[n]
        flat = jnp.concatenate(
            [jnp.concatenate([total[r * pieces + q : r * pieces + q + 1] for q in range(pieces)], axis=1) for r in range(2)],
            axis=0,
        )
        share = width // DP
        own = flat[:, 0:share]
        for d in range(1, DP):
            own = jnp.where(dp == d, flat[:, d * share : (d + 1) * share], own)
        gain_out[m, 0:2, 0:share] = own

    lax.fori_loop(n_chunks + 6 - behind, n_chunks, finish, 0)
    for cp in a_copies + b_copies + ht_copies + [tok_send, pos_send, ax_copy, bx_copy, g_core, g_y, g_x]:
        cp.wait_send()

    @pl.when(outer)
    def _():
        g_oi.wait_send()

    @pl.when(inner)
    def _():
        g_ii.wait_send()
        g_io.wait_send()

    for j in range(n_blocks):
        gb_copy(j).wait_send()
    tg_copy.wait()
    tg_here.wait()


def layer_call(tokens, positions, missing, wqkv, wout, wup, wdown, gains):
    own, patches = positions.shape
    width = tokens.shape[2]
    hidden = wup.shape[2]
    rows = 2 * own * patches
    items = missing.shape[0]
    n_blocks = hidden // width + 4
    n_chunks = n_blocks * (width // CHUNK)
    piece = (n_chunks, width // 4, CHUNK)
    vm = pltpu.VMEM
    any_spec = pl.BlockSpec(memory_space=pl.ANY)
    n_sems = S_Y + 5 * n_chunks
    scratch = [
        vm((own, patches), jnp.int32), vm((1, items), jnp.int32), vm((2, width), F32),
        vm((width, 3 * width), BF16), vm((width, width), BF16), vm((width, hidden), BF16), vm((hidden, width), BF16),
        vm((rows, width), BF16),
        vm((2, 8, 128), F32),
        vm((rows, width), BF16),
        vm((rows, 3 * width), BF16),
        vm((4 * (HEADS // 2), 2 * patches, patches), F32),
        vm((rows, width), BF16),
        vm((rows, width), F32),
        vm((rows, width), BF16),
        vm((rows, hidden), BF16),
        vm((8, hidden), F32),
        vm((8, width), F32),
        vm((16, width), F32),
        vm((32, 128), F32),
        vm((2, 2, 8, 32, 128), BF16),
        vm((8, 16, 128), F32),
        vm((4, 2, 16, 128), BF16),
        vm((2, 8, 2, 16, 128), BF16),
        vm((2, 8, 16, 128), BF16),
        vm((2, items, width), BF16),
        vm((2, items, width), BF16),
        vm((2, items, width), BF16),
        vm((16, width), F32),
        vm((8, width), F32),
        vm((3, width, rows), BF16),
        vm((3, width // 2, 2 * rows), BF16),
        vm((n_blocks, 2 * rows, width), BF16),
        vm((rows, width), BF16),
        vm((rows, width), F32),
        vm((8, width), F32),
        vm((12, 16, 128), F32),
        vm((items, hidden // DP), BF16),
        vm(piece, BF16), vm(piece, BF16), vm(piece, BF16), vm(piece, BF16), vm(piece, BF16),
        pltpu.SemaphoreType.DMA((12,)),
        pltpu.SemaphoreType.DMA((n_sems,)),
        pltpu.SemaphoreType.DMA((n_sems,)),
    ]
    return pl.pallas_call(
        layer_kernel,
        out_shape=(
            vm((2, width // DP, n_chunks * CHUNK), BF16), vm((2, hidden // DP, width), BF16),
            vm((2, own * patches, width), BF16), vm((2, 8, 128), F32), vm((8, 128), F32),
        ),
        in_specs=[any_spec] * 8,
        out_specs=(pl.BlockSpec(memory_space=pltpu.VMEM),) * 5,
        scratch_shapes=scratch,
        compiler_params=pltpu.CompilerParams(
            collective_id=0, has_side_effects=True, vmem_limit_bytes=58 * 2**20
        ),
    )(tokens, positions, missing.reshape(1, items), wqkv, wout, wup, wdown, gains)


def widen_kernel(
    grads, down, tok, gain, loss, qkv_o, out_o, up_o, down_o, tok_o, gain_o, loss_o, qkv_v, out_v, up_v, down_v, tok_v, sem
):
    hidden, width = up_v.shape[2], out_v.shape[2]
    outs = []

    def send(value, wide, dst):
        wide[...] = value.astype(F32)
        outs.append(pltpu.make_async_copy(wide, dst, sem.at[len(outs)]))
        outs[-1].start()

    for m in range(2):
        send(tok[m], tok_v.at[m], tok_o.at[m])
        send(down[m], down_v.at[m], down_o.at[m])
        for lo, size, wide, dst in (
            (0, hidden, up_v, up_o), (hidden, width, out_v, out_o), (hidden + width, 3 * width, qkv_v, qkv_o)
        ):
            send(grads[m, :, lo : lo + size], wide.at[m], dst.at[m])
    loss_o[...] = loss[0:1, 0:1]
    gain_o[...] = gain[:, 0:2, 0 : gain_o.shape[2]]
    for cp in outs:
        cp.wait()


def widen_call(grads, down, tok, gain, loss, width, hidden):
    vm = pltpu.VMEM
    vmem_spec = pl.BlockSpec(memory_space=pltpu.VMEM)
    rows = width // DP
    shapes = ((2, rows, 3 * width), (2, rows, width), (2, rows, hidden), down.shape, tok.shape)
    ins = [pltpu.with_memory_space_constraint(v, pltpu.VMEM) for v in (grads, down, tok, gain, loss)]
    return pl.pallas_call(
        widen_kernel,
        out_shape=tuple(jax.ShapeDtypeStruct(shape, F32) for shape in shapes + ((2, 2, rows), (1, 1))),
        in_specs=[vmem_spec] * 5,
        out_specs=(pl.BlockSpec(memory_space=pl.ANY),) * 5 + (vmem_spec,) * 2,
        scratch_shapes=[vm(shape, F32) for shape in shapes] + [pltpu.SemaphoreType.DMA((10,))],
        compiler_params=pltpu.CompilerParams(vmem_limit_bytes=40 * 2**20),
    )(*ins)


def fused(tokens, positions, missing, qkv_weight, out_weight, up_weight, down_weight, norm_gains):
    grads, down, tok, gain, loss = layer_call(
        tokens, positions, missing, qkv_weight, out_weight, up_weight, down_weight, norm_gains
    )
    qkv, out, up, down, tok, gain, loss = widen_call(
        grads, down, tok, gain, loss, tokens.shape[2], up_weight.shape[2]
    )
    return (loss.reshape(()), tok, qkv, out, up, down, gain)


def lead_dot(left, right):
    return lax.dot_general(
        left, right, (((0,), (0,)), ((), ())), preferred_element_type=jnp.float32
    )


def tail_dot(left, right):
    return lax.dot_general(
        left, right, (((1,), (1,)), ((), ())), preferred_element_type=jnp.float32
    )


def norm_gain(values, gain):
    centre = values - jnp.mean(values, axis=-1, keepdims=True)
    spread = jnp.mean(centre * centre, axis=-1, keepdims=True)
    return centre * lax.rsqrt(spread + eps_norm) * gain


def unit_rows(pooled):
    return pooled * lax.rsqrt(jnp.sum(pooled * pooled, axis=1, keepdims=True) + eps_norm)


def gelu_exact(values):
    return jax.nn.gelu(values, approximate=False)


def alibi_bias(positions):
    grid_rows = (positions // GRID_W).astype(jnp.float32)
    grid_cols = (positions % GRID_W).astype(jnp.float32)
    row_gap = grid_rows[:, :, None] - grid_rows[:, None, :]
    col_gap = grid_cols[:, :, None] - grid_cols[:, None, :]
    distance = jnp.sqrt(row_gap * row_gap + col_gap * col_gap)
    slopes = jnp.exp2(-8.0 * (jnp.arange(HEADS) + 1).astype(jnp.float32) / HEADS)
    return -slopes[None, :, None, None] * distance[:, None, :, :]


def log_total(logits, valid_cols, valid_rows):
    row_max = jnp.max(logits, axis=1, keepdims=True)
    summed = jnp.sum(valid_cols[None, :] * jnp.exp(logits - row_max), axis=1) + (1.0 - valid_rows)
    return row_max[:, 0] + jnp.log(summed)


def row_grads(logits, log_sums, valid_rows, valid_cols, match, total_items):
    soft = valid_cols[None, :] * jnp.exp(logits - log_sums[:, None])
    return (valid_rows[:, None] / (2.0 * total_items) * (soft - match)).astype(jnp.bfloat16)


def block_forward(token_rows, alibi_terms, qkv_weight, out_weight, up_weight, down_weight, gains):
    row_count, model_width = token_rows.shape
    images, patches = (alibi_terms.shape[0], alibi_terms.shape[2])
    head_dim = model_width // HEADS
    score_scale = head_dim ** (-0.5)
    start_rows = token_rows.astype(jnp.float32)
    normed_one = norm_gain(start_rows, gains[0]).astype(jnp.bfloat16)
    projected = jnp.dot(normed_one, qkv_weight, preferred_element_type=jnp.float32).astype(
        jnp.bfloat16
    )
    queries = projected[:, :model_width].reshape(images, patches, HEADS, head_dim)
    key_rows = projected[:, model_width : 2 * model_width].reshape(images, patches, HEADS, head_dim)
    value_rows = projected[:, 2 * model_width :].reshape(images, patches, HEADS, head_dim)
    scores = jnp.einsum("iqhd,ikhd->ihqk", queries, key_rows, preferred_element_type=jnp.float32)
    attn_probs = jax.nn.softmax(scores * score_scale + alibi_terms, axis=-1)
    probs_low = attn_probs.astype(jnp.bfloat16)
    attended = jnp.einsum(
        "ihqk,ikhd->iqhd", probs_low, value_rows, preferred_element_type=jnp.float32
    )
    attended = attended.reshape(row_count, model_width).astype(jnp.bfloat16)
    residual = start_rows + jnp.dot(attended, out_weight, preferred_element_type=jnp.float32)
    normed_two = norm_gain(residual, gains[1]).astype(jnp.bfloat16)
    hidden_pre = jnp.dot(normed_two, up_weight, preferred_element_type=jnp.float32)
    active = gelu_exact(hidden_pre).astype(jnp.bfloat16)
    out_rows = residual + jnp.dot(active, down_weight, preferred_element_type=jnp.float32)
    saved = (
        start_rows,
        normed_one,
        projected,
        attn_probs,
        probs_low,
        attended,
        residual,
        normed_two,
        hidden_pre,
        active,
    )
    return (out_rows, saved)


def block_backward(grad_rows, saved, qkv_weight, out_weight, up_weight, down_weight, gains):
    (
        start_rows,
        normed_one,
        projected,
        attn_probs,
        probs_low,
        attended,
        residual,
        normed_two,
        hidden_pre,
        active,
    ) = saved
    images, head_count, patches = (attn_probs.shape[0], attn_probs.shape[1], attn_probs.shape[2])
    row_count, model_width = grad_rows.shape
    head_dim = model_width // head_count
    score_scale = head_dim ** (-0.5)
    down_in = grad_rows.astype(jnp.bfloat16)
    grad_down = lead_dot(active, down_in)
    grad_active = tail_dot(down_in, down_weight)
    _, gelu_back = jax.vjp(gelu_exact, hidden_pre)
    grad_hidden = gelu_back(grad_active)[0].astype(jnp.bfloat16)
    grad_up = lead_dot(normed_two, grad_hidden)
    grad_h_two = tail_dot(grad_hidden, up_weight)
    _, norm_two_back = jax.vjp(norm_gain, residual, gains[1])
    grad_mid, gain_two = norm_two_back(grad_h_two)
    grad_residual = grad_rows + grad_mid
    attn_in = grad_residual.astype(jnp.bfloat16)
    grad_out = lead_dot(attended, attn_in)
    grad_att = (
        tail_dot(attn_in, out_weight)
        .astype(jnp.bfloat16)
        .reshape(images, patches, head_count, head_dim)
    )
    queries = projected[:, :model_width].reshape(images, patches, head_count, head_dim)
    key_rows = projected[:, model_width : 2 * model_width].reshape(
        images, patches, head_count, head_dim
    )
    value_rows = projected[:, 2 * model_width :].reshape(images, patches, head_count, head_dim)
    grad_values = jnp.einsum(
        "ihqk,iqhd->ikhd", probs_low, grad_att, preferred_element_type=jnp.float32
    )
    grad_probs = jnp.einsum(
        "iqhd,ikhd->ihqk", grad_att, value_rows, preferred_element_type=jnp.float32
    )
    grad_scores = attn_probs * (
        grad_probs - jnp.sum(grad_probs * attn_probs, axis=-1, keepdims=True)
    )
    grad_scores = grad_scores.astype(jnp.bfloat16)
    grad_queries = (
        jnp.einsum("ihqk,ikhd->iqhd", grad_scores, key_rows, preferred_element_type=jnp.float32)
        * score_scale
    )
    grad_keys = (
        jnp.einsum("ihqk,iqhd->ikhd", grad_scores, queries, preferred_element_type=jnp.float32)
        * score_scale
    )
    grad_proj = jnp.concatenate(
        [
            grad_queries.reshape(row_count, model_width),
            grad_keys.reshape(row_count, model_width),
            grad_values.reshape(row_count, model_width),
        ],
        axis=1,
    ).astype(jnp.bfloat16)
    grad_qkv = lead_dot(normed_one, grad_proj)
    grad_h_one = tail_dot(grad_proj, qkv_weight)
    _, norm_one_back = jax.vjp(norm_gain, start_rows, gains[0])
    grad_first, gain_one = norm_one_back(grad_h_one)
    weight_grads = (grad_qkv, grad_out, grad_up, grad_down, jnp.stack([gain_one, gain_two]))
    return (grad_residual + grad_first, weight_grads)


def local(tokens, positions, missing, qkv_weight, out_weight, up_weight, down_weight, norm_gains):
    own_images = positions.shape[0]
    model_width = tokens.shape[2]
    patches = tokens.shape[1] // own_images
    first_row = lax.axis_index(("dp", "rep")) * own_images
    alibi_terms = alibi_bias(positions)
    saved_list = []
    pooled_list = []
    normed = []
    for modality in range(2):
        out_rows, saved = block_forward(
            tokens[modality],
            alibi_terms,
            qkv_weight[modality],
            out_weight[modality],
            up_weight[modality],
            down_weight[modality],
            norm_gains[modality],
        )
        pooled = jnp.sum(out_rows.reshape(own_images, patches, model_width), axis=1)
        saved_list.append(saved)
        pooled_list.append(pooled)
        normed.append(unit_rows(pooled).astype(jnp.bfloat16))
    valid_all = 1.0 - missing.astype(jnp.float32)
    total_items = float(missing.shape[0])
    valid_own = lax.dynamic_slice_in_dim(valid_all, first_row, own_images)
    radar_all, optic_all = (
        lax.all_gather(normed[0], ("dp", "rep"), axis=0, tiled=True),
        lax.all_gather(normed[1], ("dp", "rep"), axis=0, tiled=True),
    )
    images_all = radar_all.shape[0]
    match_own = (
        lax.broadcasted_iota(jnp.int32, (own_images, images_all), 0) + first_row
        == lax.broadcasted_iota(jnp.int32, (own_images, images_all), 1)
    ).astype(jnp.float32)
    logits_r = tail_dot(normed[0], optic_all) * inv_temp
    logits_o = tail_dot(normed[1], radar_all) * inv_temp
    lse_r = log_total(logits_r, valid_all, valid_own)
    lse_o = log_total(logits_o, valid_all, valid_own)
    item_terms = valid_own * (
        lse_r
        - jnp.sum(logits_r * match_own, axis=1)
        + lse_o
        - jnp.sum(logits_o * match_own, axis=1)
    )
    grad_lr = row_grads(logits_r, lse_r, valid_own, valid_all, match_own, total_items)
    grad_lo = row_grads(logits_o, lse_o, valid_own, valid_all, match_own, total_items)
    grad_ur = jnp.dot(grad_lr, optic_all, preferred_element_type=jnp.float32) * inv_temp
    grad_uo = jnp.dot(grad_lo, radar_all, preferred_element_type=jnp.float32) * inv_temp
    summed_terms = lax.psum(jnp.sum(item_terms), ("dp", "rep"))
    loss_value = summed_terms / (2.0 * total_items)
    share_o = lead_dot(grad_lr, normed[0]) * inv_temp
    share_r = lead_dot(grad_lo, normed[1]) * inv_temp
    back_r, back_o = (
        lax.psum_scatter(share_r, ("dp", "rep"), scatter_dimension=0, tiled=True),
        lax.psum_scatter(share_o, ("dp", "rep"), scatter_dimension=0, tiled=True),
    )
    grad_ur = grad_ur + back_r
    grad_uo = grad_uo + back_o
    grad_units = (grad_ur, grad_uo)
    token_list = []
    block_grads = []
    for modality in range(2):
        _, unit_back = jax.vjp(unit_rows, pooled_list[modality])
        grad_pooled = unit_back(grad_units[modality])[0]
        grad_rows = jnp.broadcast_to(grad_pooled[:, None, :], (own_images, patches, model_width))
        grad_rows = grad_rows.reshape(own_images * patches, model_width)
        grad_tokens, weight_grads = block_backward(
            grad_rows,
            saved_list[modality],
            qkv_weight[modality],
            out_weight[modality],
            up_weight[modality],
            down_weight[modality],
            norm_gains[modality],
        )
        token_list.append(grad_tokens)
        block_grads.append(list(weight_grads))
    stacked = [jnp.stack([block_grads[0][slot], block_grads[1][slot]]) for slot in range(5)]
    shares = (
        lax.psum_scatter(stacked[0], "dp", scatter_dimension=1, tiled=True),
        lax.psum_scatter(stacked[1], "dp", scatter_dimension=1, tiled=True),
        lax.psum_scatter(stacked[2], "dp", scatter_dimension=1, tiled=True),
        lax.psum_scatter(stacked[3], "dp", scatter_dimension=1, tiled=True),
        lax.psum_scatter(stacked[4], "dp", scatter_dimension=2, tiled=True),
    )
    summed = (
        lax.psum(shares[0].astype(jnp.bfloat16), "rep").astype(jnp.float32),
        lax.psum(shares[1].astype(jnp.bfloat16), "rep").astype(jnp.float32),
        lax.psum(shares[2].astype(jnp.bfloat16), "rep").astype(jnp.float32),
        lax.psum(shares[3].astype(jnp.bfloat16), "rep").astype(jnp.float32),
        lax.psum(shares[4].astype(jnp.bfloat16), "rep").astype(jnp.float32),
    )
    stacked = list(summed)
    token_grads = jnp.stack(token_list)
    return (loss_value, token_grads, stacked[0], stacked[1], stacked[2], stacked[3], stacked[4])


def solution(mesh):
    in_specs = (P(None, ("dp", "rep"), None), P(("dp", "rep"), None), P(), P(), P(), P(), P(), P())
    out_specs = (
        P(),
        P(None, ("dp", "rep"), None),
        P(None, "dp", None),
        P(None, "dp", None),
        P(None, "dp", None),
        P(None, "dp", None),
        P(None, None, "dp"),
    )
    one_kernel = mesh.shape["dp"] == DP and mesh.shape["rep"] == REP
    step = fused if one_kernel else local
    return jax.shard_map(step, mesh=mesh, in_specs=in_specs, out_specs=out_specs, check_vma=False)
```
